32 devices in a mesh: gx: 4 (over x, core), gy: 8 (over z, y).
Axes of the slice: x: 2, y: 2, z: 4, core: 2. Of those that a mesh axis runs over, the one named last changes fastest.
Arguments:
- codes: int32 [32768, 1024], P(('gx', 'gy')), may hold values from 0 to 4095
- field_offsets: int32 [8, 1024], replicated, may hold values from 0 to 4095
- seg_mask: int32 [32768], P(('gx', 'gy')), may hold values from 0 to 1
- neg_mask: int32 [512, 512], P(('gx', 'gy')), may hold values from 0 to 1
- owners: int32 [256], replicated, may hold values from 0 to 255, each once
- w_hidden: float32 [256, 64, 64], P(('gx', 'gy')), may hold values from -0.1875 to 0.1875
- stat_left: float32 [256, 64, 64], P(('gx', 'gy')), as said below
- stat_right: float32 [256, 64, 64], P(('gx', 'gy')), as said below
- basis_left: float32 [256, 64, 64], P(('gx', 'gy')), as said below
- basis_right: float32 [256, 64, 64], P(('gx', 'gy')), as said below
- mom1_hidden: float32 [256, 64, 64], P(('gx', 'gy')), may hold values from -1.5258789e-05 to 1.5258789e-05
- mom2_hidden: float32 [256, 64, 64], P(('gx', 'gy')), may hold values from 5.0193387e-12 to 2.0077355e-11
- ema_hidden: float32 [256, 64, 64], P(('gx', 'gy')), may hold values from -0.1875 to 0.1875
- w_out: float32 [1024, 32], replicated, may hold values from -0.1875 to 0.1875
- mom1_out: float32 [1024, 32], replicated, may hold values from -3.0517578e-05 to 3.0517578e-05
- mom2_out: float32 [1024, 32], replicated, may hold values from 2.0077355e-11 to 8.030942e-11
- ema_out: float32 [1024, 32], replicated, may hold values from -0.1875 to 0.1875
- w_towers: float32 [2, 32, 32], replicated, may hold values from -0.5 to 0.5
- mom1_towers: float32 [2, 32, 32], replicated, may hold values from -7.6293945e-05 to 7.6293945e-05
- mom2_towers: float32 [2, 32, 32], replicated, may hold values from 1.2548346e-10 to 5.0193383e-10
- w_norm: float32 [2, 1024], replicated
- mom1_norm: float32 [2, 1024], replicated, may hold values from -0.00015258789 to 0.00015258789
- mom2_norm: float32 [2, 1024], replicated, may hold values from 5.0193383e-10 to 2.0077353e-09
Outputs:
- loss_sum: float32 [], replicated
- loss_count: float32 [], replicated
- grad_norm: float32 [], replicated
- w_hidden_new: float32 [256, 64, 64], P(('gx', 'gy'))
- w_hidden_low: bfloat16 [256, 64, 64], P(('gx', 'gy'))
- stat_left_new: float32 [256, 64, 64], P(('gx', 'gy'))
- stat_right_new: float32 [256, 64, 64], P(('gx', 'gy'))
- basis_left_new: float32 [256, 64, 64], P(('gx', 'gy'))
- basis_right_new: float32 [256, 64, 64], P(('gx', 'gy'))
- mom1_hidden_new: float32 [256, 64, 64], P(('gx', 'gy'))
- mom2_hidden_new: float32 [256, 64, 64], P(('gx', 'gy'))
- ema_hidden_new: float32 [256, 64, 64], P(('gx', 'gy'))
- w_out_new: float32 [1024, 32], replicated
- mom1_out_new: float32 [1024, 32], replicated
- mom2_out_new: float32 [1024, 32], replicated
- ema_out_new: float32 [1024, 32], replicated
- w_towers_new: float32 [2, 32, 32], replicated
- mom1_towers_new: float32 [2, 32, 32], replicated
- mom2_towers_new: float32 [2, 32, 32], replicated
- w_norm_new: float32 [2, 1024], replicated
- mom1_norm_new: float32 [2, 1024], replicated
- mom2_norm_new: float32 [2, 1024], replicated
The draws below stay inside these ranges and needn't reach their ends.
Inputs may be any that keep to these rules, and one draw needn't show every extreme that they name: `stat_left`: symmetric positive definite. `stat_right`: symmetric positive definite. `basis_left`: orthogonal. `basis_right`: orthogonal.
All inputs are finite; a program needn't handle non-finite values.
Results may differ from the reference program's by a relative error of at most 0.0025.
The reference program's roundings to bfloat16 on the way count: a program that leaves them out, or rounds other values in their place, can miss the bound.
Values may be sent and summed in bfloat16 or wider, within the bound.
No kernel may reach another device: no remote copies, remote signals or barrier semaphores. Data moves between devices by JAX's collectives and lax.ppermute only.
A program may use at most 128 MiB of HBM per device.

```python
import math
import jax
import jax.numpy as jnp
from jax import lax

K = 1024
D = 1024
E = 32
B = 64
FIELDS = 4
BAG = 8
HASH_RANGE = 4096
STEP = 10
ROWS_DEV = 16
ROWS = 512
SLOTS = 32768
BLOCKS = 256


def rising_mask(key, count, per_dev, devices, base, rise, shape):
    index = jnp.arange(count, dtype=jnp.int32) // per_dev
    limit = base + rise * index // max(devices - 1, 1)
    shaped = jnp.broadcast_to(limit.reshape((count,) + (1,) * (len(shape) - 1)), shape)
    return (jax.random.randint(key, shape, 0, 1000) < shaped).astype(jnp.int32)


def draw_seg_mask(key, part):
    key = jax.random.fold_in(key, 11)
    per_dev = ROWS_DEV * 2 * FIELDS * BAG
    count = ROWS * 2 * FIELDS * BAG
    return rising_mask(key, count, per_dev, ROWS // ROWS_DEV, 350, 600, (count,))


def draw_neg_mask(key, part):
    key = jax.random.fold_in(key, 12)
    return rising_mask(key, ROWS, ROWS_DEV, ROWS // ROWS_DEV, 250, 500, (ROWS, ROWS))


def definite(key):
    scale = 0.05 / 0.95 * B * (0.01 / D) ** 2
    diag_key, off_key = jax.random.split(key)
    diag = jax.random.uniform(diag_key, (BLOCKS, B), jnp.float32, 1.5, 4.0) * scale
    off = jax.random.uniform(off_key, (BLOCKS, B, B), jnp.float32, -1.0, 1.0)
    off = (off + jnp.swapaxes(off, 1, 2)) * (0.5 * scale / jnp.sqrt(jnp.float32(B)))
    eye = jnp.eye(B, dtype=jnp.float32)
    return off * (1.0 - eye) + diag[:, :, None] * eye


def draw_stat_left(key, part):
    key = jax.random.fold_in(key, 13)
    return definite(key)


def draw_stat_right(key, part):
    key = jax.random.fold_in(key, 14)
    return definite(key)


def reflections(key):
    first_key, second_key = jax.random.split(key)
    first = jax.random.normal(first_key, (BLOCKS, B), jnp.float32)
    second = jax.random.normal(second_key, (BLOCKS, B), jnp.float32)
    first = first / jnp.sqrt(jnp.sum(first * first, axis=1, keepdims=True))
    second = second / jnp.sqrt(jnp.sum(second * second, axis=1, keepdims=True))
    inner = jnp.sum(first * second, axis=1)[:, None, None]
    eye = jnp.eye(B, dtype=jnp.float32)[None]
    return eye - 2.0 * first[:, :, None] * first[:, None, :] - 2.0 * second[:, :, None] * second[:, None, :] + 4.0 * inner * first[:, :, None] * second[:, None, :]


def draw_basis_left(key, part):
    key = jax.random.fold_in(key, 15)
    return reflections(key)


def draw_basis_right(key, part):
    key = jax.random.fold_in(key, 16)
    return reflections(key)


def draw_w_norm(key, part):
    key = jax.random.fold_in(key, 17)
    gain_key, bias_key = jax.random.split(key)
    gain = jax.random.uniform(gain_key, (D,), jnp.float32, 0.6, 1.4)
    bias = jax.random.normal(bias_key, (D,), jnp.float32) * 0.3
    return jnp.stack([gain, bias])


def with_ends(values, key, least, high):
    place = [jax.random.randint(jax.random.fold_in(key, axis), (), 0, length) for axis, length in enumerate(values.shape)]
    widest = values.shape.index(max(values.shape))
    neighbour = place[:widest] + [(place[widest] + 1) % values.shape[widest]] + place[widest + 1:]
    return values.at[tuple(place)].set(least).at[tuple(neighbour)].set(high)


def shard_levels(stream_key, shape, shards, low, largest):
    level = 1.0
    for axis_at, parts in shards:
        heights = jax.random.uniform(jax.random.fold_in(jax.random.fold_in(stream_key, 6), axis_at), (parts,), jnp.float32, low / len(shards), largest / len(shards))
        level = level * jnp.repeat(jnp.exp(heights), shape[axis_at] // parts).reshape((-1,) + (1,) * (len(shape) - 1 - axis_at))
    return level


def bell_draw(own_key, dims, deviation, most, cuts=(), kind=jnp.bfloat16):
    entries = deviation * jax.random.normal(own_key, dims, jnp.float32)
    if cuts:
        entries = entries * shard_levels(own_key, dims, cuts, -0.22, 0.18)
    return jnp.clip(entries, -most, most).astype(kind)


def setup_inputs(seed: int = 0) -> dict:
    arg_keys = jax.random.split(jax.random.key(seed), 24)
    return {
        "codes": with_ends(jax.random.randint(arg_keys[0], (SLOTS, K), 0, HASH_RANGE), jax.random.fold_in(arg_keys[0], 1), 0, HASH_RANGE - 1).astype(jnp.int32),
        "field_offsets": with_ends(jax.random.randint(arg_keys[1], (2 * FIELDS, K), 0, HASH_RANGE), jax.random.fold_in(arg_keys[1], 1), 0, HASH_RANGE - 1).astype(jnp.int32),
        "seg_mask": draw_seg_mask(jax.random.fold_in(arg_keys[23], 71), 0),
        "neg_mask": draw_neg_mask(jax.random.fold_in(arg_keys[23], 71), 0),
        "owners": jax.random.permutation(arg_keys[4], BLOCKS).astype(jnp.int32),
        "w_hidden": bell_draw(arg_keys[5], (BLOCKS, B, B), K ** -0.5, 0.1875, ((0, 32),), jnp.float32),
        "stat_left": draw_stat_left(jax.random.fold_in(arg_keys[23], 71), 0),
        "stat_right": draw_stat_right(jax.random.fold_in(arg_keys[23], 71), 0),
        "basis_left": draw_basis_left(jax.random.fold_in(arg_keys[23], 71), 0),
        "basis_right": draw_basis_right(jax.random.fold_in(arg_keys[23], 71), 0),
        "mom1_hidden": bell_draw(arg_keys[10], (BLOCKS, B, B), (0.1 / 0.9 * 0.01 / D), 1.52587890625e-05, ((0, 32),), jnp.float32),
        "mom2_hidden": jnp.clip(jnp.exp(math.log(2.0077354709324702e-11) - 1.3862944 * jax.random.uniform(arg_keys[11], (BLOCKS, B, B), jnp.float32) ** shard_levels(arg_keys[11], (BLOCKS, B, B), ((0, 32),), -0.2, 0.2)), 5.0193386773311754e-12, 2.0077354709324702e-11),
        "ema_hidden": bell_draw(arg_keys[12], (BLOCKS, B, B), K ** -0.5, 0.1875, ((0, 32),), jnp.float32),
        "w_out": bell_draw(arg_keys[13], (D, E), D ** -0.5, 0.1875, (), jnp.float32),
        "mom1_out": bell_draw(arg_keys[14], (D, E), (0.1 / 0.9 * 0.02 / D), 3.0517578125e-05, (), jnp.float32),
        "mom2_out": jnp.clip(jnp.exp(jax.random.uniform(arg_keys[15], (D, E), jnp.float32, math.log(2.0077354709324702e-11), math.log(8.030941883729881e-11))), 2.0077354709324702e-11, 8.030941883729881e-11),
        "ema_out": bell_draw(arg_keys[16], (D, E), D ** -0.5, 0.1875, (), jnp.float32),
        "w_towers": bell_draw(arg_keys[17], (2, E, E), (E * FIELDS * BAG // 8) ** -0.5, 0.5, (), jnp.float32),
        "mom1_towers": bell_draw(arg_keys[18], (2, E, E), (0.1 / 0.9 * 0.05 / D), 7.62939453125e-05, (), jnp.float32),
        "mom2_towers": jnp.clip(jnp.exp(jax.random.uniform(arg_keys[19], (2, E, E), jnp.float32, math.log(1.254834569586194e-10), math.log(5.019338278344776e-10))), 1.254834569586194e-10, 5.019338278344776e-10),
        "w_norm": draw_w_norm(jax.random.fold_in(arg_keys[23], 71), 0),
        "mom1_norm": bell_draw(arg_keys[21], (2, D), (0.1 / 0.9 * 0.1 / D), 0.00015258789, (), jnp.float32),
        "mom2_norm": jnp.clip(jnp.exp(jax.random.uniform(arg_keys[22], (2, D), jnp.float32, math.log(5.019338278344776e-10), math.log(2.0077353113379104e-09))), 5.019338278344776e-10, 2.0077353113379104e-09),
    }


HIGH = lax.Precision.HIGHEST
BETA_ONE = 0.9
BETA_TWO = 0.95
EPSILON = 1e-08
RATE = 0.03
DECAY = 0.01
CLIP = 0.01
AVG_KEEP = 0.8
AVG_TAKE = 0.2

@jax.custom_vjp
def low(v):
    return lax.optimization_barrier(v.astype(jnp.bfloat16)).astype(jnp.float32)

@jax.custom_vjp
def low_back(v):
    return v

def low_keep(v):
    return (low(v), None)

def low_pass(kept, grad):
    return (grad,)

def back_keep(v):
    return (v, None)

def back_low(kept, grad):
    return (low(grad),)
low.defvjp(low_keep, low_pass)
low_back.defvjp(back_keep, back_low)

def mish(v):
    return v * jnp.tanh(jax.nn.softplus(v))

def to_blocks(full, side, bsize):
    return full.reshape(side, bsize, side, bsize).transpose(0, 2, 1, 3).reshape(side * side, bsize, bsize)

def from_blocks(blocks, side, bsize):
    return blocks.reshape(side, side, bsize, bsize).transpose(0, 2, 1, 3).reshape(side * bsize, side * bsize)

def hash_inputs(codes, field_offsets):
    width = codes.shape[1]
    salted = (codes.reshape(-1, 2 * FIELDS, BAG, width) + field_offsets[None, :, None, :]) % HASH_RANGE
    scaled = salted.astype(jnp.float32) * (2.0 / (HASH_RANGE - 1)) - 1.0
    return scaled.reshape(-1, width).astype(jnp.bfloat16)

def forward(w_first, w_second, towers, norm, inputs, live, neg_mask):
    pre = low_back(jnp.dot(inputs, low(w_first), precision=HIGH))
    live_total = jnp.sum(live)
    mean = lax.optimization_barrier(jnp.sum(live * pre, axis=0)) / live_total
    centered = pre - mean
    var = lax.optimization_barrier(jnp.sum(live * centered * centered, axis=0)) / live_total
    normed = centered * lax.rsqrt(var + 1e-05)
    act = low(mish(norm[0] * normed + norm[1]))
    emb = low_back(jnp.dot(act, low(w_second), precision=HIGH))
    bags = (emb * live).reshape(-1, 2, FIELDS * BAG, E).sum(axis=2)
    user = low(jnp.dot(bags[:, 0], towers[0], precision=HIGH))
    item = low(jnp.dot(bags[:, 1], towers[1], precision=HIGH))
    logits = jnp.dot(user, item.T, precision=HIGH) / math.sqrt(E)
    rows = logits.shape[0]
    own = jnp.eye(rows, dtype=bool)
    keep = own | (neg_mask == 1)
    top = lax.optimization_barrier(jnp.max(jnp.where(keep, logits, -jnp.inf), axis=1, keepdims=True))
    total = lax.optimization_barrier(jnp.sum(jnp.where(keep, jnp.exp(logits - top), 0.0), axis=1))
    ce = top[:, 0] + jnp.log(total) - lax.optimization_barrier(jnp.sum(jnp.where(own, logits, 0.0), axis=1))
    loss_sum = jnp.sum(ce)
    count = jnp.sum(neg_mask.astype(jnp.float32)) / rows
    return (loss_sum / count, (loss_sum, count))

def orthonormal(stat, basis):
    power = jnp.dot(stat, basis, precision=HIGH)
    gram = jnp.dot(power.T, power, precision=HIGH)
    factor = jnp.linalg.cholesky(gram)
    return lax.linalg.triangular_solve(factor, power.T, left_side=True, lower=True).T

def soap(grad, weight, left, right, basis_l, basis_r, first, second):
    left_new = BETA_TWO * left + (1 - BETA_TWO) * jnp.dot(grad, grad.T, precision=HIGH)
    right_new = BETA_TWO * right + (1 - BETA_TWO) * jnp.dot(grad.T, grad, precision=HIGH)
    first_new = BETA_ONE * first + (1 - BETA_ONE) * grad
    turned = jnp.dot(jnp.dot(basis_l.T, grad, precision=HIGH), basis_r, precision=HIGH)
    second_new = BETA_TWO * second + (1 - BETA_TWO) * turned * turned
    moved = jnp.dot(jnp.dot(basis_l.T, first_new, precision=HIGH), basis_r, precision=HIGH) / (1 - BETA_ONE ** STEP)
    ratio = moved / (jnp.sqrt(second_new / (1 - BETA_TWO ** STEP)) + EPSILON)
    update = jnp.dot(jnp.dot(basis_l, ratio, precision=HIGH), basis_r.T, precision=HIGH)
    weight_new = weight - RATE * (update + DECAY * weight)
    return (weight_new, left_new, right_new, orthonormal(left_new, basis_l), orthonormal(right_new, basis_r), first_new, second_new)

def adamw(grad, weight, first, second):
    first_new = BETA_ONE * first + (1 - BETA_ONE) * grad
    second_new = BETA_TWO * second + (1 - BETA_TWO) * grad * grad
    step = first_new / (1 - BETA_ONE ** STEP) / (jnp.sqrt(second_new / (1 - BETA_TWO ** STEP)) + EPSILON)
    return (weight - RATE * (step + DECAY * weight), first_new, second_new)

def reference(codes, field_offsets, seg_mask, neg_mask, owners, w_hidden, stat_left, stat_right, basis_left, basis_right, mom1_hidden, mom2_hidden, ema_hidden, w_out, mom1_out, mom2_out, ema_out, w_towers, mom1_towers, mom2_towers, w_norm, mom1_norm, mom2_norm):
    side = D // B
    inputs = hash_inputs(codes, field_offsets).astype(jnp.float32)
    live = seg_mask.astype(jnp.float32)[:, None]
    w_first = from_blocks(w_hidden[jnp.argsort(owners)], side, B)

    def objective(first, second, towers, norm):
        return forward(first, second, towers, norm, inputs, live, neg_mask)
    loss, pull, extra = jax.vjp(objective, w_first, w_out, w_towers, w_norm, has_aux=True)
    g_first, g_second, g_towers, g_norm = pull(jnp.ones_like(loss))
    squares = jnp.sum(g_first * g_first) + jnp.sum(g_second * g_second)
    squares = squares + jnp.sum(g_towers * g_towers) + jnp.sum(g_norm * g_norm)
    grad_norm = jnp.sqrt(squares)
    factor = CLIP / jnp.maximum(grad_norm, CLIP)
    mine = to_blocks(g_first, side, B)[owners] * factor
    hidden = jax.vmap(soap)(mine, w_hidden, stat_left, stat_right, basis_left, basis_right, mom1_hidden, mom2_hidden)
    out_new = adamw(g_second * factor, w_out, mom1_out, mom2_out)
    towers_new = adamw(g_towers * factor, w_towers, mom1_towers, mom2_towers)
    norm_new = adamw(g_norm * factor, w_norm, mom1_norm, mom2_norm)
    return (extra[0], extra[1], grad_norm, hidden[0], hidden[0].astype(jnp.bfloat16), hidden[1], hidden[2], hidden[3], hidden[4], hidden[5], hidden[6], AVG_KEEP * ema_hidden + AVG_TAKE * hidden[0], out_new[0], out_new[1], out_new[2], AVG_KEEP * ema_out + AVG_TAKE * out_new[0], towers_new[0], towers_new[1], towers_new[2], norm_new[0], norm_new[1], norm_new[2])
```

```python
import functools
import math

import jax
import jax.numpy as jnp
from jax import lax
from jax.experimental import pallas as pl
from jax.experimental.pallas import tpu as pltpu
from jax.sharding import PartitionSpec as P

FIELDS = 4
BAG = 8
HASH_RANGE = 4096
STEP = 10
BETA_ONE = 0.9
BETA_TWO = 0.95
EPSILON = 1e-08
RATE = 0.03
DECAY = 0.01
CLIP = 0.01
AVG_KEEP = 0.8
AVG_TAKE = 0.2

F32 = jnp.float32
BF = jnp.bfloat16
HIGH = lax.Precision.HIGHEST
AXES = ("gx", "gy")
LANES = 128
SLOTS_BAG = FIELDS * BAG
PAIR = 16
MIB = 1 << 20


def dot(a, b, ca=1, cb=0, precision=None):
    return lax.dot_general(
        a, b, (((ca,), (cb,)), ((), ())), precision=precision, preferred_element_type=F32
    )


hdot = functools.partial(dot, precision=HIGH)


def spec(space=pltpu.VMEM):
    return pl.BlockSpec(memory_space=space)


def call(kernel, outs, args, smem=0, scratch=(), limit=32, name=None):
    specs = [spec(pltpu.SMEM)] * smem + [spec()] * (len(args) - smem)
    return pl.pallas_call(
        kernel,
        out_shape=[jax.ShapeDtypeStruct(s, t) for s, t in outs],
        in_specs=specs,
        out_specs=[spec() for _ in outs],
        scratch_shapes=list(scratch),
        compiler_params=pltpu.CompilerParams(vmem_limit_bytes=limit * MIB),
        name=name,
    )(*args)


def swap_halves(v):
    half = v.shape[1] // 2
    return jnp.concatenate([v[:, half:], v[:, :half]], axis=1)


class Plan:
    def __init__(self, gx, gy):
        self.gx, self.gy, self.n = gx, gy, gx * gy
        self.core = gy
        self.x = 2 * gy
        self.y = 1
        bits = []
        b = 2
        while b < gy:
            bits.append(b)
            b *= 2
        b = 4
        while b < gx:
            bits.append(b * gy)
            b *= 2
        self.bits = bits
        rest = [0]
        for b in bits:
            rest = rest + [m | b for m in rest]
        self.rest = rest

    def swap(self, a, mask):
        mx, my = mask // self.gy, mask % self.gy
        if my == 0:
            return lax.ppermute(a, "gx", [(i, i ^ mx) for i in range(self.gx)])
        if mx == 0:
            return lax.ppermute(a, "gy", [(i, i ^ my) for i in range(self.gy)])
        return lax.ppermute(a, AXES, [(i, i ^ mask) for i in range(self.n)])


def pack_kernel(me_ref, owners_ref, w_ref, neg_ref, seg_ref, out_ref, *, masked):
    local, bsize = w_ref.shape[0], w_ref.shape[1]
    half = bsize // 2
    for b in range(local):
        odd = owners_ref[me_ref[0] * local + b] % 2
        top, low = w_ref[b, :half, :], w_ref[b, half:, :]
        left = jnp.where(odd == 1, low, top)
        right = jnp.where(odd == 1, top, low)
        out_ref[b * half : (b + 1) * half, :] = jnp.concatenate([left, right], axis=1).astype(BF)
    at = local * half
    if masked:
        for c in range(neg_ref.shape[1] // LANES):
            part = neg_ref[:, c * LANES : (c + 1) * LANES].astype(F32)
            out_ref[at : at + PAIR, :] = part.astype(BF)
            at += PAIR
    used = jnp.sum(seg_ref[...].astype(F32), axis=0, keepdims=True)
    out_ref[at : at + PAIR, :] = jnp.broadcast_to(used, (PAIR, LANES)).astype(BF)


def gather_pieces(plan, payload, cut):
    stack = payload[None]
    if len(plan.rest) <= 4:
        stack = jnp.concatenate([stack] + [plan.swap(stack, m) for m in plan.rest[1:]], axis=0)
    else:
        for b in plan.bits:
            stack = jnp.concatenate([stack, plan.swap(stack, b)], axis=0)
    by_x = plan.swap(stack, plan.x)
    by_y = plan.swap(stack, plan.y)
    first = plan.swap(by_x[:, :cut], plan.y)
    second = plan.swap(by_y[:, cut:], plan.x)
    mine = [
        (stack, 0, 0),
        (by_x, plan.x, 0),
        (by_y, plan.y, 0),
        (first, plan.x | plan.y, 0),
        (second, plan.x | plan.y, cut),
    ]
    other = [(plan.swap(a, plan.core), m | plan.core, row) for a, m, row in mine]
    return mine + other


def hash_kernel(codes_ref, offsets_ref, x_ref, xt_ref):
    rows, width = codes_ref.shape
    groups = 2 * FIELDS
    salted = codes_ref[...].reshape(-1, groups, BAG, width) + offsets_ref[...][None, :, None, :]
    salted = (salted & (HASH_RANGE - 1)).reshape(rows, width)
    x = (salted.astype(F32) * (2.0 / (HASH_RANGE - 1)) - 1.0).astype(BF)
    x_ref[...] = x
    xt_ref[...] = x.T


def hash_inputs(codes, offsets):
    rows, width = codes.shape
    step = 128
    return pl.pallas_call(
        hash_kernel,
        grid=(rows // step,),
        in_specs=[
            pl.BlockSpec((step, width), lambda i: (i, 0)),
            pl.BlockSpec(offsets.shape, lambda i: (0, 0)),
        ],
        out_specs=[
            pl.BlockSpec((step, width), lambda i: (i, 0)),
            pl.BlockSpec((width, step), lambda i: (0, i)),
        ],
        out_shape=[
            jax.ShapeDtypeStruct((rows, width), BF),
            jax.ShapeDtypeStruct((width, rows), BF),
        ],
        compiler_params=pltpu.CompilerParams(vmem_limit_bytes=24 * MIB),
        cost_estimate=pl.CostEstimate(
            flops=10 * rows * width, bytes_accessed=8 * rows * width, transcendentals=0
        ),
        name="hash",
    )(codes, offsets)


def pre_kernel(*refs, holds, rest, local, masked, n, pieces):
    me_ref, owners_ref = refs[:2]
    piece_refs = refs[2 : 2 + pieces]
    x_ref, live_ref = refs[2 + pieces : 4 + pieces]
    pre_ref, stats_ref, count_ref, mask_ref, w_ref, row_ref = refs[4 + pieces :]
    width = x_ref.shape[1]
    bsize = LANES // 2
    half = bsize // 2
    side = width // bsize
    tiles = width // LANES
    me = me_ref[0]
    lane_half = lax.broadcasted_iota(jnp.int32, (half, LANES), 1) // bsize
    chunks = mask_ref.shape[1] // LANES if masked else 0
    for piece, (base, row0) in zip(piece_refs, holds):
        held = piece.shape[1]
        for k, m in enumerate(rest):
            d = me ^ (m | base)
            for b in range(local):
                at = b * half - row0
                if at < 0 or at + half > held:
                    continue
                q = owners_ref[d * local + b]
                r, c = q // side, q % side
                odd = c % 2
                tile = piece[k, at : at + half, :].astype(F32)
                rows = pl.multiple_of(r * bsize, bsize)
                cols = pl.multiple_of((c // 2) * LANES, LANES)
                keep = lane_half == odd
                pltpu.store(w_ref.at[pl.ds(rows, half), pl.ds(cols, LANES)], tile, mask=keep)
                pltpu.store(
                    w_ref.at[pl.ds(rows + half, half), pl.ds(cols, LANES)],
                    swap_halves(tile),
                    mask=keep,
                )
            for c in range(chunks):
                at = local * half + c * PAIR - row0
                if at < 0 or at + PAIR > held:
                    continue
                mask_ref[pl.ds(pl.multiple_of(d * PAIR, PAIR), PAIR), c * LANES : (c + 1) * LANES] = (
                    piece[k, at : at + PAIR, :]
                )
            at = local * half + chunks * PAIR - row0
            if 0 <= at and at + PAIR <= held:
                count_ref[pl.ds(d, 1), :] = piece[k, at : at + PAIR, :].astype(F32)[:1]
    live = live_ref[...]
    used = jnp.maximum(jnp.sum(live), 1.0)
    step = 2 * LANES
    for j in range(width // step):
        cols = slice(j * step, (j + 1) * step)
        pre_ref[:, cols] = dot(x_ref[...], w_ref[:, cols].astype(BF))
        total = jnp.sum(pre_ref[:, cols] * live, axis=0, keepdims=True)
        apart = pre_ref[:, cols] - total / used
        square = jnp.sum(apart * apart * live, axis=0, keepdims=True)
        for i in range(2):
            t = 2 * j + i
            row_ref[t : t + 1, :] = total[:, i * LANES : (i + 1) * LANES]
            row_ref[tiles + t : tiles + t + 1, :] = square[:, i * LANES : (i + 1) * LANES]
    for d in range(n):
        stats_ref[d * 2 * tiles : (d + 1) * 2 * tiles, :] = row_ref[...]


def act_kernel(
    stats_ref, count_ref, norm_ref, pre_ref, live_ref, w_out_ref,
    slope_ref, act_ref, one_ref, two_ref, coef_ref, bags_ref, pay_ref,
):
    n = count_ref.shape[0]
    rows, width = pre_ref.shape
    tiles = width // LANES
    counts = jnp.sum(count_ref[...], axis=1, keepdims=True)
    used = jnp.sum(counts)
    total = stats_ref[0:tiles, :]
    for d in range(1, n):
        total = total + stats_ref[2 * d * tiles : (2 * d + 1) * tiles, :]
    mean = total / used
    square = jnp.zeros_like(mean)
    for d in range(n):
        c = counts[d : d + 1, :]
        apart = stats_ref[2 * d * tiles : (2 * d + 1) * tiles, :] / jnp.maximum(c, 1.0) - mean
        square = square + (
            stats_ref[(2 * d + 1) * tiles : (2 * d + 2) * tiles, :] + c * apart * apart
        )
    rstd = lax.rsqrt(square / used + 1e-05)
    for j in range(tiles):
        coef_ref[0:1, j * LANES : (j + 1) * LANES] = mean[j : j + 1, :]
        coef_ref[1:2, j * LANES : (j + 1) * LANES] = rstd[j : j + 1, :]
    coef_ref[2:3, :] = jnp.full((1, width), used, F32)
    step = width // 2

    def bag(b, carry):
        at = pl.ds(pl.multiple_of(b * SLOTS_BAG, SLOTS_BAG), SLOTS_BAG)
        live = live_ref[at, :]
        for c in range(2):
            cols = slice(c * step, (c + 1) * step)
            xhat = (pre_ref[at, cols] - coef_ref[0:1, cols]) * coef_ref[1:2, cols]
            y = norm_ref[0:1, cols] * xhat + norm_ref[1:2, cols]
            capped = jnp.minimum(y, 20.0)
            e = jnp.exp(capped)
            top = e * (e + 2.0)
            below = top + 2.0
            guess = pl.reciprocal(below, approx=True)
            inv = guess * (2.0 - below * guess)
            gate = top * inv
            act = (y * gate).astype(BF).astype(F32)
            slope = gate + (4.0 * capped) * (e * inv) * ((1.0 + e) * inv)
            slope_ref[at, cols] = slope
            slope = slope * live
            act_ref[pl.ds(b, 1), cols] = jnp.sum(act * live, axis=0, keepdims=True)
            one_ref[pl.ds(b, 1), cols] = jnp.sum(slope, axis=0, keepdims=True)
            two_ref[pl.ds(b, 1), cols] = jnp.sum(slope * xhat, axis=0, keepdims=True)
        return carry

    lax.fori_loop(0, rows // SLOTS_BAG, bag, 0)
    second = w_out_ref[...].astype(BF).astype(F32)
    bags = hdot(act_ref[...], second)
    pairs = bags.shape[0] // 2
    split = jnp.concatenate([hdot(pick(pairs, 0), bags), hdot(pick(pairs, 1), bags)], axis=0)
    bags_ref[...] = split
    eighth = pairs // 2
    packed = jnp.concatenate([split[i * eighth : (i + 1) * eighth] for i in range(4)], axis=1)
    for d in range(n):
        pay_ref[d * eighth : (d + 1) * eighth, :] = packed


def pick(pairs, which):
    r = lax.broadcasted_iota(jnp.int32, (pairs, 2 * pairs), 0)
    c = lax.broadcasted_iota(jnp.int32, (pairs, 2 * pairs), 1)
    return (c == 2 * r + which).astype(F32)


def spread(pairs, which):
    r = lax.broadcasted_iota(jnp.int32, (2 * pairs, pairs), 0)
    c = lax.broadcasted_iota(jnp.int32, (2 * pairs, pairs), 1)
    return (r == 2 * c + which).astype(F32)


def three(v):
    a = v.astype(BF)
    v = v - a.astype(F32)
    b = v.astype(BF)
    v = v - b.astype(F32)
    return a, b, v.astype(BF)


def loss_kernel(
    me_ref, all_ref, mask_ref, towers_ref, w_out_ref, act_ref, one_ref, two_ref,
    dact_ref, pay_ref, d_towers_ref, scalar_ref,
    score_ref, user_ref, item_ref, second_ref, row_ref, *, n,
):
    me = me_ref[0]
    embed = towers_ref.shape[1]
    total_rows = mask_ref.shape[0]
    eighth = all_ref.shape[0] // n

    def full(i):
        a = all_ref[:, 2 * i * embed : (2 * i + 1) * embed].reshape(n, eighth, embed)
        b = all_ref[:, (2 * i + 1) * embed : (2 * i + 2) * embed].reshape(n, eighth, embed)
        return jnp.stack([a, b], axis=1).reshape(total_rows, embed)

    bags_user, bags_item = full(0), full(1)
    user = hdot(bags_user, towers_ref[0]).astype(BF)
    item = hdot(bags_item, towers_ref[1]).astype(BF)
    root = math.sqrt(embed)
    score_ref[...] = dot(user, item, 1, 1) / root
    negatives = jnp.sum(mask_ref[...].astype(F32))
    count = negatives / total_rows
    step = 32

    def rows(i, carry):
        at = pl.ds(pl.multiple_of(i * step, step), step)
        logits = score_ref[at, :]
        r = lax.broadcasted_iota(jnp.int32, logits.shape, 0) + i * step
        own = r == lax.broadcasted_iota(jnp.int32, logits.shape, 1)
        keep = own | (mask_ref[at, :].astype(F32) == 1.0)
        top = jnp.max(jnp.where(keep, logits, -jnp.inf), axis=1, keepdims=True)
        weights = jnp.where(keep, jnp.exp(logits - top), 0.0)
        total = jnp.sum(weights, axis=1, keepdims=True)
        hit = jnp.sum(jnp.where(own, logits, 0.0), axis=1, keepdims=True)
        score_ref[at, :] = (weights / total - own.astype(F32)) / count / root
        return carry + (top + jnp.log(total) - hit)

    ce = lax.fori_loop(0, total_rows // step, rows, jnp.zeros((step, 1), F32))
    scalar_ref[0:1, :] = jnp.full((1, LANES), jnp.sum(ce), F32)
    scalar_ref[1:2, :] = jnp.full((1, LANES), count, F32)
    parts = three(score_ref[...])
    d_user = sum(dot(p, item) for p in parts)
    d_item = sum(dot(user, p, 0, 0) for p in parts).T
    user_ref[...] = d_user
    item_ref[...] = d_item
    d_towers_ref[0] = hdot(bags_user, d_user, 0, 0)
    d_towers_ref[1] = hdot(bags_item, d_item, 0, 0)
    mine = pl.ds(pl.multiple_of(me * PAIR, PAIR), PAIR)
    back_user = hdot(user_ref[mine, :], towers_ref[0], 1, 1).astype(BF).astype(F32)
    back_item = hdot(item_ref[mine, :], towers_ref[1], 1, 1).astype(BF).astype(F32)
    d_emb = dot(spread(PAIR, 0), back_user) + dot(spread(PAIR, 1), back_item)
    d_act = dot(d_emb.astype(BF), w_out_ref[...].astype(BF), 1, 1)
    dact_ref[...] = d_act
    d_bias = jnp.sum(d_act * one_ref[...], axis=0, keepdims=True)
    d_gain = jnp.sum(d_act * two_ref[...], axis=0, keepdims=True)
    d_low = d_emb.T.astype(BF)
    second_ref[...] = sum(dot(d_low, p) for p in three(act_ref[...]))
    width = act_ref.shape[1]
    tiles = width // LANES
    for j in range(tiles):
        cols = slice(j * LANES, (j + 1) * LANES)
        row_ref[j : j + 1, :] = d_bias[:, cols]
        row_ref[tiles + j : tiles + j + 1, :] = d_gain[:, cols]
    chunk = embed * tiles // n
    for d in range(n):
        at = d * (2 * tiles + chunk)
        pay_ref[at : at + 2 * tiles, :] = row_ref[...]
        for i in range(chunk):
            e, j = (d * chunk + i) // tiles, (d * chunk + i) % tiles
            pay_ref[at + 2 * tiles + i : at + 2 * tiles + i + 1, :] = second_ref[
                e : e + 1, j * LANES : (j + 1) * LANES
            ]


def loss_spread(plan, bags, neg_mask, towers, w_out, act, one, two):
    embed = towers.shape[1]
    rows = neg_mask.shape[0]
    bags_user, bags_item = bags[:rows], bags[rows:]
    user = hdot(bags_user, towers[0]).astype(BF)
    item = hdot(bags_item, towers[1]).astype(BF)
    items = lax.all_gather(item, AXES, axis=0, tiled=True)
    root = math.sqrt(embed)
    logits = dot(user, items, 1, 1) / root
    at = lax.axis_index(AXES) * rows + lax.broadcasted_iota(jnp.int32, logits.shape, 0)
    own = lax.broadcasted_iota(jnp.int32, logits.shape, 1) == at
    keep = own | (neg_mask == 1)
    top = jnp.max(jnp.where(keep, logits, -jnp.inf), axis=1, keepdims=True)
    weights = jnp.where(keep, jnp.exp(logits - top), 0.0)
    total = jnp.sum(weights, axis=1, keepdims=True)
    ce = top + jnp.log(total) - jnp.sum(jnp.where(own, logits, 0.0), axis=1, keepdims=True)
    count = lax.psum(jnp.sum(neg_mask.astype(F32)), AXES) / items.shape[0]
    scores = (weights / total - own.astype(F32)) / count / root
    d_user = hdot(scores, items.astype(F32))
    d_item = lax.psum_scatter(
        hdot(scores, user.astype(F32), 0, 0), AXES, scatter_dimension=0, tiled=True
    )
    d_towers = jnp.stack([hdot(bags_user, d_user, 0, 0), hdot(bags_item, d_item, 0, 0)])
    back = jnp.stack([hdot(d_user, towers[0], 1, 1), hdot(d_item, towers[1], 1, 1)], axis=1)
    d_emb = back.reshape(2 * rows, embed).astype(BF)
    d_act = dot(d_emb, w_out.astype(BF), 1, 1)
    d_second = hdot(d_emb.astype(F32), act, 0, 0)
    sums = jnp.stack([jnp.sum(d_act * one, axis=0), jnp.sum(d_act * two, axis=0)])
    sums, d_second, d_towers, loss = lax.psum((sums, d_second, d_towers, jnp.sum(ce)), AXES)
    return d_act, sums.reshape(-1, LANES), d_second, d_towers, loss, count


def grad_kernel(
    me_ref, owners_ref, sums_ref, coef_ref, norm_ref, dact_ref, slope_ref, pre_ref, live_ref, xt_ref,
    keep_ref, send_ref, chunk_ref, d_norm_ref, d_pre_ref, g_ref, row_ref,
    *, parts, order, local,
):
    rows, width = pre_ref.shape
    tiles = width // LANES
    held = sums_ref.shape[0] // parts
    total = sums_ref[0:held, :]
    for d in range(1, parts):
        total = total + sums_ref[d * held : (d + 1) * held, :]
    d_norm_ref[0:tiles, :] = total[tiles : 2 * tiles]
    d_norm_ref[tiles : 2 * tiles, :] = total[:tiles]
    chunk_ref[...] = total[2 * tiles :] if held > 2 * tiles else jnp.zeros(chunk_ref.shape, F32)
    for j in range(tiles):
        cols = slice(j * LANES, (j + 1) * LANES)
        row_ref[0:1, cols] = total[j : j + 1]
        row_ref[1:2, cols] = total[tiles + j : tiles + j + 1]
    scale = norm_ref[0:1, :] * coef_ref[1:2, :]
    flat = scale * row_ref[0:1, :] / coef_ref[2:3, :]
    tilt = scale * row_ref[1:2, :] / coef_ref[2:3, :] * coef_ref[1:2, :]
    row_ref[2:3, :] = scale
    row_ref[3:4, :] = flat
    row_ref[4:5, :] = tilt
    step = width // 2

    def bag(b, carry):
        at = pl.ds(pl.multiple_of(b * SLOTS_BAG, SLOTS_BAG), SLOTS_BAG)
        live = live_ref[at, :]
        for c in range(2):
            cols = slice(c * step, (c + 1) * step)
            lead = dact_ref[pl.ds(b, 1), cols] * row_ref[2:3, cols]
            apart = (pre_ref[at, cols] - coef_ref[0:1, cols]) * row_ref[4:5, cols]
            d_pre = live * (slope_ref[at, cols] * lead - row_ref[3:4, cols] - apart)
            d_pre_ref[at, cols] = d_pre.astype(BF)
        return carry

    lax.fori_loop(0, rows // SLOTS_BAG, bag, 0)
    block = 2 * LANES
    for j in range(width // block):
        cols = slice(j * block, (j + 1) * block)
        g_ref[:, cols] = dot(xt_ref[...], d_pre_ref[:, cols])
    bsize = LANES // 2
    half = bsize // 2
    side = width // bsize
    lane_half = lax.broadcasted_iota(jnp.int32, (half, LANES), 1) // bsize
    me = me_ref[0]
    for out, masks in ((keep_ref, order[0]), (send_ref, order[1])):
        for i, m in enumerate(masks):
            for b in range(local):
                q = owners_ref[(me ^ m) * local + b]
                r, c = q // side, q % side
                at = pl.ds(pl.multiple_of(r * bsize, bsize), half)
                low = pl.ds(pl.multiple_of(r * bsize + half, half), half)
                cols = pl.ds(pl.multiple_of((c // 2) * LANES, LANES), LANES)
                packed = jnp.where(
                    lane_half == c % 2, g_ref[at, cols], swap_halves(g_ref[low, cols])
                )
                to = (i * local + b) * half
                out[to : to + half, :] = packed.astype(out.dtype)


def scatter_sum(plan, keep, send, rows):
    rest = len(plan.rest)
    shape = (2, 2, rest, rows, LANES)
    got = plan.swap(send, plan.core)
    mine = (keep + got.astype(F32)).reshape(shape)
    cut = rows // 2
    one, two = mine[..., :cut, :], mine[..., cut:, :]
    got_one = plan.swap(one[1].astype(BF), plan.x)
    got_two = plan.swap(two[:, 1].astype(BF), plan.y)
    one = one[0] + got_one.astype(F32)
    two = two[:, 0] + got_two.astype(F32)
    got_one = plan.swap(one[1].astype(BF), plan.y)
    got_two = plan.swap(two[1].astype(BF), plan.x)
    one = one[0] + got_one.astype(F32)
    two = two[0] + got_two.astype(F32)
    both = jnp.concatenate([one, two], axis=1)
    if rest <= 4:
        got = [plan.swap(both[k].astype(BF), m) for k, m in enumerate(plan.rest) if k]
        total = both[0]
        for g in got:
            total = total + g.astype(F32)
        return total
    for b in reversed(plan.bits):
        both = both.reshape(2, -1, rows, LANES)
        both = both[0] + plan.swap(both[1].astype(BF), b).astype(F32)
    return both.reshape(rows, LANES)


def norm_kernel(g_ref, chunk_ref, pay_ref, *, n):
    squares = jnp.sum(g_ref[...] * g_ref[...]) + jnp.sum(chunk_ref[...] * chunk_ref[...])
    rows = pay_ref.shape[0] // n
    chunk = chunk_ref.shape[0]
    for d in range(n):
        pay_ref[d * rows : d * rows + chunk, :] = chunk_ref[...]
        pay_ref[d * rows + chunk : (d + 1) * rows, :] = jnp.full((rows - chunk, LANES), squares, F32)


def adamw(grad, weight, first, second):
    first = BETA_ONE * first + (1 - BETA_ONE) * grad
    second = BETA_TWO * second + (1 - BETA_TWO) * grad * grad
    step = (
        first / (1 - BETA_ONE**STEP) / (jnp.sqrt(second / (1 - BETA_TWO**STEP)) + EPSILON)
    )
    return weight - RATE * (step + DECAY * weight), first, second


def eliminate(mat_ref):
    size = mat_ref.shape[1]
    group = 8
    for g in range(size // group):
        at = g * group
        for i in range(group):
            j = at + i
            row = mat_ref[:, j : j + 1, :]
            inv = lax.rsqrt(row[:, :, j : j + 1])
            row = row * inv
            head = mat_ref[:, at : at + group, :]
            index = lax.broadcasted_iota(jnp.int32, (1, group, 1), 1)
            down = head - (head[:, :, j : j + 1] * inv) * row
            mat_ref[:, at : at + group, :] = jnp.where(
                index > i, down, jnp.where(index == i, row, head)
            )
            if at + group < size:
                tail = mat_ref[:, at + group :, :]
                mat_ref[:, at + group :, :] = tail - (tail[:, :, j : j + 1] * inv) * row


def step_kernel(
    me_ref, owners_ref, got_ref, g_ref, d_norm_ref, d_towers_ref,
    w_ref, left_ref, right_ref, bl_ref, br_ref, first_ref, second_ref, ema_ref,
    wo_ref, mo_ref, vo_ref, eo_ref, wt_ref, mt_ref, vt_ref, wn_ref, mn_ref, vn_ref,
    gn_out, w_out, low_out, left_out, right_out, bl_out, br_out, first_out, second_out, ema_out,
    wo_out, mo_out, vo_out, eo_out, wt_out, mt_out, vt_out, wn_out, mn_out, vn_out,
    mat_ref, wide_ref, dn_ref, *, n,
):
    local, bsize = w_ref.shape[0], w_ref.shape[1]
    half = bsize // 2
    width, embed = wo_ref.shape
    tiles = width // LANES
    held = got_ref.shape[0] // n
    if n > 1:
        chunk = embed * tiles // n
        squares = 0.0
        for d in range(n):
            squares = squares + got_ref[d * held + chunk : d * held + chunk + 1, :]
            for i in range(chunk):
                e, j = (d * chunk + i) // tiles, (d * chunk + i) % tiles
                wide_ref[e : e + 1, j * LANES : (j + 1) * LANES] = got_ref[
                    d * held + i : d * held + i + 1, :
                ]
        squares = jnp.max(squares)
    else:
        squares = jnp.max(got_ref[0:1, :LANES])
        wide_ref[...] = got_ref[8 : 8 + embed, :]
    squares = squares + jnp.sum(d_towers_ref[...] * d_towers_ref[...])
    squares = squares + jnp.sum(d_norm_ref[...] * d_norm_ref[...])
    norm = jnp.sqrt(jnp.full((1, LANES), squares, F32))
    gn_out[...] = norm
    factor = (CLIP / jnp.maximum(norm, CLIP))[:, :1]
    for b in range(local):
        odd = owners_ref[me_ref[0] * local + b] % 2
        tile = g_ref[b * half : (b + 1) * half, :]
        tile = jnp.where(odd == 1, swap_halves(tile), tile)
        grad = jnp.concatenate([tile[:, :bsize], tile[:, bsize:]], axis=0) * factor
        bl, br = bl_ref[b], br_ref[b]
        left = BETA_TWO * left_ref[b] + (1 - BETA_TWO) * hdot(grad, grad, 1, 1)
        right = BETA_TWO * right_ref[b] + (1 - BETA_TWO) * hdot(grad, grad, 0, 0)
        left_out[b], right_out[b] = left, right
        first = BETA_ONE * first_ref[b] + (1 - BETA_ONE) * grad
        first_out[b] = first
        turned = hdot(hdot(bl, grad, 0, 0), br)
        second = BETA_TWO * second_ref[b] + (1 - BETA_TWO) * turned * turned
        second_out[b] = second
        moved = hdot(hdot(bl, first, 0, 0), br) / (1 - BETA_ONE**STEP)
        ratio = moved / (jnp.sqrt(second / (1 - BETA_TWO**STEP)) + EPSILON)
        update = hdot(hdot(bl, ratio), br, 1, 1)
        new = w_ref[b] - RATE * (update + DECAY * w_ref[b])
        w_out[b] = new
        low_out[b] = new.astype(BF)
        ema_out[b] = AVG_KEEP * ema_ref[b] + AVG_TAKE * new
        for i, (stat, basis) in enumerate(((left, bl), (right, br))):
            power = hdot(basis, stat, 0, 0)
            gram = hdot(power, power, 1, 1)
            mat_ref[2 * b + i] = jnp.concatenate([gram, power], axis=1)
    eliminate(mat_ref)
    for b in range(local):
        bl_out[b] = mat_ref[2 * b, :, bsize:].T
        br_out[b] = mat_ref[2 * b + 1, :, bsize:].T
    new, m, v = adamw(wide_ref[...].T * factor, wo_ref[...], mo_ref[...], vo_ref[...])
    wo_out[...], mo_out[...], vo_out[...] = new, m, v
    eo_out[...] = AVG_KEEP * eo_ref[...] + AVG_TAKE * new
    for t in range(2):
        wt_out[t], mt_out[t], vt_out[t] = adamw(
            d_towers_ref[t] * factor, wt_ref[t], mt_ref[t], vt_ref[t]
        )
        for j in range(tiles):
            dn_ref[t : t + 1, j * LANES : (j + 1) * LANES] = d_norm_ref[
                t * tiles + j : t * tiles + j + 1, :
            ]
    wn_out[...], mn_out[...], vn_out[...] = adamw(
        dn_ref[...] * factor, wn_ref[...], mn_ref[...], vn_ref[...]
    )


def exchange(payload):
    return lax.all_to_all(payload, AXES, 0, 0, tiled=True)


def on_device(
    plan,
    codes, field_offsets, seg_mask, neg_mask, owners,
    w_hidden, stat_left, stat_right, basis_left, basis_right, mom1_hidden, mom2_hidden, ema_hidden,
    w_out, mom1_out, mom2_out, ema_out,
    w_towers, mom1_towers, mom2_towers,
    w_norm, mom1_norm, mom2_norm,
):
    n = plan.n
    local, bsize = w_hidden.shape[0], w_hidden.shape[1]
    width, embed = w_out.shape
    slots = codes.shape[0]
    rows, total_rows = neg_mask.shape
    tiles = width // LANES
    half = bsize // 2
    bags = slots // SLOTS_BAG
    masked = total_rows <= 1024 and n <= embed
    me = lax.axis_index(AXES).astype(jnp.int32)[None]

    chunks = total_rows // LANES if masked else 0
    size = local * half + chunks * PAIR + PAIR
    (payload,) = call(
        functools.partial(pack_kernel, masked=masked),
        [((size, LANES), BF)],
        [me, owners, w_hidden, neg_mask, seg_mask.reshape(-1, LANES)],
        smem=2,
        name="pack",
    )
    cut = max(half, size // 2 // half * half)
    cut = min(cut, local * half)
    pieces = gather_pieces(plan, payload, cut)
    x, x_turned = hash_inputs(codes, field_offsets)
    live = seg_mask.astype(F32)[:, None]
    mask_shape = (total_rows, total_rows) if masked else (PAIR, LANES)
    pre, stats, counts, mask = call(
        functools.partial(
            pre_kernel,
            holds=[(m, row) for _, m, row in pieces],
            rest=plan.rest,
            local=local,
            masked=masked,
            n=n,
            pieces=len(pieces),
        ),
        [
            ((slots, width), F32),
            ((n * 2 * tiles, LANES), F32),
            ((n, LANES), F32),
            (mask_shape, BF),
        ],
        [me, owners] + [a for a, _, _ in pieces] + [x, live],
        smem=2,
        scratch=[pltpu.VMEM((width, width), F32), pltpu.VMEM((2 * tiles, LANES), F32)],
        limit=40,
        name="pre",
    )
    stats = exchange(stats)
    slope, act, one, two, coef, bag_sums, pay = call(
        act_kernel,
        [
            ((slots, width), F32),
            ((bags, width), F32),
            ((bags, width), F32),
            ((bags, width), F32),
            ((8, width), F32),
            ((bags, embed), F32),
            ((n * 8, LANES), F32),
        ],
        [stats, counts, w_norm, pre, live, w_out],
        limit=40,
        name="act",
    )
    if masked:
        chunk = embed * tiles // n
        everyone = exchange(pay)
        d_act, pay, d_towers, scalars = call(
            functools.partial(loss_kernel, n=n),
            [
                ((bags, width), F32),
                ((n * (2 * tiles + chunk), LANES), F32),
                ((2, embed, embed), F32),
                ((8, LANES), F32),
            ],
            [me, everyone, mask, w_towers, w_out, act, one, two],
            smem=1,
            scratch=[
                pltpu.VMEM((total_rows, total_rows), F32),
                pltpu.VMEM((total_rows, embed), F32),
                pltpu.VMEM((total_rows, embed), F32),
                pltpu.VMEM((embed, width), F32),
                pltpu.VMEM((2 * tiles, LANES), F32),
            ],
            name="loss",
        )
        sums, parts = exchange(pay), n
        loss_sum, count = scalars[0, 0], scalars[1, 0]
    else:
        d_act, sums, d_second, d_towers, loss_sum, count = loss_spread(
            plan, bag_sums, neg_mask, w_towers, w_out, act, one, two
        )
        parts = 1
        chunk = 8
    groups = [m for m in (0, plan.y, plan.x, plan.x | plan.y)]
    keep_order = [g | r for g in groups for r in plan.rest]
    order = (keep_order, [m | plan.core for m in keep_order])
    kept, sent, second_chunk, d_norm = call(
        functools.partial(grad_kernel, parts=parts, order=order, local=local),
        [
            ((n // 2 * local * half, LANES), F32),
            ((n // 2 * local * half, LANES), BF),
            ((chunk, LANES), F32),
            ((2 * tiles, LANES), F32),
        ],
        [me, owners, sums, coef, w_norm, d_act, slope, pre, live, x_turned],
        smem=2,
        scratch=[
            pltpu.VMEM((slots, width), BF),
            pltpu.VMEM((width, width), F32),
            pltpu.VMEM((8, width), F32),
        ],
        limit=48,
        name="grad",
    )
    grad = scatter_sum(plan, kept, sent, local * half)
    if masked:
        held = (chunk // 8 + 1) * 8
        (pay,) = call(
            functools.partial(norm_kernel, n=n),
            [((n * held, LANES), F32)],
            [grad, second_chunk],
            name="norm",
        )
        got = exchange(pay)
    else:
        squares = lax.psum(jnp.sum(grad * grad), AXES) + jnp.sum(d_second * d_second)
        got = jnp.concatenate([jnp.full((8, width), squares, F32), d_second], axis=0)
    blocks = (local, bsize, bsize)
    outs = [((1, LANES), F32), (blocks, F32), (blocks, BF)] + [(blocks, F32)] * 7
    outs += [((width, embed), F32)] * 4 + [((2, embed, embed), F32)] * 3 + [((2, width), F32)] * 3
    new = call(
        functools.partial(step_kernel, n=n if masked else 1),
        outs,
        [
            me, owners, got, grad, d_norm, d_towers,
            w_hidden, stat_left, stat_right, basis_left, basis_right,
            mom1_hidden, mom2_hidden, ema_hidden,
            w_out, mom1_out, mom2_out, ema_out,
            w_towers, mom1_towers, mom2_towers,
            w_norm, mom1_norm, mom2_norm,
        ],
        smem=2,
        scratch=[
            pltpu.VMEM((2 * local, bsize, 2 * bsize), F32),
            pltpu.VMEM((embed, width), F32),
            pltpu.VMEM((2, width), F32),
        ],
        name="step",
    )
    return (loss_sum, count, new[0][0, 0], *new[1:])


def solution(mesh):
    split = P(("gx", "gy"))
    plan = Plan(mesh.shape["gx"], mesh.shape["gy"])
    return jax.shard_map(
        functools.partial(on_device, plan),
        mesh=mesh,
        in_specs=(split, P(), split, split, P()) + (split,) * 8 + (P(),) * 10,
        out_specs=(P(),) * 3 + (split,) * 9 + (P(),) * 10,
        check_vma=False,
    )
```

```python
import functools
import math

import jax
import jax.numpy as jnp
from jax import lax
from jax.experimental import pallas as pl
from jax.experimental.pallas import tpu as pltpu
from jax.sharding import PartitionSpec as P

FIELDS = 4
BAG = 8
HASH_RANGE = 4096
STEP = 10
BETA_ONE = 0.9
BETA_TWO = 0.95
EPSILON = 1e-08
RATE = 0.03
DECAY = 0.01
CLIP = 0.01
AVG_KEEP = 0.8
AVG_TAKE = 0.2

F32 = jnp.float32
BF = jnp.bfloat16
HIGH = lax.Precision.HIGHEST
AXES = ("gx", "gy")
LANES = 128
SLOTS_BAG = FIELDS * BAG
PAIR = 16
MIB = 1 << 20


def dot(a, b, ca=1, cb=0, precision=None):
    return lax.dot_general(
        a, b, (((ca,), (cb,)), ((), ())), precision=precision, preferred_element_type=F32
    )


hdot = functools.partial(dot, precision=HIGH)


def spec(space=pltpu.VMEM):
    return pl.BlockSpec(memory_space=space)


def in_hbm(a):
    return pltpu.with_memory_space_constraint(a, pltpu.HBM)


def call(kernel, outs, args, smem=0, hbm=0, smem_outs=0, scratch=(), limit=16, name=None, cost=None):
    args = list(args)
    specs = [spec(pltpu.SMEM)] * smem + [spec()] * (len(args) - smem - hbm) + [spec(pltpu.HBM)] * hbm
    if hbm:
        args[-hbm:] = [in_hbm(a) for a in args[-hbm:]]
    spaces = [pltpu.VMEM] * (len(outs) - smem_outs) + [pltpu.SMEM] * smem_outs
    estimate = None
    if cost:
        estimate = pl.CostEstimate(flops=cost, bytes_accessed=cost // 100, transcendentals=0)
    return pl.pallas_call(
        kernel,
        out_shape=[jax.ShapeDtypeStruct(s, t) for s, t in outs],
        in_specs=specs,
        out_specs=[spec(space) for space in spaces],
        scratch_shapes=list(scratch),
        compiler_params=pltpu.CompilerParams(vmem_limit_bytes=limit * MIB),
        cost_estimate=estimate,
        name=name,
    )(*args)


def fetch(sources, targets, sems):
    copies = [pltpu.make_async_copy(a, b, sems.at[i]) for i, (a, b) in enumerate(zip(sources, targets))]
    for c in copies:
        c.start()
    for c in copies:
        c.wait()


def swap_halves(v):
    half = v.shape[1] // 2
    return jnp.concatenate([v[:, half:], v[:, :half]], axis=1)


def place(q, side):
    shift = side.bit_length() - 1
    return q >> shift, (q & (side - 1)) >> 1, q & 1


class Plan:
    def __init__(self, gx, gy):
        self.gx, self.gy, self.n = gx, gy, gx * gy
        self.core = gy
        self.x = 2 * gy
        self.y = 1
        bits = []
        b = 2
        while b < gy:
            bits.append(b)
            b *= 2
        b = 4
        while b < gx:
            bits.append(b * gy)
            b *= 2
        self.bits = bits
        rest = [0]
        for b in bits:
            rest = rest + [m | b for m in rest]
        self.rest = rest

    def swap(self, a, mask):
        mx, my = mask // self.gy, mask % self.gy
        if my == 0:
            return lax.ppermute(a, "gx", [(i, i ^ mx) for i in range(self.gx)])
        if mx == 0:
            return lax.ppermute(a, "gy", [(i, i ^ my) for i in range(self.gy)])
        return lax.ppermute(a, AXES, [(i, i ^ mask) for i in range(self.n)])


def pack_kernel(
    me_ref, owners_ref, w_hbm, neg_hbm, seg_hbm, out_ref, w_ref, neg_ref, seg_ref, sems, *, masked
):
    fetch((w_hbm, neg_hbm, seg_hbm), (w_ref, neg_ref, seg_ref), sems)
    local, bsize = w_ref.shape[0], w_ref.shape[1]
    half = bsize // 2
    for b in range(local):
        odd = owners_ref[me_ref[0] * local + b] % 2
        top, low = w_ref[b, :half, :], w_ref[b, half:, :]
        left = jnp.where(odd == 1, low, top)
        right = jnp.where(odd == 1, top, low)
        out_ref[b * half : (b + 1) * half, :] = jnp.concatenate([left, right], axis=1).astype(BF)
    at = local * half
    if masked:
        for c in range(neg_ref.shape[1] // LANES):
            part = neg_ref[:, c * LANES : (c + 1) * LANES].astype(F32)
            out_ref[at : at + PAIR, :] = part.astype(BF)
            at += PAIR
    used = jnp.sum(seg_ref[...].astype(F32), axis=0, keepdims=True)
    out_ref[at : at + PAIR, :] = jnp.broadcast_to(used, (PAIR, LANES)).astype(BF)


def gather_pieces(plan, payload, cut, zero, early, late):
    stack = payload[None]
    if len(plan.rest) <= 4:
        stack = jnp.concatenate([stack] + [plan.swap(stack, m) for m in plan.rest[1:]], axis=0)
    else:
        for b in plan.bits:
            stack = jnp.concatenate([stack, plan.swap(stack, b)], axis=0)
    stack, early = lax.optimization_barrier((stack, early))
    by_x = plan.swap(stack, plan.x)
    by_y = plan.swap(stack, plan.y)
    by_x, by_y, late = lax.optimization_barrier((by_x, by_y, late))
    first = plan.swap(by_x[:, :cut] + zero, plan.y)
    second = plan.swap(by_y[:, cut:] + zero, plan.x)
    mine = [
        (stack, 0, 0),
        (by_x, plan.x, 0),
        (by_y, plan.y, 0),
        (first, plan.x | plan.y, 0),
        (second, plan.x | plan.y, cut),
    ]
    other = [(plan.swap(a, plan.core), m | plan.core, row) for a, m, row in mine]
    return mine + other, early, late


def hash_kernel(codes_hbm, offsets_hbm, x_ref, xt_ref, codes_ref, offsets_ref, sems):
    rows, width = codes_ref.shape
    groups = 2 * FIELDS
    step = 128
    head = pltpu.make_async_copy(offsets_hbm, offsets_ref, sems.at[0])
    head.start()
    parts = []
    for i in range(rows // step):
        at = pl.ds(i * step, step)
        parts.append(pltpu.make_async_copy(codes_hbm.at[at], codes_ref.at[at], sems.at[1 + i]))
        parts[i].start()
    head.wait()
    for i, part in enumerate(parts):
        part.wait()
        at = slice(i * step, (i + 1) * step)
        salted = codes_ref[at, :].reshape(-1, groups, BAG, width) + offsets_ref[...][None, :, None, :]
        salted = (salted & (HASH_RANGE - 1)).reshape(step, width)
        x = (salted.astype(F32) * (2.0 / (HASH_RANGE - 1)) - 1.0).astype(BF)
        x_ref[at, :] = x
        xt_ref[:, at] = x.T


def hash_inputs(codes, offsets):
    rows, width = codes.shape
    return call(
        hash_kernel,
        [((rows, width), BF), ((width, rows), BF)],
        [codes, offsets],
        hbm=2,
        scratch=[
            pltpu.VMEM(codes.shape, jnp.int32),
            pltpu.VMEM(offsets.shape, jnp.int32),
            pltpu.SemaphoreType.DMA((1 + rows // 128,)),
        ],
        limit=12,
        name="hash",
        cost=20_000_000,
    )


def pre_kernel(*refs, holds, rest, local, masked, n, pieces):
    me_ref, owners_ref = refs[:2]
    piece_refs = refs[2 : 2 + pieces]
    x_ref, live_ref = refs[2 + pieces : 4 + pieces]
    pre_ref, stats_ref, count_ref, mask_ref, w_ref, row_ref = refs[4 + pieces :]
    width = x_ref.shape[1]
    bsize = LANES // 2
    half = bsize // 2
    side = width // bsize
    tiles = width // LANES
    me = me_ref[0]
    chunks = mask_ref.shape[1] // LANES if masked else 0
    for piece, (base, row0) in zip(piece_refs, holds):
        held = piece.shape[1]
        for k, m in enumerate(rest):
            d = me ^ (m | base)
            for b in range(local):
                at = b * half - row0
                if at < 0 or at + half > held:
                    continue
                r, c, odd = place(owners_ref[d * local + b], side)
                tile = piece[k, at : at + half, :]
                rows = pl.multiple_of(r * bsize, bsize)
                low = pl.multiple_of(r * bsize + half, half)
                cols = pl.ds(pl.multiple_of(c * LANES, LANES), LANES)
                w_ref[odd, pl.ds(rows, half), cols] = tile
                w_ref[odd, pl.ds(low, half), cols] = swap_halves(tile)
            for c in range(chunks):
                at = local * half + c * PAIR - row0
                if at < 0 or at + PAIR > held:
                    continue
                mask_ref[pl.ds(pl.multiple_of(d * PAIR, PAIR), PAIR), c * LANES : (c + 1) * LANES] = (
                    piece[k, at : at + PAIR, :]
                )
            at = local * half + chunks * PAIR - row0
            if 0 <= at and at + PAIR <= held:
                count_ref[pl.ds(d, 1), :] = piece[k, at : at + PAIR, :].astype(F32)[:1]
    live = live_ref[...]
    used = jnp.maximum(jnp.sum(live[:, :1]), 1.0)
    step = 2 * LANES
    left = lax.broadcasted_iota(jnp.int32, (width, step), 1) % LANES < bsize
    for j in range(width // step):
        cols = slice(j * step, (j + 1) * step)
        pre_ref[:, cols] = dot(x_ref[...], jnp.where(left, w_ref[0, :, cols], w_ref[1, :, cols]))
        for i in range(2):
            t = 2 * j + i
            tile = slice(t * LANES, (t + 1) * LANES)
            total = jnp.sum(pre_ref[:, tile] * live, axis=0, keepdims=True)
            apart = pre_ref[:, tile] - total / used
            row_ref[t : t + 1, :] = total
            row_ref[tiles + t : tiles + t + 1, :] = jnp.sum(
                apart * apart * live, axis=0, keepdims=True
            )
    for d in range(n):
        stats_ref[d * 2 * tiles : (d + 1) * 2 * tiles, :] = row_ref[...]


def act_kernel(
    stats_ref, count_ref, norm_ref, pre_ref, live_ref, pick_ref, w_out_ref,
    slope_ref, act_ref, one_ref, two_ref, coef_ref, bags_ref, pay_ref,
    low_ref, ones_ref, twos_ref,
):
    n = count_ref.shape[0]
    rows, width = pre_ref.shape
    tiles = width // LANES
    counts = jnp.sum(count_ref[...], axis=1, keepdims=True)
    used = jnp.sum(counts)
    total = stats_ref[0:tiles, :]
    for d in range(1, n):
        total = total + stats_ref[2 * d * tiles : (2 * d + 1) * tiles, :]
    mean = total / used
    square = jnp.zeros_like(mean)
    for d in range(n):
        c = counts[d : d + 1, :]
        apart = stats_ref[2 * d * tiles : (2 * d + 1) * tiles, :] / jnp.maximum(c, 1.0) - mean
        square = square + (
            stats_ref[(2 * d + 1) * tiles : (2 * d + 2) * tiles, :] + c * apart * apart
        )
    rstd = lax.rsqrt(square / used + 1e-05)
    for j in range(tiles):
        coef_ref[0:1, j * LANES : (j + 1) * LANES] = mean[j : j + 1, :]
        coef_ref[1:2, j * LANES : (j + 1) * LANES] = rstd[j : j + 1, :]
    coef_ref[2:3, :] = jnp.full((1, width), used, F32)
    coef_ref[3:4, :] = coef_ref[1:2, :] * norm_ref[0:1, :]
    bags = rows // SLOTS_BAG
    group = 8

    def fold(v):
        return (v[:group] + v[group : 2 * group]) + (v[2 * group : 3 * group] + v[3 * group :])

    def unfold(ref, j):
        total = ref[j, pl.ds(0, bags, stride=group), :]
        for i in range(1, group):
            total = total + ref[j, pl.ds(i, bags, stride=group), :]
        return total

    for j in range(tiles):
        cols = slice(j * LANES, (j + 1) * LANES)
        centre, scale, bias = coef_ref[0:1, cols], coef_ref[3:4, cols], norm_ref[1:2, cols]
        for b in range(bags):
            at = slice(b * SLOTS_BAG, (b + 1) * SLOTS_BAG)
            to = slice(b * group, (b + 1) * group)
            apart = pre_ref[at, cols] - centre
            y = scale * apart + bias
            capped = jnp.minimum(y, 20.0)
            e = jnp.exp(capped)
            top = e * (e + 2.0)
            below = top + 2.0
            guess = pl.reciprocal(below, approx=True)
            inv = guess * (2.0 - below * guess)
            gate = top * inv
            low_ref[at, :] = (y * gate).astype(BF)
            part = e * inv
            slope = gate + (4.0 * capped) * (part * (inv + part))
            slope_ref[at, cols] = slope
            slope = slope * live_ref[at, :]
            ones_ref[j, to, :] = fold(slope)
            twos_ref[j, to, :] = fold(slope * apart)
        act_ref[:, cols] = dot(pick_ref[...], low_ref[...])
        one_ref[:, cols] = unfold(ones_ref, j)
        two_ref[:, cols] = unfold(twos_ref, j) * coef_ref[1:2, cols]
    second = w_out_ref[...].astype(BF).astype(F32)
    bags = hdot(act_ref[...], second, 1, 1)
    pairs = bags.shape[0] // 2
    split = jnp.concatenate([hdot(pick(pairs, 0), bags), hdot(pick(pairs, 1), bags)], axis=0)
    bags_ref[...] = split
    eighth = pairs // 2
    packed = jnp.concatenate([split[i * eighth : (i + 1) * eighth] for i in range(4)], axis=1)
    for d in range(n):
        pay_ref[d * eighth : (d + 1) * eighth, :] = packed


def pick(pairs, which):
    r = lax.broadcasted_iota(jnp.int32, (pairs, 2 * pairs), 0)
    c = lax.broadcasted_iota(jnp.int32, (pairs, 2 * pairs), 1)
    return (c == 2 * r + which).astype(F32)


def spread(pairs, which):
    r = lax.broadcasted_iota(jnp.int32, (2 * pairs, pairs), 0)
    c = lax.broadcasted_iota(jnp.int32, (2 * pairs, pairs), 1)
    return (r == 2 * c + which).astype(F32)


def three(v):
    a = v.astype(BF)
    v = v - a.astype(F32)
    b = v.astype(BF)
    v = v - b.astype(F32)
    return a, b, v.astype(BF)


def loss_kernel(
    me_ref, all_ref, mask_ref, towers_ref, w_out_ref, act_ref, one_ref, two_ref,
    dact_ref, pay_ref, d_towers_ref, loss_ref, total_ref,
    score_ref, user_ref, item_ref, second_ref, row_ref, *, n,
):
    me = me_ref[0]
    embed = towers_ref.shape[1]
    total_rows = mask_ref.shape[0]
    eighth = all_ref.shape[0] // n

    def full(i):
        a = all_ref[:, 2 * i * embed : (2 * i + 1) * embed].reshape(n, eighth, embed)
        b = all_ref[:, (2 * i + 1) * embed : (2 * i + 2) * embed].reshape(n, eighth, embed)
        return jnp.stack([a, b], axis=1).reshape(total_rows, embed)

    bags_user, bags_item = full(0), full(1)
    user = hdot(bags_user, towers_ref[0]).astype(BF)
    item = hdot(bags_item, towers_ref[1]).astype(BF)
    root = math.sqrt(embed)
    score_ref[...] = dot(user, item, 1, 1) / root
    negatives = jnp.sum(mask_ref[...].astype(F32))
    count = negatives / total_rows
    step = 32

    def rows(i, carry):
        at = slice(i * step, (i + 1) * step)
        logits = score_ref[at, :]
        r = lax.broadcasted_iota(jnp.int32, logits.shape, 0) + i * step
        own = r == lax.broadcasted_iota(jnp.int32, logits.shape, 1)
        keep = own | (mask_ref[at, :].astype(F32) == 1.0)
        top = jnp.max(jnp.where(keep, logits, -jnp.inf), axis=1, keepdims=True)
        weights = jnp.where(keep, jnp.exp(logits - top), 0.0)
        total = jnp.sum(weights, axis=1, keepdims=True)
        hit = jnp.sum(jnp.where(own, logits, 0.0), axis=1, keepdims=True)
        score_ref[at, :] = (weights / total - own.astype(F32)) / count / root
        return carry + (top + jnp.log(total) - hit)

    ce = jnp.zeros((step, 1), F32)
    for i in range(total_rows // step):
        ce = rows(i, ce)
    loss_ref[0, 0] = jnp.sum(ce)
    total_ref[0, 0] = count
    parts = three(score_ref[...])
    d_user = sum(dot(p, item) for p in parts)
    d_item = sum(dot(user, p, 0, 0) for p in parts).T
    user_ref[...] = d_user
    item_ref[...] = d_item
    d_towers_ref[0] = hdot(bags_user, d_user, 0, 0)
    d_towers_ref[1] = hdot(bags_item, d_item, 0, 0)
    mine = pl.ds(pl.multiple_of(me * PAIR, PAIR), PAIR)
    back_user = hdot(user_ref[mine, :], towers_ref[0], 1, 1).astype(BF).astype(F32)
    back_item = hdot(item_ref[mine, :], towers_ref[1], 1, 1).astype(BF).astype(F32)
    d_emb = dot(spread(PAIR, 0), back_user) + dot(spread(PAIR, 1), back_item)
    d_act = dot(d_emb.astype(BF), w_out_ref[...].astype(BF))
    dact_ref[...] = d_act
    d_bias = jnp.sum(d_act * one_ref[...], axis=0, keepdims=True)
    d_gain = jnp.sum(d_act * two_ref[...], axis=0, keepdims=True)
    d_low = d_emb.T.astype(BF)
    second = sum(dot(d_low, p) for p in three(act_ref[...]))
    width = act_ref.shape[1]
    tiles = width // LANES
    for j in range(tiles):
        second_ref[pl.ds(j, embed, stride=tiles), :] = second[:, j * LANES : (j + 1) * LANES]
    for j in range(tiles):
        cols = slice(j * LANES, (j + 1) * LANES)
        row_ref[j : j + 1, :] = d_bias[:, cols]
        row_ref[tiles + j : tiles + j + 1, :] = d_gain[:, cols]
    sums = row_ref[...].astype(BF)
    chunk = embed * tiles // n
    for d in range(n):
        part = second_ref[d * chunk : (d + 1) * chunk, :]
        high = part.astype(BF)
        low = (part - high.astype(F32)).astype(BF)
        at = d * (2 * tiles + 2 * chunk)
        pay_ref[at : at + 2 * tiles, :] = sums
        pay_ref[at + 2 * tiles : at + 2 * tiles + 2 * chunk, :] = jnp.concatenate([high, low], axis=0)


def loss_spread(plan, bags, neg_mask, towers, w_out, act, one, two):
    embed = towers.shape[1]
    rows = neg_mask.shape[0]
    bags_user, bags_item = bags[:rows], bags[rows:]
    user = hdot(bags_user, towers[0]).astype(BF)
    item = hdot(bags_item, towers[1]).astype(BF)
    items = lax.all_gather(item, AXES, axis=0, tiled=True)
    root = math.sqrt(embed)
    logits = dot(user, items, 1, 1) / root
    at = lax.axis_index(AXES) * rows + lax.broadcasted_iota(jnp.int32, logits.shape, 0)
    own = lax.broadcasted_iota(jnp.int32, logits.shape, 1) == at
    keep = own | (neg_mask == 1)
    top = jnp.max(jnp.where(keep, logits, -jnp.inf), axis=1, keepdims=True)
    weights = jnp.where(keep, jnp.exp(logits - top), 0.0)
    total = jnp.sum(weights, axis=1, keepdims=True)
    ce = top + jnp.log(total) - jnp.sum(jnp.where(own, logits, 0.0), axis=1, keepdims=True)
    count = lax.psum(jnp.sum(neg_mask.astype(F32)), AXES) / items.shape[0]
    scores = (weights / total - own.astype(F32)) / count / root
    d_user = hdot(scores, items.astype(F32))
    d_item = lax.psum_scatter(
        hdot(scores, user.astype(F32), 0, 0), AXES, scatter_dimension=0, tiled=True
    )
    d_towers = jnp.stack([hdot(bags_user, d_user, 0, 0), hdot(bags_item, d_item, 0, 0)])
    back = jnp.stack([hdot(d_user, towers[0], 1, 1), hdot(d_item, towers[1], 1, 1)], axis=1)
    d_emb = back.reshape(2 * rows, embed).astype(BF)
    d_act = dot(d_emb, w_out.astype(BF))
    d_second = hdot(d_emb.astype(F32), act, 0, 0)
    sums = jnp.stack([jnp.sum(d_act * one, axis=0), jnp.sum(d_act * two, axis=0)])
    sums, d_second, d_towers, loss = lax.psum((sums, d_second, d_towers, jnp.sum(ce)), AXES)
    return d_act, sums.reshape(-1, LANES), d_second, d_towers, loss, count


def grad_kernel(
    me_ref, owners_ref, sums_ref, coef_ref, norm_ref, dact_ref, slope_ref, pre_ref, live_ref, xt_ref,
    keep_ref, send_ref, chunk_ref, d_norm_ref, d_pre_ref, g_ref, row_ref,
    *, parts, order, local,
):
    rows, width = pre_ref.shape
    tiles = width // LANES
    held = sums_ref.shape[0] // parts
    total = sums_ref[0:held, :].astype(F32)
    for d in range(1, parts):
        total = total + sums_ref[d * held : (d + 1) * held, :].astype(F32)
    d_norm_ref[0:tiles, :] = total[tiles : 2 * tiles]
    d_norm_ref[tiles : 2 * tiles, :] = total[:tiles]
    if held > 2 * tiles:
        chunk = chunk_ref.shape[0]
        chunk_ref[...] = total[2 * tiles : 2 * tiles + chunk] + total[2 * tiles + chunk :]
    else:
        chunk_ref[...] = jnp.zeros(chunk_ref.shape, F32)
    for j in range(tiles):
        cols = slice(j * LANES, (j + 1) * LANES)
        row_ref[0:1, cols] = total[j : j + 1]
        row_ref[1:2, cols] = total[tiles + j : tiles + j + 1]
    scale = norm_ref[0:1, :] * coef_ref[1:2, :]
    flat = scale * row_ref[0:1, :] / coef_ref[2:3, :]
    tilt = scale * row_ref[1:2, :] / coef_ref[2:3, :] * coef_ref[1:2, :]
    row_ref[2:3, :] = scale
    row_ref[3:4, :] = flat
    row_ref[4:5, :] = tilt
    block = 2 * LANES
    for j in range(width // block):
        for i in range(2):
            cols = slice(j * block + i * LANES, j * block + (i + 1) * LANES)
            for b in range(rows // SLOTS_BAG):
                at = slice(b * SLOTS_BAG, (b + 1) * SLOTS_BAG)
                lead = dact_ref[b : b + 1, cols] * row_ref[2:3, cols]
                apart = (pre_ref[at, cols] - coef_ref[0:1, cols]) * row_ref[4:5, cols]
                d_pre = slope_ref[at, cols] * lead - row_ref[3:4, cols] - apart
                d_pre_ref[at, cols] = (live_ref[at, :] * d_pre).astype(BF)
        cols = slice(j * block, (j + 1) * block)
        g_ref[:, cols] = dot(xt_ref[...], d_pre_ref[:, cols])
    bsize = LANES // 2
    half = bsize // 2
    side = width // bsize
    lane_half = lax.broadcasted_iota(jnp.int32, (half, LANES), 1) // bsize
    me = me_ref[0]
    for out, masks in ((send_ref, order[1]), (keep_ref, order[0])):
        for i, m in enumerate(masks):
            for b in range(local):
                r, c, odd = place(owners_ref[(me ^ m) * local + b], side)
                at = pl.ds(pl.multiple_of(r * bsize, bsize), half)
                low = pl.ds(pl.multiple_of(r * bsize + half, half), half)
                cols = pl.ds(pl.multiple_of(c * LANES, LANES), LANES)
                to = (i * local + b) * half
                out[to : to + half, :] = jnp.where(
                    lane_half == odd,
                    g_ref[at, cols].astype(out.dtype),
                    swap_halves(g_ref[low, cols].astype(out.dtype)),
                )


def scatter_sum(plan, keep, send, rows):
    rest = len(plan.rest)
    shape = (2, 2, rest, rows, LANES)
    got = plan.swap(send, plan.core)
    mine = (keep + got.astype(F32)).reshape(shape)
    cut = rows // 2
    one, two = mine[..., :cut, :], mine[..., cut:, :]
    got_one = plan.swap(one[1].astype(BF), plan.x)
    got_two = plan.swap(two[:, 1].astype(BF), plan.y)
    one = one[0] + got_one.astype(F32)
    two = two[:, 0] + got_two.astype(F32)
    got_one = plan.swap(one[1].astype(BF), plan.y)
    got_two = plan.swap(two[1].astype(BF), plan.x)
    one = one[0] + got_one.astype(F32)
    two = two[0] + got_two.astype(F32)
    if rest <= 4:
        both = jnp.concatenate([one[1:], two[1:]], axis=1).astype(BF)
        return one, two, [plan.swap(both[k], m) for k, m in enumerate(plan.rest[1:])]
    both = jnp.concatenate([one, two], axis=1)
    for b in reversed(plan.bits):
        both = both.reshape(2, -1, rows, LANES)
        both = both[0] + plan.swap(both[1].astype(BF), b).astype(F32)
    return both[:, :cut], both[:, cut:], []


def norm_kernel(*refs, n):
    one_ref, two_ref, chunk_ref = refs[:3]
    got = refs[3:-2]
    g_ref, pay_ref = refs[-2:]
    total = jnp.concatenate([one_ref[0], two_ref[0]], axis=0)
    for g in got:
        total = total + g[...].astype(F32)
    g_ref[...] = total
    chunk = chunk_ref[...]
    squares = jnp.sum(total * total, keepdims=True) + jnp.sum(chunk * chunk, keepdims=True)
    high = chunk.astype(BF)
    low = chunk - high.astype(F32)
    for i, v in enumerate(three(squares)):
        low = jnp.where(spare(chunk.shape, i), v.astype(F32), low)
    packed = jnp.concatenate([high, low.astype(BF)], axis=0)
    rows = packed.shape[0]
    for d in range(n):
        pay_ref[d * rows : (d + 1) * rows, :] = packed


def spare(shape, i):
    row = lax.broadcasted_iota(jnp.int32, shape, 0)
    lane = lax.broadcasted_iota(jnp.int32, shape, 1)
    return (row == shape[0] - 1) & (lane == LANES - 3 + i)


def adamw(grad, weight, first, second):
    first = BETA_ONE * first + (1 - BETA_ONE) * grad
    second = BETA_TWO * second + (1 - BETA_TWO) * grad * grad
    step = (
        first / (1 - BETA_ONE**STEP) / (jnp.sqrt(second / (1 - BETA_TWO**STEP)) + EPSILON)
    )
    return weight - RATE * (step + DECAY * weight), first, second


def panel_factor(panel, at):
    group = panel.shape[1]
    index = lax.broadcasted_iota(jnp.int32, (1, group, 1), 1)
    cols = [jnp.broadcast_to(panel[:, :, at + i : at + i + 1], panel.shape) for i in range(group)]
    for i in range(group):
        inv = lax.rsqrt(cols[i][:, i : i + 1, :])
        row = panel[:, i : i + 1, :] * inv
        f = cols[i] * inv
        panel = jnp.where(index > i, panel - f * row, jnp.where(index == i, row, panel))
        for j in range(i + 1, group):
            cols[j] = cols[j] - f * f[:, j : j + 1, :]
    return panel


def eliminate(mat_ref):
    count, size = mat_ref.shape[0], mat_ref.shape[1]
    group = 8
    for at in range(0, size, group):
        rest = at + group
        panel = panel_factor(mat_ref[:, at:rest, :], at)
        mat_ref[:, at:rest, :] = panel
        if rest == size:
            return
        a, b, c = (v.astype(F32) for v in three(panel))
        lhs = jnp.concatenate([a, a, b, b, a, c], axis=1)
        rhs = jnp.concatenate([a, b, a, b, c, a], axis=1).astype(BF)
        for m in range(count):
            turned = lhs[m].T[rest:size, :].astype(BF)
            mat_ref[m, rest:, :] = mat_ref[m, rest:, :] - dot(turned, rhs[m])


def pair(a, b):
    return jnp.concatenate([a, b], axis=1)


def prepare_kernel(
    w_hbm, left_hbm, right_hbm, bl_hbm, br_hbm, first_hbm, second_hbm, ema_hbm,
    moments_ref, stats_ref, bases_ref, weights_ref, turned_ref, powers_ref,
    w_ref, left_ref, right_ref, bl_ref, br_ref, first_ref, second_ref, ema_ref, sems,
):
    fetch(
        (w_hbm, left_hbm, right_hbm, bl_hbm, br_hbm, first_hbm, second_hbm, ema_hbm),
        (w_ref, left_ref, right_ref, bl_ref, br_ref, first_ref, second_ref, ema_ref),
        sems,
    )
    each = range(w_ref.shape[0])
    for b in each:
        moments_ref[b] = pair(first_ref[b], second_ref[b])
        stats_ref[b] = pair(left_ref[b], right_ref[b])
        bases_ref[b] = pair(bl_ref[b], br_ref[b])
        weights_ref[b] = pair(w_ref[b], ema_ref[b])
    half = [hdot(bl_ref[b], first_ref[b], 0, 0) for b in each]
    for b in each:
        turned_ref[b] = hdot(half[b], br_ref[b])
    lefts = [hdot(bl_ref[b], left_ref[b], 0, 0) for b in each]
    rights = [hdot(br_ref[b], right_ref[b], 0, 0) for b in each]
    for b in each:
        powers_ref[b] = pair(lefts[b], rights[b])


def turn_kernel(
    me_ref, owners_ref, g_ref, bases_ref,
    wo_hbm, mo_hbm, vo_hbm, eo_hbm, wt_hbm, mt_hbm, vt_hbm, wn_hbm, mn_hbm, vn_hbm,
    grad_ref, squares_ref, powers_ref, scale_ref,
    wide_ref, towers_ref, norms_ref, sems,
):
    local, bsize = bases_ref.shape[0], bases_ref.shape[1]
    sources = (wo_hbm, mo_hbm, vo_hbm, eo_hbm, wt_hbm, mt_hbm, vt_hbm, wn_hbm, mn_hbm, vn_hbm)
    targets = [wide_ref.at[i] for i in range(4)]
    targets += [towers_ref.at[i] for i in range(3)] + [norms_ref.at[i] for i in range(3)]
    copies = [pltpu.make_async_copy(a, b, sems.at[i]) for i, (a, b) in enumerate(zip(sources, targets))]
    for c in copies:
        c.start()
    largest = jnp.max(jnp.abs(g_ref[...]), keepdims=True)
    largest = jnp.where(largest > 0.0, largest, 1.0)
    scale_ref[...] = jnp.broadcast_to(largest, scale_ref.shape)
    half = bsize // 2
    each = range(local)
    grads = []
    for b in each:
        odd = owners_ref[me_ref[0] * local + b] % 2
        tile = g_ref[b * half : (b + 1) * half, :]
        tile = jnp.where(odd == 1, swap_halves(tile), tile)
        grads.append(jnp.concatenate([tile[:, :bsize], tile[:, bsize:]], axis=0) / largest)
    bl = [bases_ref[b, :, :bsize] for b in each]
    br = [bases_ref[b, :, bsize:] for b in each]
    by_left = [hdot(bl[b], grads[b], 0, 0) for b in each]
    by_right = [hdot(grads[b], br[b]) for b in each]
    outer = [hdot(grads[b], grads[b], 1, 1) for b in each]
    inner = [hdot(grads[b], grads[b], 0, 0) for b in each]
    for b in each:
        squares_ref[b] = pair(outer[b], inner[b])
    for b in each:
        grad_ref[b] = pair(grads[b], hdot(by_left[b], br[b]))
    lefts = [hdot(by_left[b], grads[b], 1, 1) for b in each]
    rights = [hdot(by_right[b], grads[b], 0, 0) for b in each]
    for b in each:
        powers_ref[b] = pair(lefts[b], rights[b])
    for c in copies:
        c.wait()


def step_kernel(
    got_ref, d_norm_ref, d_towers_ref,
    grad_ref, squares_ref, powers_ref, scale_ref,
    old_ref, towers_ref, norms_ref,
    moments_ref, stats_ref, bases_ref, weights_ref, turned_first_ref, powers_old_ref,
    w_out, low_out, left_out, right_out, bl_out, br_out, first_out, second_out, ema_out,
    wo_out, mo_out, vo_out, eo_out, wt_out, mt_out, vt_out, wn_out, mn_out, vn_out, gn_out,
    mat_ref, wide_ref, dn_ref, flat_ref, *, n,
):
    local, bsize = bases_ref.shape[0], bases_ref.shape[1]
    embed, width = old_ref.shape[1:]
    tiles = width // LANES
    held = got_ref.shape[0] // n
    if n > 1:
        chunk = held // 2
        used = functools.reduce(jnp.logical_or, [spare((chunk, LANES), i) for i in range(3)])
        squares = jnp.zeros((chunk, LANES), F32)
        for d in range(n):
            part = got_ref[d * held : (d + 1) * held, :].astype(F32)
            squares = squares + jnp.where(used, part[chunk:], 0.0)
            flat_ref[d * chunk : (d + 1) * chunk, :] = part[:chunk] + jnp.where(used, 0.0, part[chunk:])
        squares = jnp.sum(squares)
        for j in range(tiles):
            wide_ref[:, j * LANES : (j + 1) * LANES] = flat_ref[pl.ds(j, embed, stride=tiles), :]
    else:
        squares = jnp.max(got_ref[0:1, :LANES])
        wide_ref[...] = got_ref[8 : 8 + embed, :]
    squares = squares + jnp.sum(d_towers_ref[...] * d_towers_ref[...])
    squares = squares + jnp.sum(d_norm_ref[...] * d_norm_ref[...])
    norm = jnp.sqrt(jnp.full((1, LANES), squares, F32))
    gn_out[0, 0] = jnp.max(norm)
    factor = (CLIP / jnp.maximum(norm, CLIP))[:, :1]
    each = range(local)
    lead = factor * scale_ref[0:1, 0:1]
    twice = (1 - BETA_TWO) * lead * lead
    lefts, rights = [], []
    for b in each:
        powers = BETA_TWO * powers_old_ref[b] + twice * powers_ref[b]
        lefts.append(powers[:, :bsize])
        rights.append(powers[:, bsize:])
    for b in each:
        mat_ref[2 * b] = pair(hdot(lefts[b], lefts[b], 1, 1), lefts[b])
        mat_ref[2 * b + 1] = pair(hdot(rights[b], rights[b], 1, 1), rights[b])
    ratios = []
    for b in each:
        stats = BETA_TWO * stats_ref[b] + twice * squares_ref[b]
        left_out[b], right_out[b] = stats[:, :bsize], stats[:, bsize:]
        first_out[b] = BETA_ONE * moments_ref[b, :, :bsize] + (1 - BETA_ONE) * lead * grad_ref[b, :, :bsize]
        turned = grad_ref[b, :, bsize:]
        second = BETA_TWO * moments_ref[b, :, bsize:] + twice * turned * turned
        second_out[b] = second
        moved = BETA_ONE * turned_first_ref[b] + (1 - BETA_ONE) * lead * turned
        moved = moved / (1 - BETA_ONE**STEP)
        ratios.append(moved / (jnp.sqrt(second / (1 - BETA_TWO**STEP)) + EPSILON))
    half = [hdot(bases_ref[b, :, :bsize], ratios[b]) for b in each]
    updates = [hdot(half[b], bases_ref[b, :, bsize:], 1, 1) for b in each]
    for b in each:
        old = weights_ref[b, :, :bsize]
        new = old - RATE * (updates[b] + DECAY * old)
        w_out[b] = new
        low_out[b] = new.astype(BF)
        ema_out[b] = AVG_KEEP * weights_ref[b, :, bsize:] + AVG_TAKE * new
    new, m, v = adamw(wide_ref[...] * factor, old_ref[0], old_ref[1], old_ref[2])
    wo_out[...], mo_out[...], vo_out[...] = new, m, v
    eo_out[...] = AVG_KEEP * old_ref[3] + AVG_TAKE * new
    for t in range(2):
        wt_out[t], mt_out[t], vt_out[t] = adamw(
            d_towers_ref[t] * factor, towers_ref[0, t], towers_ref[1, t], towers_ref[2, t]
        )
        for j in range(tiles):
            dn_ref[t : t + 1, j * LANES : (j + 1) * LANES] = d_norm_ref[
                t * tiles + j : t * tiles + j + 1, :
            ]
    wn_out[...], mn_out[...], vn_out[...] = adamw(
        dn_ref[...] * factor, norms_ref[0], norms_ref[1], norms_ref[2]
    )
    eliminate(mat_ref)
    for b in each:
        bl_out[b] = mat_ref[2 * b, :, bsize:].T
        br_out[b] = mat_ref[2 * b + 1, :, bsize:].T


def exchange(payload):
    return lax.all_to_all(payload, AXES, 0, 0, tiled=True)


def on_device(
    plan,
    codes, field_offsets, seg_mask, neg_mask, owners,
    w_hidden, stat_left, stat_right, basis_left, basis_right, mom1_hidden, mom2_hidden, ema_hidden,
    w_out, mom1_out, mom2_out, ema_out,
    w_towers, mom1_towers, mom2_towers,
    w_norm, mom1_norm, mom2_norm,
):
    n = plan.n
    local, bsize = w_hidden.shape[0], w_hidden.shape[1]
    width, embed = w_out.shape
    slots = codes.shape[0]
    rows, total_rows = neg_mask.shape
    tiles = width // LANES
    half = bsize // 2
    bags = slots // SLOTS_BAG
    masked = total_rows <= 1024 and n <= embed
    me = lax.axis_index(AXES).astype(jnp.int32)[None]

    chunks = total_rows // LANES if masked else 0
    size = local * half + chunks * PAIR + PAIR
    (payload,) = call(
        functools.partial(pack_kernel, masked=masked),
        [((size, LANES), BF)],
        [me, in_hbm(owners), w_hidden, neg_mask, seg_mask.reshape(-1, LANES)],
        smem=2,
        hbm=3,
        scratch=[
            pltpu.VMEM(w_hidden.shape, F32),
            pltpu.VMEM(neg_mask.shape, jnp.int32),
            pltpu.VMEM((slots // LANES, LANES), jnp.int32),
            pltpu.SemaphoreType.DMA((3,)),
        ],
        name="pack",
    )
    cut = max(half, size // 2 // half * half)
    cut = min(cut, local * half)
    blocks = (local, bsize, bsize)
    twin = (local, bsize, 2 * bsize)
    state = [
        w_hidden, stat_left, stat_right, basis_left, basis_right, mom1_hidden, mom2_hidden, ema_hidden
    ]
    prepared = call(
        prepare_kernel,
        [(twin, F32)] * 4 + [(blocks, F32), (twin, F32)],
        state,
        hbm=len(state),
        scratch=[pltpu.VMEM(blocks, F32)] * len(state) + [pltpu.SemaphoreType.DMA((len(state),))],
        limit=12,
        name="prepare",
        cost=10_000_000,
    )
    turned_out, turned_mom1, turned_mom2, turned_ema = (
        a.T for a in (w_out, mom1_out, mom2_out, ema_out)
    )
    early = hash_inputs(codes, field_offsets)
    live = jnp.broadcast_to(seg_mask.astype(F32)[:, None], (slots, LANES))
    slot_bag = lax.broadcasted_iota(jnp.int32, (bags, slots), 1) // SLOTS_BAG
    in_bag = slot_bag == lax.broadcasted_iota(jnp.int32, (bags, slots), 0)
    chosen = jnp.where(in_bag, seg_mask.astype(F32)[None], 0.0).astype(BF)
    late = (*prepared, live, chosen)
    zero = (me[0] >> 16).astype(BF)
    pieces, (x, x_turned), (*prepared, live, chosen) = gather_pieces(
        plan, payload, cut, zero, early, late
    )
    mask_shape = (total_rows, total_rows) if masked else (PAIR, LANES)
    pre, stats, counts, mask = call(
        functools.partial(
            pre_kernel,
            holds=[(m, row) for _, m, row in pieces],
            rest=plan.rest,
            local=local,
            masked=masked,
            n=n,
            pieces=len(pieces),
        ),
        [
            ((slots, width), F32),
            ((n * 2 * tiles, LANES), F32),
            ((n, LANES), F32),
            (mask_shape, BF),
        ],
        [me, owners] + [a for a, _, _ in pieces] + [x, live],
        smem=2,
        scratch=[pltpu.VMEM((2, width, width), BF), pltpu.VMEM((2 * tiles, LANES), F32)],
        limit=16,
        name="pre",
    )
    stats = exchange(stats)
    slope, act, one, two, coef, bag_sums, pay = call(
        act_kernel,
        [
            ((slots, width), F32),
            ((bags, width), F32),
            ((bags, width), F32),
            ((bags, width), F32),
            ((8, width), F32),
            ((bags, embed), F32),
            ((n * 8, LANES), F32),
        ],
        [stats, counts, w_norm, pre, live, chosen, turned_out],
        scratch=[
            pltpu.VMEM((slots, LANES), BF),
            pltpu.VMEM((tiles, bags * 8, LANES), F32),
            pltpu.VMEM((tiles, bags * 8, LANES), F32),
        ],
        limit=12,
        name="act",
    )
    if masked:
        chunk = embed * tiles // n
        everyone = exchange(pay)
        d_act, pay, d_towers, loss_sum, count = call(
            functools.partial(loss_kernel, n=n),
            [
                ((bags, width), F32),
                ((n * (2 * tiles + 2 * chunk), LANES), BF),
                ((2, embed, embed), F32),
                ((1, 1), F32),
                ((1, 1), F32),
            ],
            [me, everyone, mask, w_towers, turned_out, act, one, two],
            smem=1,
            smem_outs=2,
            scratch=[
                pltpu.VMEM((total_rows, total_rows), F32),
                pltpu.VMEM((total_rows, embed), F32),
                pltpu.VMEM((total_rows, embed), F32),
                pltpu.VMEM((embed * tiles, LANES), F32),
                pltpu.VMEM((2 * tiles, LANES), F32),
            ],
            name="loss",
        )
        sums, parts = exchange(pay), n
        loss_sum, count = loss_sum[0, 0], count[0, 0]
    else:
        d_act, sums, d_second, d_towers, loss_sum, count = loss_spread(
            plan, bag_sums, neg_mask, w_towers, turned_out, act, one, two
        )
        parts = 1
        chunk = 8
    groups = [m for m in (0, plan.y, plan.x, plan.x | plan.y)]
    keep_order = [g | r for g in groups for r in plan.rest]
    order = (keep_order, [m | plan.core for m in keep_order])
    kept, sent, second_chunk, d_norm = call(
        functools.partial(grad_kernel, parts=parts, order=order, local=local),
        [
            ((n // 2 * local * half, LANES), F32),
            ((n // 2 * local * half, LANES), BF),
            ((chunk, LANES), F32),
            ((2 * tiles, LANES), F32),
        ],
        [me, owners, sums, coef, w_norm, d_act, slope, pre, live, x_turned],
        smem=2,
        scratch=[
            pltpu.VMEM((slots, width), BF),
            pltpu.VMEM((width, width), F32),
            pltpu.VMEM((8, width), F32),
        ],
        limit=20,
        name="grad",
    )
    one_sum, two_sum, others = scatter_sum(plan, kept, sent, local * half)
    copies = n if masked else 1
    grad, pay = call(
        functools.partial(norm_kernel, n=copies),
        [((local * half, LANES), F32), ((copies * 2 * chunk, LANES), BF)],
        [one_sum, two_sum, second_chunk, *others],
        name="norm",
    )
    if masked:
        got = exchange(pay)
    else:
        squares = lax.psum(jnp.sum(grad * grad), AXES) + jnp.sum(d_second * d_second)
        got = jnp.concatenate([jnp.full((8, width), squares, F32), d_second], axis=0)
    moments, stats, bases, weights, turned_first, powers_old = prepared
    plain = [
        turned_out, turned_mom1, turned_mom2, turned_ema,
        w_towers, mom1_towers, mom2_towers,
        w_norm, mom1_norm, mom2_norm,
    ]
    turned = call(
        turn_kernel,
        [(twin, F32)] * 3
        + [((8, LANES), F32), ((4, embed, width), F32), ((3, 2, embed, embed), F32), ((3, 2, width), F32)],
        [me, owners, grad, bases, *plain],
        smem=2,
        hbm=len(plain),
        scratch=[pltpu.SemaphoreType.DMA((len(plain),))],
        name="turn",
        cost=10_000_000,
    )
    outs = [(blocks, F32), (blocks, BF)] + [(blocks, F32)] * 7
    outs += [((embed, width), F32)] * 4 + [((2, embed, embed), F32)] * 3 + [((2, width), F32)] * 3
    new = call(
        functools.partial(step_kernel, n=n if masked else 1),
        outs + [((1, 1), F32)],
        [
            got, d_norm, d_towers, *turned,
            moments, stats, bases, weights, turned_first, powers_old,
        ],
        smem_outs=1,
        scratch=[
            pltpu.VMEM((2 * local, bsize, 2 * bsize), F32),
            pltpu.VMEM((embed, width), F32),
            pltpu.VMEM((2, width), F32),
            pltpu.VMEM((embed * tiles, LANES), F32),
        ],
        name="step",
    )
    return (loss_sum, count, new[-1][0, 0], *new[:9], *(a.T for a in new[9:13]), *new[13:-1])


def solution(mesh):
    split = P(("gx", "gy"))
    plan = Plan(mesh.shape["gx"], mesh.shape["gy"])
    return jax.shard_map(
        functools.partial(on_device, plan),
        mesh=mesh,
        in_specs=(split, P(), split, split, P()) + (split,) * 8 + (P(),) * 10,
        out_specs=(P(),) * 3 + (split,) * 9 + (P(),) * 10,
        check_vma=False,
    )
```

```python
import functools
import math

import jax
import jax.numpy as jnp
from jax import lax
from jax.experimental import pallas as pl
from jax.experimental.pallas import tpu as pltpu
from jax.sharding import PartitionSpec as P

FIELDS = 4
BAG = 8
HASH_RANGE = 4096
STEP = 10
BETA_ONE = 0.9
BETA_TWO = 0.95
EPSILON = 1e-08
RATE = 0.03
DECAY = 0.01
CLIP = 0.01
AVG_KEEP = 0.8
AVG_TAKE = 0.2

F32 = jnp.float32
BF = jnp.bfloat16
HIGH = lax.Precision.HIGHEST
AXES = ("gx", "gy")
LANES = 128
SLOTS_BAG = FIELDS * BAG
PAIR = 16
MIB = 1 << 20


def dot(a, b, ca=1, cb=0, precision=None):
    return lax.dot_general(
        a, b, (((ca,), (cb,)), ((), ())), precision=precision, preferred_element_type=F32
    )


hdot = functools.partial(dot, precision=HIGH)


def spec(space=pltpu.VMEM):
    return pl.BlockSpec(memory_space=space)


def in_hbm(a):
    return pltpu.with_memory_space_constraint(a, pltpu.HBM)


def call(kernel, outs, args, smem=0, hbm=0, smem_outs=0, aliases=None, scratch=(), limit=16, name=None, cost=None):
    args = list(args)
    specs = [spec(pltpu.SMEM)] * smem + [spec()] * (len(args) - smem - hbm) + [spec(pltpu.HBM)] * hbm
    if hbm:
        args[-hbm:] = [in_hbm(a) for a in args[-hbm:]]
    spaces = [pltpu.VMEM] * (len(outs) - smem_outs) + [pltpu.SMEM] * smem_outs
    estimate = None
    if cost:
        estimate = pl.CostEstimate(flops=cost, bytes_accessed=cost // 100, transcendentals=0)
    return pl.pallas_call(
        kernel,
        out_shape=[jax.ShapeDtypeStruct(s, t) for s, t in outs],
        in_specs=specs,
        out_specs=[spec(space) for space in spaces],
        scratch_shapes=list(scratch),
        compiler_params=pltpu.CompilerParams(vmem_limit_bytes=limit * MIB),
        cost_estimate=estimate,
        input_output_aliases=aliases or {},
        name=name,
    )(*args)


def fetch(sources, targets, sems):
    copies = [pltpu.make_async_copy(a, b, sems.at[i]) for i, (a, b) in enumerate(zip(sources, targets))]
    for c in copies:
        c.start()
    for c in copies:
        c.wait()


def swap_halves(v):
    half = v.shape[1] // 2
    return jnp.concatenate([v[:, half:], v[:, :half]], axis=1)


def place(q, side):
    shift = side.bit_length() - 1
    return q >> shift, (q & (side - 1)) >> 1, q & 1


class Plan:
    def __init__(self, gx, gy):
        self.gx, self.gy, self.n = gx, gy, gx * gy
        self.core = gy
        self.x = 2 * gy
        self.y = 1
        bits = []
        b = 2
        while b < gy:
            bits.append(b)
            b *= 2
        b = 4
        while b < gx:
            bits.append(b * gy)
            b *= 2
        self.bits = bits
        rest = [0]
        for b in bits:
            rest = rest + [m | b for m in rest]
        self.rest = rest

    def swap(self, a, mask):
        mx, my = mask // self.gy, mask % self.gy
        if my == 0:
            return lax.ppermute(a, "gx", [(i, i ^ mx) for i in range(self.gx)])
        if mx == 0:
            return lax.ppermute(a, "gy", [(i, i ^ my) for i in range(self.gy)])
        return lax.ppermute(a, AXES, [(i, i ^ mask) for i in range(self.n)])


def pack_kernel(
    me_ref, owners_ref, w_hbm, neg_hbm, seg_hbm, out_ref, w_ref, neg_ref, seg_ref, sems, *, masked
):
    fetch((w_hbm, neg_hbm, seg_hbm), (w_ref, neg_ref, seg_ref), sems)
    local, bsize = w_ref.shape[0], w_ref.shape[1]
    half = bsize // 2
    for b in range(local):
        odd = owners_ref[me_ref[0] * local + b] % 2
        top, low = w_ref[b, :half, :], w_ref[b, half:, :]
        left = jnp.where(odd == 1, low, top)
        right = jnp.where(odd == 1, top, low)
        out_ref[b * half : (b + 1) * half, :] = jnp.concatenate([left, right], axis=1).astype(BF)
    at = local * half
    if masked:
        for c in range(neg_ref.shape[1] // LANES):
            part = neg_ref[:, c * LANES : (c + 1) * LANES].astype(F32)
            out_ref[at : at + PAIR, :] = part.astype(BF)
            at += PAIR
    used = jnp.sum(seg_ref[...].astype(F32), axis=0, keepdims=True)
    out_ref[at : at + PAIR, :] = jnp.broadcast_to(used, (PAIR, LANES)).astype(BF)


def gather_pieces(plan, payload, cut, zero, early, late):
    stack = payload[None]
    if len(plan.rest) <= 4:
        stack = jnp.concatenate([stack] + [plan.swap(stack, m) for m in plan.rest[1:]], axis=0)
    else:
        for b in plan.bits:
            stack = jnp.concatenate([stack, plan.swap(stack, b)], axis=0)
    stack, early = lax.optimization_barrier((stack, early))
    by_x = plan.swap(stack, plan.x)
    by_y = plan.swap(stack, plan.y)
    by_x, by_y, late = lax.optimization_barrier((by_x, by_y, late))
    first = plan.swap(by_x[:, :cut] + zero, plan.y)
    second = plan.swap(by_y[:, cut:] + zero, plan.x)
    mine = [
        (stack, 0, 0),
        (by_x, plan.x, 0),
        (by_y, plan.y, 0),
        (first, plan.x | plan.y, 0),
        (second, plan.x | plan.y, cut),
    ]
    other = [(plan.swap(a, plan.core), m | plan.core, row) for a, m, row in mine]
    return mine + other, early, late


def hash_kernel(codes_hbm, offsets_hbm, x_ref, xt_ref, codes_ref, offsets_ref, sems):
    rows, width = codes_ref.shape
    groups = 2 * FIELDS
    step = 128
    head = pltpu.make_async_copy(offsets_hbm, offsets_ref, sems.at[0])
    head.start()
    parts = []
    for i in range(rows // step):
        at = pl.ds(i * step, step)
        parts.append(pltpu.make_async_copy(codes_hbm.at[at], codes_ref.at[at], sems.at[1 + i]))
        parts[i].start()
    head.wait()
    for i, part in enumerate(parts):
        part.wait()
        at = slice(i * step, (i + 1) * step)
        salted = codes_ref[at, :].reshape(-1, groups, BAG, width) + offsets_ref[...][None, :, None, :]
        salted = (salted & (HASH_RANGE - 1)).reshape(step, width)
        x = (salted.astype(F32) * (2.0 / (HASH_RANGE - 1)) - 1.0).astype(BF)
        x_ref[at, :] = x
        xt_ref[:, at] = x.T


def hash_inputs(codes, offsets):
    rows, width = codes.shape
    return call(
        hash_kernel,
        [((rows, width), BF), ((width, rows), BF)],
        [codes, offsets],
        hbm=2,
        scratch=[
            pltpu.VMEM(codes.shape, jnp.int32),
            pltpu.VMEM(offsets.shape, jnp.int32),
            pltpu.SemaphoreType.DMA((1 + rows // 128,)),
        ],
        limit=12,
        name="hash",
        cost=20_000_000,
    )


def assemble(w_ref, me, owners_ref, piece_refs, holds, local):
    width = w_ref.shape[1]
    bsize = LANES // 2
    half = bsize // 2
    side = width // bsize
    for piece, (masks, row0) in zip(piece_refs, holds):
        for k, m in enumerate(masks):
            for b in range(local):
                at = b * half - row0
                if at < 0 or at + half > piece.shape[1]:
                    continue
                r, c, odd = place(owners_ref[(me ^ m) * local + b], side)
                tile = piece[k, at : at + half, :]
                rows = pl.multiple_of(r * bsize, bsize)
                low = pl.multiple_of(r * bsize + half, half)
                cols = pl.ds(pl.multiple_of(c * LANES, LANES), LANES)
                w_ref[odd, pl.ds(rows, half), cols] = tile
                w_ref[odd, pl.ds(low, half), cols] = swap_halves(tile)


def assemble_kernel(me_ref, owners_ref, *refs, holds, local):
    assemble(refs[-1], me_ref[0], owners_ref, refs[:-1], holds, local)


def pre_kernel(*refs, holds, done, local, masked, core):
    me_ref, owners_ref = refs[:2]
    pieces = len(holds)
    piece_refs = refs[3 : 3 + pieces]
    x_ref, live_ref = refs[3 + pieces : 5 + pieces]
    pre_ref, keep_ref, send_ref, count_ref, mask_ref, w_ref, row_ref = refs[5 + pieces :]
    width = x_ref.shape[1]
    bsize = LANES // 2
    half = bsize // 2
    tiles = width // LANES
    me = me_ref[0]
    chunks = mask_ref.shape[1] // LANES if masked else 0
    rest = [i for i in range(pieces) if i not in done]
    assemble(w_ref, me, owners_ref, [piece_refs[i] for i in rest], [holds[i] for i in rest], local)
    for piece, (masks, row0) in zip(piece_refs, holds):
        held = piece.shape[1]
        for k, m in enumerate(masks):
            d = me ^ m
            for c in range(chunks):
                at = local * half + c * PAIR - row0
                if at < 0 or at + PAIR > held:
                    continue
                mask_ref[pl.ds(pl.multiple_of(d * PAIR, PAIR), PAIR), c * LANES : (c + 1) * LANES] = (
                    piece[k, at : at + PAIR, :]
                )
            at = local * half + chunks * PAIR - row0
            if 0 <= at and at + PAIR <= held:
                count_ref[pl.ds(d, 1), :] = piece[k, at : at + PAIR, :].astype(F32)[:1]
    live = live_ref[...]
    used = jnp.maximum(jnp.sum(live[:, :1]), 1.0)
    step = 2 * LANES
    left = lax.broadcasted_iota(jnp.int32, (width, step), 1) % LANES < bsize
    for j in range(width // step):
        cols = slice(j * step, (j + 1) * step)
        pre_ref[:, cols] = dot(x_ref[...], jnp.where(left, w_ref[0, :, cols], w_ref[1, :, cols]))
        for i in range(2):
            t = 2 * j + i
            tile = slice(t * LANES, (t + 1) * LANES)
            total = jnp.sum(pre_ref[:, tile] * live, axis=0, keepdims=True)
            apart = pre_ref[:, tile] - total / used
            row_ref[t : t + 1, :] = total
            row_ref[tiles + t : tiles + t + 1, :] = jnp.sum(
                apart * apart * live, axis=0, keepdims=True
            )
    half = tiles // 2
    parts = [
        jnp.concatenate([row_ref[h * half : (h + 1) * half, :], row_ref[tiles + h * half : tiles + (h + 1) * half, :]])
        for h in range(2)
    ]
    odd = (me // core) % 2
    keep_ref[...] = jnp.where(odd == 1, parts[1], parts[0])
    send_ref[...] = jnp.where(odd == 1, parts[0], parts[1])


def combine(pairs):
    used = sum(c for c, _, _ in pairs)
    total = sum(t for _, t, _ in pairs)
    mean = total / jnp.maximum(used, 1.0)
    square = 0.0
    for c, t, q in pairs:
        apart = t / jnp.maximum(c, 1.0) - mean
        square = square + (q + c * apart * apart)
    return used, total, square


def merge_kernel(me_ref, count_ref, keep_ref, got_ref, out_ref, *, core):
    half = keep_ref.shape[0] // 2
    n = count_ref.shape[0]
    counts = [
        jnp.sum(count_ref[pl.ds(d, 1), :], keepdims=True) for d in (me_ref[0], me_ref[0] ^ core)
    ]
    pairs = [(c, ref[:half, :], ref[half:, :]) for c, ref in zip(counts, (keep_ref, got_ref))]
    _, total, square = combine(pairs)
    packed = jnp.concatenate([total, square])
    for d in range(n):
        out_ref[2 * half * d : 2 * half * (d + 1), :] = packed


def act_kernel(
    stats_ref, count_ref, norm_ref, pre_ref, live_ref, pick_ref, w_out_ref,
    slope_ref, act_ref, one_ref, two_ref, coef_ref, bags_ref, pay_ref,
    low_ref, ones_ref, twos_ref,
    *, core,
):
    n = count_ref.shape[0]
    rows, width = pre_ref.shape
    tiles = width // LANES
    counts = jnp.sum(count_ref[...], axis=1, keepdims=True)
    half = tiles // 2
    used, total, square = [], [], []
    for h in range(2):
        pairs = [
            (
                counts[d : d + 1, :] + counts[d ^ core : (d ^ core) + 1, :],
                stats_ref[d * tiles : d * tiles + half, :],
                stats_ref[d * tiles + half : (d + 1) * tiles, :],
            )
            for d in range(n)
            if (d // core) % 2 == h
        ]
        for held, v in zip((used, total, square), combine(pairs)):
            held.append(v)
    used = jnp.max(used[0])
    mean, square = jnp.concatenate(total) / used, jnp.concatenate(square)
    rstd = lax.rsqrt(square / used + 1e-05)
    for j in range(tiles):
        coef_ref[0:1, j * LANES : (j + 1) * LANES] = mean[j : j + 1, :]
        coef_ref[1:2, j * LANES : (j + 1) * LANES] = rstd[j : j + 1, :]
    coef_ref[2:3, :] = jnp.full((1, width), used, F32)
    coef_ref[3:4, :] = coef_ref[1:2, :] * norm_ref[0:1, :]
    bags = rows // SLOTS_BAG
    group = 8

    def fold(v):
        return (v[:group] + v[group : 2 * group]) + (v[2 * group : 3 * group] + v[3 * group :])

    def unfold(ref, j):
        total = ref[j, pl.ds(0, bags, stride=group), :]
        for i in range(1, group):
            total = total + ref[j, pl.ds(i, bags, stride=group), :]
        return total

    for j in range(tiles):
        cols = slice(j * LANES, (j + 1) * LANES)
        centre, scale, bias = coef_ref[0:1, cols], coef_ref[3:4, cols], norm_ref[1:2, cols]
        for b in range(bags):
            at = slice(b * SLOTS_BAG, (b + 1) * SLOTS_BAG)
            to = slice(b * group, (b + 1) * group)
            apart = pre_ref[at, cols] - centre
            y = scale * apart + bias
            capped = jnp.minimum(y, 20.0)
            e = jnp.exp(capped)
            top = e * (e + 2.0)
            below = top + 2.0
            inv = 1.0 / below
            gate = top * inv
            low_ref[at, :] = (y * gate).astype(BF)
            part = e * inv
            slope = gate + (4.0 * capped) * (part * (inv + part))
            slope_ref[at, cols] = slope
            slope = slope * live_ref[at, :]
            ones_ref[j, to, :] = fold(slope)
            twos_ref[j, to, :] = fold(slope * apart)
        act_ref[:, cols] = dot(pick_ref[...], low_ref[...])
        one_ref[:, cols] = unfold(ones_ref, j)
        two_ref[:, cols] = unfold(twos_ref, j) * coef_ref[1:2, cols]
    second = w_out_ref[...].astype(BF).astype(F32)
    bags = hdot(act_ref[...], second, 1, 1)
    pairs = bags.shape[0] // 2
    split = jnp.concatenate([hdot(pick(pairs, 0), bags), hdot(pick(pairs, 1), bags)], axis=0)
    bags_ref[...] = split
    eighth = pairs // 2
    packed = jnp.concatenate([split[i * eighth : (i + 1) * eighth] for i in range(4)], axis=1)
    for d in range(n):
        pay_ref[d * eighth : (d + 1) * eighth, :] = packed


def pick(pairs, which):
    r = lax.broadcasted_iota(jnp.int32, (pairs, 2 * pairs), 0)
    c = lax.broadcasted_iota(jnp.int32, (pairs, 2 * pairs), 1)
    return (c == 2 * r + which).astype(F32)


def spread(pairs, which):
    r = lax.broadcasted_iota(jnp.int32, (2 * pairs, pairs), 0)
    c = lax.broadcasted_iota(jnp.int32, (2 * pairs, pairs), 1)
    return (r == 2 * c + which).astype(F32)


def three(v):
    a = v.astype(BF)
    v = v - a.astype(F32)
    b = v.astype(BF)
    v = v - b.astype(F32)
    return a, b, v.astype(BF)


def loss_kernel(
    me_ref, all_ref, mask_ref, towers_ref, w_out_ref, act_ref, one_ref, two_ref,
    dact_ref, pay_ref, d_towers_ref, loss_ref, total_ref,
    score_ref, user_ref, item_ref, second_ref, row_ref, *, n,
):
    me = me_ref[0]
    embed = towers_ref.shape[1]
    total_rows = mask_ref.shape[0]
    eighth = all_ref.shape[0] // n

    def full(i):
        a = all_ref[:, 2 * i * embed : (2 * i + 1) * embed].reshape(n, eighth, embed)
        b = all_ref[:, (2 * i + 1) * embed : (2 * i + 2) * embed].reshape(n, eighth, embed)
        return jnp.stack([a, b], axis=1).reshape(total_rows, embed)

    bags_user, bags_item = full(0), full(1)
    user = hdot(bags_user, towers_ref[0]).astype(BF)
    item = hdot(bags_item, towers_ref[1]).astype(BF)
    root = math.sqrt(embed)
    score_ref[...] = dot(user, item, 1, 1) / root
    negatives = jnp.sum(mask_ref[...].astype(F32))
    count = negatives / total_rows
    step = 32

    def rows(i, carry):
        at = slice(i * step, (i + 1) * step)
        logits = score_ref[at, :]
        r = lax.broadcasted_iota(jnp.int32, logits.shape, 0) + i * step
        own = r == lax.broadcasted_iota(jnp.int32, logits.shape, 1)
        keep = own | (mask_ref[at, :].astype(F32) == 1.0)
        top = jnp.max(jnp.where(keep, logits, -jnp.inf), axis=1, keepdims=True)
        weights = jnp.where(keep, jnp.exp(logits - top), 0.0)
        total = jnp.sum(weights, axis=1, keepdims=True)
        hit = jnp.sum(jnp.where(own, logits, 0.0), axis=1, keepdims=True)
        score_ref[at, :] = (weights / total - own.astype(F32)) / count / root
        return carry + (top + jnp.log(total) - hit)

    ce = jnp.zeros((step, 1), F32)
    for i in range(total_rows // step):
        ce = rows(i, ce)
    loss_ref[0, 0] = jnp.sum(ce)
    total_ref[0, 0] = count
    parts = three(score_ref[...])
    d_user = sum(dot(p, item) for p in parts)
    d_item = sum(dot(user, p, 0, 0) for p in parts).T
    user_ref[...] = d_user
    item_ref[...] = d_item
    d_towers_ref[0] = hdot(bags_user, d_user, 0, 0)
    d_towers_ref[1] = hdot(bags_item, d_item, 0, 0)
    mine = pl.ds(pl.multiple_of(me * PAIR, PAIR), PAIR)
    back_user = hdot(user_ref[mine, :], towers_ref[0], 1, 1).astype(BF).astype(F32)
    back_item = hdot(item_ref[mine, :], towers_ref[1], 1, 1).astype(BF).astype(F32)
    d_emb = dot(spread(PAIR, 0), back_user) + dot(spread(PAIR, 1), back_item)
    d_act = dot(d_emb.astype(BF), w_out_ref[...].astype(BF))
    dact_ref[...] = d_act
    d_bias = jnp.sum(d_act * one_ref[...], axis=0, keepdims=True)
    d_gain = jnp.sum(d_act * two_ref[...], axis=0, keepdims=True)
    d_low = d_emb.T.astype(BF)
    second = sum(dot(d_low, p) for p in three(act_ref[...]))
    width = act_ref.shape[1]
    tiles = width // LANES
    for j in range(tiles):
        second_ref[pl.ds(j, embed, stride=tiles), :] = second[:, j * LANES : (j + 1) * LANES]
    for j in range(tiles):
        cols = slice(j * LANES, (j + 1) * LANES)
        row_ref[j : j + 1, :] = d_bias[:, cols]
        row_ref[tiles + j : tiles + j + 1, :] = d_gain[:, cols]
    sums = row_ref[...].astype(BF)
    chunk = embed * tiles // n
    for d in range(n):
        part = second_ref[d * chunk : (d + 1) * chunk, :]
        high = part.astype(BF)
        low = (part - high.astype(F32)).astype(BF)
        at = d * (2 * tiles + 2 * chunk)
        pay_ref[at : at + 2 * tiles, :] = sums
        pay_ref[at + 2 * tiles : at + 2 * tiles + 2 * chunk, :] = jnp.concatenate([high, low], axis=0)


def loss_spread(plan, bags, neg_mask, towers, w_out, act, one, two):
    embed = towers.shape[1]
    rows = neg_mask.shape[0]
    bags_user, bags_item = bags[:rows], bags[rows:]
    user = hdot(bags_user, towers[0]).astype(BF)
    item = hdot(bags_item, towers[1]).astype(BF)
    items = lax.all_gather(item, AXES, axis=0, tiled=True)
    root = math.sqrt(embed)
    logits = dot(user, items, 1, 1) / root
    at = lax.axis_index(AXES) * rows + lax.broadcasted_iota(jnp.int32, logits.shape, 0)
    own = lax.broadcasted_iota(jnp.int32, logits.shape, 1) == at
    keep = own | (neg_mask == 1)
    top = jnp.max(jnp.where(keep, logits, -jnp.inf), axis=1, keepdims=True)
    weights = jnp.where(keep, jnp.exp(logits - top), 0.0)
    total = jnp.sum(weights, axis=1, keepdims=True)
    ce = top + jnp.log(total) - jnp.sum(jnp.where(own, logits, 0.0), axis=1, keepdims=True)
    count = lax.psum(jnp.sum(neg_mask.astype(F32)), AXES) / items.shape[0]
    scores = (weights / total - own.astype(F32)) / count / root
    d_user = hdot(scores, items.astype(F32))
    d_item = lax.psum_scatter(
        hdot(scores, user.astype(F32), 0, 0), AXES, scatter_dimension=0, tiled=True
    )
    d_towers = jnp.stack([hdot(bags_user, d_user, 0, 0), hdot(bags_item, d_item, 0, 0)])
    back = jnp.stack([hdot(d_user, towers[0], 1, 1), hdot(d_item, towers[1], 1, 1)], axis=1)
    d_emb = back.reshape(2 * rows, embed).astype(BF)
    d_act = dot(d_emb, w_out.astype(BF))
    d_second = hdot(d_emb.astype(F32), act, 0, 0)
    sums = jnp.stack([jnp.sum(d_act * one, axis=0), jnp.sum(d_act * two, axis=0)])
    sums, d_second, d_towers, loss = lax.psum((sums, d_second, d_towers, jnp.sum(ce)), AXES)
    return d_act, sums.reshape(-1, LANES), d_second, d_towers, loss, count


def grad_kernel(
    me_ref, owners_ref, sums_ref, coef_ref, norm_ref, dact_ref, slope_ref, pre_ref, live_ref, xt_ref,
    keep_ref, send_ref, chunk_ref, d_norm_ref, d_pre_ref, g_ref, row_ref,
    *, parts, order, local,
):
    rows, width = pre_ref.shape
    tiles = width // LANES
    held = sums_ref.shape[0] // parts
    total = sums_ref[0:held, :].astype(F32)
    for d in range(1, parts):
        total = total + sums_ref[d * held : (d + 1) * held, :].astype(F32)
    d_norm_ref[0:tiles, :] = total[tiles : 2 * tiles]
    d_norm_ref[tiles : 2 * tiles, :] = total[:tiles]
    if held > 2 * tiles:
        chunk = chunk_ref.shape[0]
        chunk_ref[...] = total[2 * tiles : 2 * tiles + chunk] + total[2 * tiles + chunk :]
    else:
        chunk_ref[...] = jnp.zeros(chunk_ref.shape, F32)
    for j in range(tiles):
        cols = slice(j * LANES, (j + 1) * LANES)
        row_ref[0:1, cols] = total[j : j + 1]
        row_ref[1:2, cols] = total[tiles + j : tiles + j + 1]
    scale = norm_ref[0:1, :] * coef_ref[1:2, :]
    flat = scale * row_ref[0:1, :] / coef_ref[2:3, :]
    tilt = scale * row_ref[1:2, :] / coef_ref[2:3, :] * coef_ref[1:2, :]
    row_ref[2:3, :] = scale
    row_ref[3:4, :] = flat
    row_ref[4:5, :] = tilt
    block = 2 * LANES
    for j in range(width // block):
        for i in range(2):
            cols = slice(j * block + i * LANES, j * block + (i + 1) * LANES)
            for b in range(rows // SLOTS_BAG):
                at = slice(b * SLOTS_BAG, (b + 1) * SLOTS_BAG)
                lead = dact_ref[b : b + 1, cols] * row_ref[2:3, cols]
                apart = (pre_ref[at, cols] - coef_ref[0:1, cols]) * row_ref[4:5, cols]
                d_pre = slope_ref[at, cols] * lead - row_ref[3:4, cols] - apart
                d_pre_ref[at, cols] = (live_ref[at, :] * d_pre).astype(BF)
        cols = slice(j * block, (j + 1) * block)
        g_ref[:, cols] = dot(xt_ref[...], d_pre_ref[:, cols])
    bsize = LANES // 2
    half = bsize // 2
    side = width // bsize
    lane_half = lax.broadcasted_iota(jnp.int32, (half, LANES), 1) // bsize
    me = me_ref[0]
    for out, masks in ((send_ref, order[1]), (keep_ref, order[0])):
        for i, m in enumerate(masks):
            for b in range(local):
                r, c, odd = place(owners_ref[(me ^ m) * local + b], side)
                at = pl.ds(pl.multiple_of(r * bsize, bsize), half)
                low = pl.ds(pl.multiple_of(r * bsize + half, half), half)
                cols = pl.ds(pl.multiple_of(c * LANES, LANES), LANES)
                to = (i * local + b) * half
                out[to : to + half, :] = jnp.where(
                    lane_half == odd,
                    g_ref[at, cols].astype(out.dtype),
                    swap_halves(g_ref[low, cols].astype(out.dtype)),
                )


def scatter_sum(plan, keep, send, rows):
    rest = len(plan.rest)
    shape = (2, 2, rest, rows, LANES)
    got = plan.swap(send, plan.core)
    mine = (keep + got.astype(F32)).reshape(shape)
    cut = rows // 2
    one, two = mine[..., :cut, :], mine[..., cut:, :]
    got_one = plan.swap(one[1].astype(BF), plan.x)
    got_two = plan.swap(two[:, 1].astype(BF), plan.y)
    one = one[0] + got_one.astype(F32)
    two = two[:, 0] + got_two.astype(F32)
    got_one = plan.swap(one[1].astype(BF), plan.y)
    got_two = plan.swap(two[1].astype(BF), plan.x)
    one = one[0] + got_one.astype(F32)
    two = two[0] + got_two.astype(F32)
    if rest <= 4:
        both = jnp.concatenate([one[1:], two[1:]], axis=1).astype(BF)
        return one, two, [plan.swap(both[k], m) for k, m in enumerate(plan.rest[1:])]
    both = jnp.concatenate([one, two], axis=1)
    for b in reversed(plan.bits):
        both = both.reshape(2, -1, rows, LANES)
        both = both[0] + plan.swap(both[1].astype(BF), b).astype(F32)
    return both[:, :cut], both[:, cut:], []


def norm_kernel(*refs, n):
    one_ref, two_ref, chunk_ref = refs[:3]
    got = refs[3:-2]
    g_ref, pay_ref = refs[-2:]
    total = jnp.concatenate([one_ref[0], two_ref[0]], axis=0)
    for g in got:
        total = total + g[...].astype(F32)
    g_ref[...] = total
    chunk = chunk_ref[...]
    squares = jnp.sum(total * total, keepdims=True) + jnp.sum(chunk * chunk, keepdims=True)
    high = chunk.astype(BF)
    low = chunk - high.astype(F32)
    for i, v in enumerate(three(squares)):
        low = jnp.where(spare(chunk.shape, i), v.astype(F32), low)
    packed = jnp.concatenate([high, low.astype(BF)], axis=0)
    rows = packed.shape[0]
    for d in range(n):
        pay_ref[d * rows : (d + 1) * rows, :] = packed


def spare(shape, i):
    row = lax.broadcasted_iota(jnp.int32, shape, 0)
    lane = lax.broadcasted_iota(jnp.int32, shape, 1)
    return (row == shape[0] - 1) & (lane == LANES - 3 + i)


def adamw(grad, weight, first, second):
    first = BETA_ONE * first + (1 - BETA_ONE) * grad
    second = BETA_TWO * second + (1 - BETA_TWO) * grad * grad
    step = (
        first / (1 - BETA_ONE**STEP) / (jnp.sqrt(second / (1 - BETA_TWO**STEP)) + EPSILON)
    )
    return weight - RATE * (step + DECAY * weight), first, second


def eliminate(gram_ref, power_ref):
    count, size, lanes = gram_ref.shape
    group = 8
    lane = lax.broadcasted_iota(jnp.int32, (count * group, lanes), 1)
    left = lax.broadcasted_iota(jnp.int32, (1, lanes), 1) < size
    for at in range(0, size, group):
        rest = at + group
        gram, power = gram_ref[:, at:rest, :], power_ref[:, at:rest, :]
        flat = gram.reshape(count * group, lanes)
        cols = [
            jnp.take_along_axis(flat, (lane // size) * size + at + i, axis=1).reshape(gram.shape)
            for i in range(group)
        ]
        for i in range(group):
            inv = lax.rsqrt(cols[i][:, i : i + 1, :])
            row, power_row = gram[:, i : i + 1, :] * inv, power[:, i : i + 1, :] * inv
            gram_ref[:, at + i : at + i + 1, :] = row
            power_ref[:, at + i : at + i + 1, :] = power_row
            f = cols[i] * inv
            gram, power = gram - f * row, power - f * power_row
            for j in range(i + 1, group):
                cols[j] = cols[j] - f * f[:, j : j + 1, :]
        if rest == size:
            return
        a, b, c = (v.astype(F32) for v in three(gram_ref[:, at:rest, :]))
        d, e, f = (v.astype(F32) for v in three(power_ref[:, at:rest, :]))
        lhs = jnp.concatenate([a, a, b, b, a, c], axis=1).astype(BF)
        rhs = jnp.concatenate([a, b, a, b, c, a], axis=1)
        rhs = jnp.concatenate([rhs, jnp.concatenate([d, e, d, e, f, d], axis=1)], axis=2).astype(BF)
        turned = [lhs[m].T for m in range(count)]
        for m in range(count):
            one = dot(turned[m][rest:size], rhs[m])
            two = dot(turned[m][size + rest :], rhs[m])
            gram_ref[m, rest:, :] = gram_ref[m, rest:, :] - jnp.where(left, one[:, :lanes], two[:, :lanes])
            power_ref[m, rest:, :] = power_ref[m, rest:, :] - jnp.where(left, one[:, lanes:], two[:, lanes:])


def pair(a, b):
    return jnp.concatenate([a, b], axis=1)


def prepare_kernel(
    w_hbm, left_hbm, right_hbm, bl_hbm, br_hbm, first_hbm, second_hbm, ema_hbm,
    moments_ref, stats_ref, bases_ref, weights_ref, turned_ref, powers_ref,
    w_ref, left_ref, right_ref, bl_ref, br_ref, first_ref, second_ref, ema_ref, sems,
):
    fetch(
        (w_hbm, left_hbm, right_hbm, bl_hbm, br_hbm, first_hbm, second_hbm, ema_hbm),
        (w_ref, left_ref, right_ref, bl_ref, br_ref, first_ref, second_ref, ema_ref),
        sems,
    )
    each = range(w_ref.shape[0])
    for b in each:
        moments_ref[b] = pair(first_ref[b], second_ref[b])
        stats_ref[b] = pair(left_ref[b], right_ref[b])
        bases_ref[b] = pair(bl_ref[b], br_ref[b])
        weights_ref[b] = pair(w_ref[b], ema_ref[b])
    half = [hdot(bl_ref[b], first_ref[b], 0, 0) for b in each]
    for b in each:
        turned_ref[b] = hdot(half[b], br_ref[b])
    lefts = [hdot(bl_ref[b], left_ref[b], 0, 0) for b in each]
    rights = [hdot(br_ref[b], right_ref[b], 0, 0) for b in each]
    for b in each:
        powers_ref[b] = pair(lefts[b], rights[b])


def turn_kernel(
    me_ref, owners_ref, g_ref, bases_ref,
    wo_hbm, mo_hbm, vo_hbm, eo_hbm, wt_hbm, mt_hbm, vt_hbm, wn_hbm, mn_hbm, vn_hbm,
    grad_ref, squares_ref, powers_ref, scale_ref,
    wide_ref, towers_ref, norms_ref, sems,
):
    local, bsize = bases_ref.shape[0], bases_ref.shape[1]
    sources = (wo_hbm, mo_hbm, vo_hbm, eo_hbm, wt_hbm, mt_hbm, vt_hbm, wn_hbm, mn_hbm, vn_hbm)
    targets = [wide_ref.at[i] for i in range(4)]
    targets += [towers_ref.at[i] for i in range(3)] + [norms_ref.at[i] for i in range(3)]
    copies = [pltpu.make_async_copy(a, b, sems.at[i]) for i, (a, b) in enumerate(zip(sources, targets))]
    for c in copies:
        c.start()
    largest = jnp.max(jnp.abs(g_ref[...]), keepdims=True)
    largest = jnp.where(largest > 0.0, largest, 1.0)
    scale_ref[...] = jnp.broadcast_to(largest, scale_ref.shape)
    half = bsize // 2
    each = range(local)
    grads = []
    for b in each:
        odd = owners_ref[me_ref[0] * local + b] % 2
        tile = g_ref[b * half : (b + 1) * half, :]
        tile = jnp.where(odd == 1, swap_halves(tile), tile)
        grads.append(jnp.concatenate([tile[:, :bsize], tile[:, bsize:]], axis=0) / largest)
    bl = [bases_ref[b, :, :bsize] for b in each]
    br = [bases_ref[b, :, bsize:] for b in each]
    by_left = [hdot(bl[b], grads[b], 0, 0) for b in each]
    by_right = [hdot(grads[b], br[b]) for b in each]
    outer = [hdot(grads[b], grads[b], 1, 1) for b in each]
    inner = [hdot(grads[b], grads[b], 0, 0) for b in each]
    for b in each:
        squares_ref[b] = pair(outer[b], inner[b])
    for b in each:
        grad_ref[b] = pair(grads[b], hdot(by_left[b], br[b]))
    lefts = [hdot(by_left[b], grads[b], 1, 1) for b in each]
    rights = [hdot(by_right[b], grads[b], 0, 0) for b in each]
    for b in each:
        powers_ref[b] = pair(lefts[b], rights[b])
    for c in copies:
        c.wait()


def step_kernel(
    got_ref, d_norm_ref, d_towers_ref,
    grad_ref, squares_ref, powers_ref, scale_ref,
    old_ref, towers_ref, norms_ref,
    moments_ref, stats_ref, bases_ref, weights_ref, turned_first_ref, powers_old_ref,
    *refs, n,
):
    (
        w_out, low_out, left_out, right_out, bl_out, br_out, first_out, second_out, ema_out,
        wo_out, mo_out, vo_out, eo_out, wt_out, mt_out, vt_out, wn_out, mn_out, vn_out, gn_out,
        gram_ref, power_ref, wide_ref, dn_ref, flat_ref,
    ) = refs
    local, bsize = bases_ref.shape[0], bases_ref.shape[1]
    embed, width = old_ref.shape[1:]
    tiles = width // LANES
    held = got_ref.shape[0] // n
    if n > 1:
        chunk = held // 2
        used = functools.reduce(jnp.logical_or, [spare((chunk, LANES), i) for i in range(3)])
        squares = jnp.zeros((chunk, LANES), F32)
        for d in range(n):
            part = got_ref[d * held : (d + 1) * held, :].astype(F32)
            squares = squares + jnp.where(used, part[chunk:], 0.0)
            flat_ref[d * chunk : (d + 1) * chunk, :] = part[:chunk] + jnp.where(used, 0.0, part[chunk:])
        squares = jnp.sum(squares)
        for j in range(tiles):
            wide_ref[:, j * LANES : (j + 1) * LANES] = flat_ref[pl.ds(j, embed, stride=tiles), :]
    else:
        squares = jnp.max(got_ref[0:1, :LANES])
        wide_ref[...] = got_ref[8 : 8 + embed, :]
    squares = squares + jnp.sum(d_towers_ref[...] * d_towers_ref[...])
    squares = squares + jnp.sum(d_norm_ref[...] * d_norm_ref[...])
    norm = jnp.sqrt(jnp.full((1, LANES), squares, F32))
    gn_out[0, 0] = jnp.max(norm)
    factor = (CLIP / jnp.maximum(norm, CLIP))[:, :1]
    each = range(local)
    lead = factor * scale_ref[0:1, 0:1]
    twice = (1 - BETA_TWO) * lead * lead
    lefts, rights = [], []
    for b in each:
        powers = BETA_TWO * powers_old_ref[b] + twice * powers_ref[b]
        power_ref[b] = powers
        lefts.append(powers[:, :bsize])
        rights.append(powers[:, bsize:])
    for b in each:
        gram_ref[b] = pair(hdot(lefts[b], lefts[b], 1, 1), hdot(rights[b], rights[b], 1, 1))
    ratios = []
    for b in each:
        stats = BETA_TWO * stats_ref[b] + twice * squares_ref[b]
        left_out[b], right_out[b] = stats[:, :bsize], stats[:, bsize:]
        first_out[b] = BETA_ONE * moments_ref[b, :, :bsize] + (1 - BETA_ONE) * lead * grad_ref[b, :, :bsize]
        turned = grad_ref[b, :, bsize:]
        second = BETA_TWO * moments_ref[b, :, bsize:] + twice * turned * turned
        second_out[b] = second
        moved = BETA_ONE * turned_first_ref[b] + (1 - BETA_ONE) * lead * turned
        moved = moved / (1 - BETA_ONE**STEP)
        ratios.append(moved / (jnp.sqrt(second / (1 - BETA_TWO**STEP)) + EPSILON))
    half = [hdot(bases_ref[b, :, :bsize], ratios[b]) for b in each]
    updates = [hdot(half[b], bases_ref[b, :, bsize:], 1, 1) for b in each]
    for b in each:
        old = weights_ref[b, :, :bsize]
        new = old - RATE * (updates[b] + DECAY * old)
        w_out[b] = new
        low_out[b] = new.astype(BF)
        ema_out[b] = AVG_KEEP * weights_ref[b, :, bsize:] + AVG_TAKE * new
    new, m, v = adamw(wide_ref[...] * factor, old_ref[0], old_ref[1], old_ref[2])
    wo_out[...], mo_out[...], vo_out[...] = new, m, v
    eo_out[...] = AVG_KEEP * old_ref[3] + AVG_TAKE * new
    for t in range(2):
        wt_out[t], mt_out[t], vt_out[t] = adamw(
            d_towers_ref[t] * factor, towers_ref[0, t], towers_ref[1, t], towers_ref[2, t]
        )
        for j in range(tiles):
            dn_ref[t : t + 1, j * LANES : (j + 1) * LANES] = d_norm_ref[
                t * tiles + j : t * tiles + j + 1, :
            ]
    wn_out[...], mn_out[...], vn_out[...] = adamw(
        dn_ref[...] * factor, norms_ref[0], norms_ref[1], norms_ref[2]
    )
    eliminate(gram_ref, power_ref)
    for b in each:
        turned = power_ref[b].T
        bl_out[b], br_out[b] = turned[:bsize], turned[bsize:]


def exchange(payload):
    return lax.all_to_all(payload, AXES, 0, 0, tiled=True)


def on_device(
    plan,
    codes, field_offsets, seg_mask, neg_mask, owners,
    w_hidden, stat_left, stat_right, basis_left, basis_right, mom1_hidden, mom2_hidden, ema_hidden,
    w_out, mom1_out, mom2_out, ema_out,
    w_towers, mom1_towers, mom2_towers,
    w_norm, mom1_norm, mom2_norm,
):
    n = plan.n
    local, bsize = w_hidden.shape[0], w_hidden.shape[1]
    width, embed = w_out.shape
    slots = codes.shape[0]
    rows, total_rows = neg_mask.shape
    tiles = width // LANES
    half = bsize // 2
    bags = slots // SLOTS_BAG
    masked = total_rows <= 1024 and n <= embed
    me = lax.axis_index(AXES).astype(jnp.int32)[None]

    chunks = total_rows // LANES if masked else 0
    size = local * half + chunks * PAIR + PAIR
    (payload,) = call(
        functools.partial(pack_kernel, masked=masked),
        [((size, LANES), BF)],
        [me, in_hbm(owners), w_hidden, neg_mask, seg_mask.reshape(-1, LANES)],
        smem=2,
        hbm=3,
        scratch=[
            pltpu.VMEM(w_hidden.shape, F32),
            pltpu.VMEM(neg_mask.shape, jnp.int32),
            pltpu.VMEM((slots // LANES, LANES), jnp.int32),
            pltpu.SemaphoreType.DMA((3,)),
        ],
        name="pack",
    )
    cut = max(half, size // 2 // half * half)
    cut = min(cut, local * half)
    blocks = (local, bsize, bsize)
    twin = (local, bsize, 2 * bsize)
    state = [
        w_hidden, stat_left, stat_right, basis_left, basis_right, mom1_hidden, mom2_hidden, ema_hidden
    ]
    prepared = call(
        prepare_kernel,
        [(twin, F32)] * 4 + [(blocks, F32), (twin, F32)],
        state,
        hbm=len(state),
        scratch=[pltpu.VMEM(blocks, F32)] * len(state) + [pltpu.SemaphoreType.DMA((len(state),))],
        limit=12,
        name="prepare",
        cost=10_000_000,
    )
    turned_out, turned_mom1, turned_mom2, turned_ema = (
        a.T for a in (w_out, mom1_out, mom2_out, ema_out)
    )
    early = hash_inputs(codes, field_offsets)
    live = jnp.broadcast_to(seg_mask.astype(F32)[:, None], (slots, LANES))
    slot_bag = lax.broadcasted_iota(jnp.int32, (bags, slots), 1) // SLOTS_BAG
    in_bag = slot_bag == lax.broadcasted_iota(jnp.int32, (bags, slots), 0)
    chosen = jnp.where(in_bag, seg_mask.astype(F32)[None], 0.0).astype(BF)
    late = (*prepared, live, chosen)
    zero = (me[0] >> 16).astype(BF)
    pieces, (x, x_turned), (*prepared, live, chosen) = gather_pieces(
        plan, payload, cut, zero, early, late
    )
    mask_shape = (total_rows, total_rows) if masked else (PAIR, LANES)
    holds = [([m | base for m in plan.rest], row) for _, base, row in pieces]
    arrays = [a for a, _, _ in pieces]
    done = [0, 1, 2, 5, 6, 7]
    (planes,) = call(
        functools.partial(assemble_kernel, holds=[holds[i] for i in done], local=local),
        [((2, width, width), BF)],
        [me, owners] + [arrays[i] for i in done],
        smem=2,
        limit=8,
        name="assemble",
        cost=10_000_000,
    )
    pre, kept, sent, counts, mask, _ = call(
        functools.partial(
            pre_kernel, holds=holds, done=done, local=local, masked=masked, core=plan.core
        ),
        [
            ((slots, width), F32),
            ((tiles, LANES), F32),
            ((tiles, LANES), F32),
            ((n, LANES), F32),
            (mask_shape, BF),
            ((2, width, width), BF),
        ],
        [me, owners, planes] + arrays + [x, live],
        smem=2,
        scratch=[pltpu.VMEM((2 * tiles, LANES), F32)],
        aliases={2: 5},
        limit=16,
        name="pre",
    )
    (stats,) = call(
        functools.partial(merge_kernel, core=plan.core),
        [((n * tiles, LANES), F32)],
        [me, counts, kept, plan.swap(sent, plan.core)],
        smem=1,
        limit=4,
        name="merge",
    )
    stats = exchange(stats)
    slope, act, one, two, coef, bag_sums, pay = call(
        functools.partial(act_kernel, core=plan.core),
        [
            ((slots, width), F32),
            ((bags, width), F32),
            ((bags, width), F32),
            ((bags, width), F32),
            ((8, width), F32),
            ((bags, embed), F32),
            ((n * 8, LANES), F32),
        ],
        [stats, counts, w_norm, pre, live, chosen, turned_out],
        scratch=[
            pltpu.VMEM((slots, LANES), BF),
            pltpu.VMEM((tiles, bags * 8, LANES), F32),
            pltpu.VMEM((tiles, bags * 8, LANES), F32),
        ],
        limit=12,
        name="act",
    )
    if masked:
        chunk = embed * tiles // n
        everyone = exchange(pay)
        d_act, pay, d_towers, loss_sum, count = call(
            functools.partial(loss_kernel, n=n),
            [
                ((bags, width), F32),
                ((n * (2 * tiles + 2 * chunk), LANES), BF),
                ((2, embed, embed), F32),
                ((1, 1), F32),
                ((1, 1), F32),
            ],
            [me, everyone, mask, w_towers, turned_out, act, one, two],
            smem=1,
            smem_outs=2,
            scratch=[
                pltpu.VMEM((total_rows, total_rows), F32),
                pltpu.VMEM((total_rows, embed), F32),
                pltpu.VMEM((total_rows, embed), F32),
                pltpu.VMEM((embed * tiles, LANES), F32),
                pltpu.VMEM((2 * tiles, LANES), F32),
            ],
            name="loss",
        )
        sums, parts = exchange(pay), n
        loss_sum, count = loss_sum[0, 0], count[0, 0]
    else:
        d_act, sums, d_second, d_towers, loss_sum, count = loss_spread(
            plan, bag_sums, neg_mask, w_towers, turned_out, act, one, two
        )
        parts = 1
        chunk = 8
    groups = [m for m in (0, plan.y, plan.x, plan.x | plan.y)]
    keep_order = [g | r for g in groups for r in plan.rest]
    order = (keep_order, [m | plan.core for m in keep_order])
    kept, sent, second_chunk, d_norm = call(
        functools.partial(grad_kernel, parts=parts, order=order, local=local),
        [
            ((n // 2 * local * half, LANES), F32),
            ((n // 2 * local * half, LANES), BF),
            ((chunk, LANES), F32),
            ((2 * tiles, LANES), F32),
        ],
        [me, owners, sums, coef, w_norm, d_act, slope, pre, live, x_turned],
        smem=2,
        scratch=[
            pltpu.VMEM((slots, width), BF),
            pltpu.VMEM((width, width), F32),
            pltpu.VMEM((8, width), F32),
        ],
        limit=20,
        name="grad",
    )
    one_sum, two_sum, others = scatter_sum(plan, kept, sent, local * half)
    copies = n if masked else 1
    grad, pay = call(
        functools.partial(norm_kernel, n=copies),
        [((local * half, LANES), F32), ((copies * 2 * chunk, LANES), BF)],
        [one_sum, two_sum, second_chunk, *others],
        name="norm",
    )
    if masked:
        got = exchange(pay)
    else:
        squares = lax.psum(jnp.sum(grad * grad), AXES) + jnp.sum(d_second * d_second)
        got = jnp.concatenate([jnp.full((8, width), squares, F32), d_second], axis=0)
    moments, stats, bases, weights, turned_first, powers_old = prepared
    plain = [
        turned_out, turned_mom1, turned_mom2, turned_ema,
        w_towers, mom1_towers, mom2_towers,
        w_norm, mom1_norm, mom2_norm,
    ]
    turned = call(
        turn_kernel,
        [(twin, F32)] * 3
        + [((8, LANES), F32), ((4, embed, width), F32), ((3, 2, embed, embed), F32), ((3, 2, width), F32)],
        [me, owners, grad, bases, *plain],
        smem=2,
        hbm=len(plain),
        scratch=[pltpu.SemaphoreType.DMA((len(plain),))],
        name="turn",
        cost=10_000_000,
    )
    outs = [(blocks, F32), (blocks, BF)] + [(blocks, F32)] * 7
    outs += [((embed, width), F32)] * 4 + [((2, embed, embed), F32)] * 3 + [((2, width), F32)] * 3
    new = call(
        functools.partial(step_kernel, n=n if masked else 1),
        outs + [((1, 1), F32)],
        [
            got, d_norm, d_towers, *turned,
            moments, stats, bases, weights, turned_first, powers_old,
        ],
        smem_outs=1,
        scratch=[
            pltpu.VMEM(twin, F32),
            pltpu.VMEM(twin, F32),
            pltpu.VMEM((embed, width), F32),
            pltpu.VMEM((2, width), F32),
            pltpu.VMEM((embed * tiles, LANES), F32),
        ],
        name="step",
    )
    return (loss_sum, count, new[-1][0, 0], *new[:9], *(a.T for a in new[9:13]), *new[13:-1])


def solution(mesh):
    split = P(("gx", "gy"))
    plan = Plan(mesh.shape["gx"], mesh.shape["gy"])
    return jax.shard_map(
        functools.partial(on_device, plan),
        mesh=mesh,
        in_specs=(split, P(), split, split, P()) + (split,) * 8 + (P(),) * 10,
        out_specs=(P(),) * 3 + (split,) * 9 + (P(),) * 10,
        check_vma=False,
    )
```

```python
import functools
import math

import jax
import jax.numpy as jnp
from jax import lax
from jax.experimental import pallas as pl
from jax.experimental.pallas import tpu as pltpu
from jax.sharding import PartitionSpec as P

FIELDS = 4
BAG = 8
HASH_RANGE = 4096
STEP = 10
BETA_ONE = 0.9
BETA_TWO = 0.95
EPSILON = 1e-08
RATE = 0.03
DECAY = 0.01
CLIP = 0.01
AVG_KEEP = 0.8
AVG_TAKE = 0.2

F32 = jnp.float32
BF = jnp.bfloat16
HIGH = lax.Precision.HIGHEST
AXES = ("gx", "gy")
LANES = 128
SLOTS_BAG = FIELDS * BAG
PAIR = 16
MIB = 1 << 20


def dot(a, b, ca=1, cb=0, precision=None):
    return lax.dot_general(
        a, b, (((ca,), (cb,)), ((), ())), precision=precision, preferred_element_type=F32
    )


hdot = functools.partial(dot, precision=HIGH)


def spec(space=pltpu.VMEM):
    return pl.BlockSpec(memory_space=space)


def in_hbm(a):
    return pltpu.with_memory_space_constraint(a, pltpu.HBM)


def call(kernel, outs, args, smem=0, hbm=0, smem_outs=0, aliases=None, scratch=(), limit=16, name=None, cost=None):
    args = list(args)
    specs = [spec(pltpu.SMEM)] * smem + [spec()] * (len(args) - smem - hbm) + [spec(pltpu.HBM)] * hbm
    if hbm:
        args[-hbm:] = [in_hbm(a) for a in args[-hbm:]]
    spaces = [pltpu.VMEM] * (len(outs) - smem_outs) + [pltpu.SMEM] * smem_outs
    estimate = None
    if cost:
        estimate = pl.CostEstimate(flops=cost, bytes_accessed=cost // 100, transcendentals=0)
    return pl.pallas_call(
        kernel,
        out_shape=[jax.ShapeDtypeStruct(s, t) for s, t in outs],
        in_specs=specs,
        out_specs=[spec(space) for space in spaces],
        scratch_shapes=list(scratch),
        compiler_params=pltpu.CompilerParams(vmem_limit_bytes=limit * MIB),
        cost_estimate=estimate,
        input_output_aliases=aliases or {},
        name=name,
    )(*args)


def fetch(sources, targets, sems):
    copies = [pltpu.make_async_copy(a, b, sems.at[i]) for i, (a, b) in enumerate(zip(sources, targets))]
    for c in copies:
        c.start()
    for c in copies:
        c.wait()


def swap_halves(v):
    half = v.shape[1] // 2
    return jnp.concatenate([v[:, half:], v[:, :half]], axis=1)


def place(q, side):
    shift = side.bit_length() - 1
    return q >> shift, (q & (side - 1)) >> 1, q & 1


class Plan:
    def __init__(self, gx, gy):
        self.gx, self.gy, self.n = gx, gy, gx * gy
        self.core = gy
        self.x = 2 * gy
        self.y = 1
        bits = []
        b = 2
        while b < gy:
            bits.append(b)
            b *= 2
        b = 4
        while b < gx:
            bits.append(b * gy)
            b *= 2
        self.bits = bits
        rest = [0]
        for b in bits:
            rest = rest + [m | b for m in rest]
        self.rest = rest

    def swap(self, a, mask):
        mx, my = mask // self.gy, mask % self.gy
        if my == 0:
            return lax.ppermute(a, "gx", [(i, i ^ mx) for i in range(self.gx)])
        if mx == 0:
            return lax.ppermute(a, "gy", [(i, i ^ my) for i in range(self.gy)])
        return lax.ppermute(a, AXES, [(i, i ^ mask) for i in range(self.n)])


def pack_kernel(
    me_ref, owners_ref, w_hbm, neg_hbm, seg_hbm, out_ref, w_ref, neg_ref, seg_ref, sems, *, masked
):
    fetch((w_hbm, neg_hbm, seg_hbm), (w_ref, neg_ref, seg_ref), sems)
    local, bsize = w_ref.shape[0], w_ref.shape[1]
    half = bsize // 2
    for b in range(local):
        odd = owners_ref[me_ref[0] * local + b] % 2
        top, low = w_ref[b, :half, :], w_ref[b, half:, :]
        left = jnp.where(odd == 1, low, top)
        right = jnp.where(odd == 1, top, low)
        out_ref[b * half : (b + 1) * half, :] = jnp.concatenate([left, right], axis=1).astype(BF)
    at = local * half
    if masked:
        for c in range(neg_ref.shape[1] // LANES):
            part = neg_ref[:, c * LANES : (c + 1) * LANES].astype(F32)
            out_ref[at : at + PAIR, :] = part.astype(BF)
            at += PAIR
    used = jnp.sum(seg_ref[...].astype(F32), axis=0, keepdims=True)
    out_ref[at : at + PAIR, :] = jnp.broadcast_to(used, (PAIR, LANES)).astype(BF)


def gather_pieces(plan, payload, cut, zero, early, late, place_blocks):
    stack = payload[None]
    if len(plan.rest) <= 4:
        stack = jnp.concatenate([stack] + [plan.swap(stack, m) for m in plan.rest[1:]], axis=0)
    else:
        for b in plan.bits:
            stack = jnp.concatenate([stack, plan.swap(stack, b)], axis=0)
    stack, early = lax.optimization_barrier((stack, early))
    by_x = plan.swap(stack, plan.x)
    by_y = plan.swap(stack, plan.y)
    by_x, by_y, late = lax.optimization_barrier((by_x, by_y, late))
    first = plan.swap(by_x[:, :cut] + zero, plan.y)
    second = plan.swap(by_y[:, cut:] + zero, plan.x)
    ready = [(stack, 0, 0), (by_x, plan.x, 0), (by_y, plan.y, 0)]
    ready += swapped(plan, ready)
    planes = place_blocks(ready)
    first, second, planes = lax.optimization_barrier((first, second, planes))
    last = [(first, plan.x | plan.y, 0), (second, plan.x | plan.y, cut)]
    return ready + last + swapped(plan, last), len(ready), planes, early, late


def swapped(plan, pieces):
    return [(plan.swap(a, plan.core), m | plan.core, row) for a, m, row in pieces]


def hash_kernel(codes_hbm, offsets_hbm, x_ref, xt_ref, codes_ref, offsets_ref, sems):
    rows, width = codes_ref.shape
    groups = 2 * FIELDS
    step = 128
    head = pltpu.make_async_copy(offsets_hbm, offsets_ref, sems.at[0])
    head.start()
    parts = []
    for i in range(rows // step):
        at = pl.ds(i * step, step)
        parts.append(pltpu.make_async_copy(codes_hbm.at[at], codes_ref.at[at], sems.at[1 + i]))
        parts[i].start()
    head.wait()
    for i, part in enumerate(parts):
        part.wait()
        at = slice(i * step, (i + 1) * step)
        salted = codes_ref[at, :].reshape(-1, groups, BAG, width) + offsets_ref[...][None, :, None, :]
        salted = (salted & (HASH_RANGE - 1)).reshape(step, width)
        x = (salted.astype(F32) * (2.0 / (HASH_RANGE - 1)) - 1.0).astype(BF)
        x_ref[at, :] = x
        quarter = LANES // 4
        turned = x.T.reshape(-1, 2, quarter, step)
        for h in range(2):
            xt_ref[h * width // 2 : (h + 1) * width // 2, at] = turned[:, h].reshape(-1, step)


def hash_inputs(codes, offsets):
    rows, width = codes.shape
    return call(
        hash_kernel,
        [((rows, width), BF), ((width, rows), BF)],
        [codes, offsets],
        hbm=2,
        scratch=[
            pltpu.VMEM(codes.shape, jnp.int32),
            pltpu.VMEM(offsets.shape, jnp.int32),
            pltpu.SemaphoreType.DMA((1 + rows // 128,)),
        ],
        limit=12,
        name="hash",
        cost=20_000_000,
    )


def assemble(w_ref, me, owners_ref, piece_refs, holds, local):
    width = w_ref.shape[1]
    bsize = LANES // 2
    half = bsize // 2
    side = width // bsize
    for piece, (masks, row0) in zip(piece_refs, holds):
        for k, m in enumerate(masks):
            for b in range(local):
                at = b * half - row0
                if at < 0 or at + half > piece.shape[1]:
                    continue
                r, c, odd = place(owners_ref[(me ^ m) * local + b], side)
                tile = piece[k, at : at + half, :]
                rows = pl.multiple_of(r * bsize, bsize)
                low = pl.multiple_of(r * bsize + half, half)
                cols = pl.ds(pl.multiple_of(c * LANES, LANES), LANES)
                w_ref[odd, pl.ds(rows, half), cols] = tile
                w_ref[odd, pl.ds(low, half), cols] = swap_halves(tile)


def assemble_kernel(me_ref, owners_ref, *refs, holds, local):
    assemble(refs[-1], me_ref[0], owners_ref, refs[:-1], holds, local)


def pre_kernel(*refs, holds, done, local, masked, core):
    me_ref, owners_ref = refs[:2]
    pieces = len(holds)
    piece_refs = refs[3 : 3 + pieces]
    x_ref, live_ref = refs[3 + pieces : 5 + pieces]
    pre_ref, keep_ref, send_ref, count_ref, mask_ref, w_ref, row_ref = refs[5 + pieces :]
    width = x_ref.shape[1]
    bsize = LANES // 2
    half = bsize // 2
    tiles = width // LANES
    me = me_ref[0]
    chunks = mask_ref.shape[1] // LANES if masked else 0
    assemble(w_ref, me, owners_ref, piece_refs[done:], holds[done:], local)
    for piece, (masks, row0) in zip(piece_refs, holds):
        held = piece.shape[1]
        for k, m in enumerate(masks):
            d = me ^ m
            for c in range(chunks):
                at = local * half + c * PAIR - row0
                if at < 0 or at + PAIR > held:
                    continue
                mask_ref[pl.ds(pl.multiple_of(d * PAIR, PAIR), PAIR), c * LANES : (c + 1) * LANES] = (
                    piece[k, at : at + PAIR, :]
                )
            at = local * half + chunks * PAIR - row0
            if 0 <= at and at + PAIR <= held:
                count_ref[pl.ds(d, 1), :] = piece[k, at : at + PAIR, :].astype(F32)[:1]
    live = live_ref[...]
    used = jnp.maximum(jnp.sum(live[:, :1]), 1.0)
    step = 2 * LANES
    left = lax.broadcasted_iota(jnp.int32, (width, step), 1) % LANES < bsize
    for j in range(width // step):
        cols = slice(j * step, (j + 1) * step)
        pre_ref[:, cols] = dot(x_ref[...], jnp.where(left, w_ref[0, :, cols], w_ref[1, :, cols]))
        for i in range(2):
            t = 2 * j + i
            tile = slice(t * LANES, (t + 1) * LANES)
            total = jnp.sum(pre_ref[:, tile] * live, axis=0, keepdims=True)
            apart = pre_ref[:, tile] - total / used
            row_ref[t : t + 1, :] = total
            row_ref[tiles + t : tiles + t + 1, :] = jnp.sum(
                apart * apart * live, axis=0, keepdims=True
            )
    half = tiles // 2
    parts = [
        jnp.concatenate([row_ref[h * half : (h + 1) * half, :], row_ref[tiles + h * half : tiles + (h + 1) * half, :]])
        for h in range(2)
    ]
    odd = (me // core) % 2
    keep_ref[...] = jnp.where(odd == 1, parts[1], parts[0])
    send_ref[...] = jnp.where(odd == 1, parts[0], parts[1])


def combine(pairs):
    used = sum(c for c, _, _ in pairs)
    total = sum(t for _, t, _ in pairs)
    mean = total / jnp.maximum(used, 1.0)
    square = 0.0
    for c, t, q in pairs:
        apart = t / jnp.maximum(c, 1.0) - mean
        square = square + (q + c * apart * apart)
    return used, total, square


def merge_kernel(me_ref, count_ref, keep_ref, got_ref, out_ref, *, core):
    half = keep_ref.shape[0] // 2
    n = count_ref.shape[0]
    counts = [
        jnp.sum(count_ref[pl.ds(d, 1), :], keepdims=True) for d in (me_ref[0], me_ref[0] ^ core)
    ]
    pairs = [(c, ref[:half, :], ref[half:, :]) for c, ref in zip(counts, (keep_ref, got_ref))]
    _, total, square = combine(pairs)
    packed = jnp.concatenate([total, square])
    for d in range(n):
        out_ref[2 * half * d : 2 * half * (d + 1), :] = packed


def act_kernel(
    stats_ref, count_ref, norm_ref, pre_ref, live_ref, pick_ref, w_out_ref,
    slope_ref, act_ref, one_ref, two_ref, coef_ref, bags_ref, pay_ref,
    low_ref, ones_ref, twos_ref,
    *, core,
):
    n = count_ref.shape[0]
    rows, width = pre_ref.shape
    tiles = width // LANES
    counts = jnp.sum(count_ref[...], axis=1, keepdims=True)
    half = tiles // 2
    used, total, square = [], [], []
    for h in range(2):
        pairs = [
            (
                counts[d : d + 1, :] + counts[d ^ core : (d ^ core) + 1, :],
                stats_ref[d * tiles : d * tiles + half, :],
                stats_ref[d * tiles + half : (d + 1) * tiles, :],
            )
            for d in range(n)
            if (d // core) % 2 == h
        ]
        for held, v in zip((used, total, square), combine(pairs)):
            held.append(v)
    used = jnp.max(used[0])
    mean, square = jnp.concatenate(total) / used, jnp.concatenate(square)
    rstd = lax.rsqrt(square / used + 1e-05)
    for j in range(tiles):
        coef_ref[0:1, j * LANES : (j + 1) * LANES] = mean[j : j + 1, :]
        coef_ref[1:2, j * LANES : (j + 1) * LANES] = rstd[j : j + 1, :]
    coef_ref[2:3, :] = jnp.full((1, width), used, F32)
    coef_ref[3:4, :] = coef_ref[1:2, :] * norm_ref[0:1, :]
    bags = rows // SLOTS_BAG
    group = 8

    def fold(v):
        return (v[:group] + v[group : 2 * group]) + (v[2 * group : 3 * group] + v[3 * group :])

    def unfold(ref, j):
        total = ref[j, pl.ds(0, bags, stride=group), :]
        for i in range(1, group):
            total = total + ref[j, pl.ds(i, bags, stride=group), :]
        return total

    for j in range(tiles):
        cols = slice(j * LANES, (j + 1) * LANES)
        centre, scale, bias = coef_ref[0:1, cols], coef_ref[3:4, cols], norm_ref[1:2, cols]
        for b in range(bags):
            at = slice(b * SLOTS_BAG, (b + 1) * SLOTS_BAG)
            to = slice(b * group, (b + 1) * group)
            apart = pre_ref[at, cols] - centre
            y = scale * apart + bias
            capped = jnp.minimum(y, 20.0)
            e = jnp.exp(capped)
            top = e * (e + 2.0)
            below = top + 2.0
            inv = 1.0 / below
            gate = top * inv
            low_ref[at, :] = (y * gate).astype(BF)
            part = e * inv
            slope = gate + (4.0 * capped) * (part * (inv + part))
            slope_ref[at, cols] = slope
            slope = slope * live_ref[at, :]
            ones_ref[j, to, :] = fold(slope)
            twos_ref[j, to, :] = fold(slope * apart)
        act_ref[:, cols] = dot(pick_ref[...], low_ref[...])
        one_ref[:, cols] = unfold(ones_ref, j)
        two_ref[:, cols] = unfold(twos_ref, j) * coef_ref[1:2, cols]
    second = w_out_ref[...].astype(BF).astype(F32)
    bags = hdot(act_ref[...], second, 1, 1)
    pairs = bags.shape[0] // 2
    split = jnp.concatenate([hdot(pick(pairs, 0), bags), hdot(pick(pairs, 1), bags)], axis=0)
    bags_ref[...] = split
    eighth = pairs // 2
    packed = jnp.concatenate([split[i * eighth : (i + 1) * eighth] for i in range(4)], axis=1)
    for d in range(n):
        pay_ref[d * eighth : (d + 1) * eighth, :] = packed


def pick(pairs, which):
    r = lax.broadcasted_iota(jnp.int32, (pairs, 2 * pairs), 0)
    c = lax.broadcasted_iota(jnp.int32, (pairs, 2 * pairs), 1)
    return (c == 2 * r + which).astype(F32)


def spread(pairs, which):
    r = lax.broadcasted_iota(jnp.int32, (2 * pairs, pairs), 0)
    c = lax.broadcasted_iota(jnp.int32, (2 * pairs, pairs), 1)
    return (r == 2 * c + which).astype(F32)


def three(v):
    a = v.astype(BF)
    v = v - a.astype(F32)
    b = v.astype(BF)
    v = v - b.astype(F32)
    return a, b, v.astype(BF)


def loss_kernel(
    me_ref, all_ref, mask_ref, towers_ref, w_out_ref, act_ref, one_ref, two_ref,
    dact_ref, pay_ref, d_towers_ref, loss_ref, total_ref,
    score_ref, user_ref, item_ref, second_ref, row_ref, *, n,
):
    me = me_ref[0]
    embed = towers_ref.shape[1]
    total_rows = mask_ref.shape[0]
    eighth = all_ref.shape[0] // n

    def full(i):
        a = all_ref[:, 2 * i * embed : (2 * i + 1) * embed].reshape(n, eighth, embed)
        b = all_ref[:, (2 * i + 1) * embed : (2 * i + 2) * embed].reshape(n, eighth, embed)
        return jnp.stack([a, b], axis=1).reshape(total_rows, embed)

    bags_user, bags_item = full(0), full(1)
    user = hdot(bags_user, towers_ref[0]).astype(BF)
    item = hdot(bags_item, towers_ref[1]).astype(BF)
    root = math.sqrt(embed)
    score_ref[...] = dot(user, item, 1, 1) / root
    negatives = jnp.sum(mask_ref[...].astype(F32))
    count = negatives / total_rows
    step = 32

    def rows(i, carry):
        at = slice(i * step, (i + 1) * step)
        logits = score_ref[at, :]
        r = lax.broadcasted_iota(jnp.int32, logits.shape, 0) + i * step
        own = r == lax.broadcasted_iota(jnp.int32, logits.shape, 1)
        keep = own | (mask_ref[at, :].astype(F32) == 1.0)
        top = jnp.max(jnp.where(keep, logits, -jnp.inf), axis=1, keepdims=True)
        weights = jnp.where(keep, jnp.exp(logits - top), 0.0)
        total = jnp.sum(weights, axis=1, keepdims=True)
        hit = jnp.sum(jnp.where(own, logits, 0.0), axis=1, keepdims=True)
        score_ref[at, :] = (weights / total - own.astype(F32)) / count / root
        return carry + (top + jnp.log(total) - hit)

    ce = jnp.zeros((step, 1), F32)
    for i in range(total_rows // step):
        ce = rows(i, ce)
    loss_ref[0, 0] = jnp.sum(ce)
    total_ref[0, 0] = count
    parts = three(score_ref[...])
    d_user = sum(dot(p, item) for p in parts)
    d_item = sum(dot(user, p, 0, 0) for p in parts).T
    user_ref[...] = d_user
    item_ref[...] = d_item
    d_towers_ref[0] = hdot(bags_user, d_user, 0, 0)
    d_towers_ref[1] = hdot(bags_item, d_item, 0, 0)
    mine = pl.ds(pl.multiple_of(me * PAIR, PAIR), PAIR)
    back_user = hdot(user_ref[mine, :], towers_ref[0], 1, 1).astype(BF).astype(F32)
    back_item = hdot(item_ref[mine, :], towers_ref[1], 1, 1).astype(BF).astype(F32)
    d_emb = dot(spread(PAIR, 0), back_user) + dot(spread(PAIR, 1), back_item)
    d_act = dot(d_emb.astype(BF), w_out_ref[...].astype(BF))
    dact_ref[...] = d_act
    d_bias = jnp.sum(d_act * one_ref[...], axis=0, keepdims=True)
    d_gain = jnp.sum(d_act * two_ref[...], axis=0, keepdims=True)
    d_low = d_emb.T.astype(BF)
    second = sum(dot(d_low, p) for p in three(act_ref[...]))
    width = act_ref.shape[1]
    tiles = width // LANES
    for j in range(tiles):
        second_ref[pl.ds(j, embed, stride=tiles), :] = second[:, j * LANES : (j + 1) * LANES]
    for j in range(tiles):
        cols = slice(j * LANES, (j + 1) * LANES)
        row_ref[j : j + 1, :] = d_bias[:, cols]
        row_ref[tiles + j : tiles + j + 1, :] = d_gain[:, cols]
    sums = row_ref[...].astype(BF)
    chunk = embed * tiles // n
    for d in range(n):
        part = second_ref[d * chunk : (d + 1) * chunk, :]
        high = part.astype(BF)
        low = (part - high.astype(F32)).astype(BF)
        at = d * (2 * tiles + 2 * chunk)
        pay_ref[at : at + 2 * tiles, :] = sums
        pay_ref[at + 2 * tiles : at + 2 * tiles + 2 * chunk, :] = jnp.concatenate([high, low], axis=0)


def loss_spread(plan, bags, neg_mask, towers, w_out, act, one, two):
    embed = towers.shape[1]
    rows = neg_mask.shape[0]
    bags_user, bags_item = bags[:rows], bags[rows:]
    user = hdot(bags_user, towers[0]).astype(BF)
    item = hdot(bags_item, towers[1]).astype(BF)
    items = lax.all_gather(item, AXES, axis=0, tiled=True)
    root = math.sqrt(embed)
    logits = dot(user, items, 1, 1) / root
    at = lax.axis_index(AXES) * rows + lax.broadcasted_iota(jnp.int32, logits.shape, 0)
    own = lax.broadcasted_iota(jnp.int32, logits.shape, 1) == at
    keep = own | (neg_mask == 1)
    top = jnp.max(jnp.where(keep, logits, -jnp.inf), axis=1, keepdims=True)
    weights = jnp.where(keep, jnp.exp(logits - top), 0.0)
    total = jnp.sum(weights, axis=1, keepdims=True)
    ce = top + jnp.log(total) - jnp.sum(jnp.where(own, logits, 0.0), axis=1, keepdims=True)
    count = lax.psum(jnp.sum(neg_mask.astype(F32)), AXES) / items.shape[0]
    scores = (weights / total - own.astype(F32)) / count / root
    d_user = hdot(scores, items.astype(F32))
    d_item = lax.psum_scatter(
        hdot(scores, user.astype(F32), 0, 0), AXES, scatter_dimension=0, tiled=True
    )
    d_towers = jnp.stack([hdot(bags_user, d_user, 0, 0), hdot(bags_item, d_item, 0, 0)])
    back = jnp.stack([hdot(d_user, towers[0], 1, 1), hdot(d_item, towers[1], 1, 1)], axis=1)
    d_emb = back.reshape(2 * rows, embed).astype(BF)
    d_act = dot(d_emb, w_out.astype(BF))
    d_second = hdot(d_emb.astype(F32), act, 0, 0)
    sums = jnp.stack([jnp.sum(d_act * one, axis=0), jnp.sum(d_act * two, axis=0)])
    sums, d_second, d_towers, loss = lax.psum((sums, d_second, d_towers, jnp.sum(ce)), AXES)
    return d_act, sums.reshape(-1, LANES), d_second, d_towers, loss, count


def block_halves(me, owners_ref, g_ref, outs, masks, local):
    width = g_ref.shape[2]
    bsize = LANES // 2
    half, quarter = bsize // 2, bsize // 4
    side = width // bsize
    lane_half = lax.broadcasted_iota(jnp.int32, (quarter, LANES), 1) // bsize
    for i, m in enumerate(masks):
        for b in range(local):
            r, c, odd = place(owners_ref[(me ^ m) * local + b], side)
            base = pl.multiple_of(r * half, half)
            cols = pl.ds(pl.multiple_of(c * LANES, LANES), LANES)
            keep = lane_half == odd
            to = (i * local + b) * quarter
            for h, out in enumerate(outs):
                tile = g_ref[h, pl.ds(base, half), cols].astype(out.dtype)
                out[to : to + quarter, :] = jnp.where(keep, tile[:quarter], swap_halves(tile[quarter:]))


def grad_kernel(
    me_ref, owners_ref, sums_ref, coef_ref, norm_ref, dact_ref, slope_ref, pre_ref, live_ref, xt_ref,
    top_ref, low_ref, chunk_ref, d_norm_ref, g_ref, d_pre_ref, row_ref,
    *, parts, order, local,
):
    rows, width = pre_ref.shape
    tiles = width // LANES
    held = sums_ref.shape[0] // parts
    total = sums_ref[0:held, :].astype(F32)
    for d in range(1, parts):
        total = total + sums_ref[d * held : (d + 1) * held, :].astype(F32)
    d_norm_ref[0:tiles, :] = total[tiles : 2 * tiles]
    d_norm_ref[tiles : 2 * tiles, :] = total[:tiles]
    if held > 2 * tiles:
        chunk = chunk_ref.shape[0]
        chunk_ref[...] = total[2 * tiles : 2 * tiles + chunk] + total[2 * tiles + chunk :]
    else:
        chunk_ref[...] = jnp.zeros(chunk_ref.shape, F32)
    for j in range(tiles):
        cols = slice(j * LANES, (j + 1) * LANES)
        row_ref[0:1, cols] = total[j : j + 1]
        row_ref[1:2, cols] = total[tiles + j : tiles + j + 1]
    scale = norm_ref[0:1, :] * coef_ref[1:2, :]
    flat = scale * row_ref[0:1, :] / coef_ref[2:3, :]
    tilt = scale * row_ref[1:2, :] / coef_ref[2:3, :] * coef_ref[1:2, :]
    row_ref[2:3, :] = scale
    row_ref[3:4, :] = flat
    row_ref[4:5, :] = tilt
    block = 2 * LANES
    for j in range(width // block):
        for i in range(2):
            cols = slice(j * block + i * LANES, j * block + (i + 1) * LANES)
            for b in range(rows // SLOTS_BAG):
                at = slice(b * SLOTS_BAG, (b + 1) * SLOTS_BAG)
                lead = dact_ref[b : b + 1, cols] * row_ref[2:3, cols]
                apart = (pre_ref[at, cols] - coef_ref[0:1, cols]) * row_ref[4:5, cols]
                d_pre = slope_ref[at, cols] * lead - row_ref[3:4, cols] - apart
                d_pre_ref[at, cols] = (live_ref[at, :] * d_pre).astype(BF)
        cols = slice(j * block, (j + 1) * block)
        g_ref[:, :, cols] = dot(xt_ref[...], d_pre_ref[:, cols]).reshape(2, width // 2, block)
    block_halves(me_ref[0], owners_ref, g_ref, (top_ref, low_ref), order, local)


def keep_kernel(me_ref, owners_ref, g_ref, top_ref, low_ref, *, order, local):
    block_halves(me_ref[0], owners_ref, g_ref, (top_ref, low_ref), order, local)


def scatter_sum(plan, kept, sent, rows):
    rest = len(plan.rest)
    shape = (2, 2, rest, rows, LANES)
    one, two = (
        (k + plan.swap(s, plan.core).astype(F32)).reshape(shape) for k, s in zip(kept, sent)
    )
    got_one = plan.swap(one[1].astype(BF), plan.x)
    got_two = plan.swap(two[:, 1].astype(BF), plan.y)
    one = one[0] + got_one.astype(F32)
    two = two[:, 0] + got_two.astype(F32)
    got_one = plan.swap(one[1].astype(BF), plan.y)
    got_two = plan.swap(two[1].astype(BF), plan.x)
    one = one[0] + got_one.astype(F32)
    two = two[0] + got_two.astype(F32)
    if rest <= 4:
        both = jnp.concatenate([one[1:], two[1:]], axis=1).astype(BF)
        return one, two, [plan.swap(both[k], m) for k, m in enumerate(plan.rest[1:])]
    both = jnp.concatenate([one, two], axis=1)
    for b in reversed(plan.bits):
        both = both.reshape(2, -1, 2 * rows, LANES)
        both = both[0] + plan.swap(both[1].astype(BF), b).astype(F32)
    return both[:, :rows], both[:, rows:], []


def norm_kernel(*refs, n):
    one_ref, two_ref, chunk_ref = refs[:3]
    got = refs[3:-2]
    g_ref, pay_ref = refs[-2:]
    total = jnp.concatenate([one_ref[0], two_ref[0]], axis=0)
    for g in got:
        total = total + g[...].astype(F32)
    g_ref[...] = total
    chunk = chunk_ref[...]
    squares = jnp.sum(total * total, keepdims=True) + jnp.sum(chunk * chunk, keepdims=True)
    high = chunk.astype(BF)
    low = chunk - high.astype(F32)
    for i, v in enumerate(three(squares)):
        low = jnp.where(spare(chunk.shape, i), v.astype(F32), low)
    packed = jnp.concatenate([high, low.astype(BF)], axis=0)
    rows = packed.shape[0]
    for d in range(n):
        pay_ref[d * rows : (d + 1) * rows, :] = packed


def spare(shape, i):
    row = lax.broadcasted_iota(jnp.int32, shape, 0)
    lane = lax.broadcasted_iota(jnp.int32, shape, 1)
    return (row == shape[0] - 1) & (lane == LANES - 3 + i)


def adamw(grad, weight, first, second):
    first = BETA_ONE * first + (1 - BETA_ONE) * grad
    second = BETA_TWO * second + (1 - BETA_TWO) * grad * grad
    step = (
        first / (1 - BETA_ONE**STEP) / (jnp.sqrt(second / (1 - BETA_TWO**STEP)) + EPSILON)
    )
    return weight - RATE * (step + DECAY * weight), first, second


def eliminate(gram_ref, power_ref):
    count, size, lanes = gram_ref.shape
    group = 8
    lane = lax.broadcasted_iota(jnp.int32, (count * group, lanes), 1)
    left = lax.broadcasted_iota(jnp.int32, (1, lanes), 1) < size
    for at in range(0, size, group):
        rest = at + group
        gram, power = gram_ref[:, at:rest, :], power_ref[:, at:rest, :]
        flat = gram.reshape(count * group, lanes)
        cols = [
            jnp.take_along_axis(flat, (lane // size) * size + at + i, axis=1).reshape(gram.shape)
            for i in range(group)
        ]
        for i in range(group):
            inv = lax.rsqrt(cols[i][:, i : i + 1, :])
            row, power_row = gram[:, i : i + 1, :] * inv, power[:, i : i + 1, :] * inv
            gram_ref[:, at + i : at + i + 1, :] = row
            power_ref[:, at + i : at + i + 1, :] = power_row
            f = cols[i] * inv
            gram, power = gram - f * row, power - f * power_row
            for j in range(i + 1, group):
                cols[j] = cols[j] - f * f[:, j : j + 1, :]
        if rest == size:
            return
        a, b, c = (v.astype(F32) for v in three(gram_ref[:, at:rest, :]))
        d, e, f = (v.astype(F32) for v in three(power_ref[:, at:rest, :]))
        lhs = jnp.concatenate([a, a, b, b, a, c], axis=1).astype(BF)
        rhs = jnp.concatenate([a, b, a, b, c, a], axis=1)
        rhs = jnp.concatenate([rhs, jnp.concatenate([d, e, d, e, f, d], axis=1)], axis=2).astype(BF)
        turned = [lhs[m].T for m in range(count)]
        for m in range(count):
            one = dot(turned[m][rest:size], rhs[m])
            two = dot(turned[m][size + rest :], rhs[m])
            gram_ref[m, rest:, :] = gram_ref[m, rest:, :] - jnp.where(left, one[:, :lanes], two[:, :lanes])
            power_ref[m, rest:, :] = power_ref[m, rest:, :] - jnp.where(left, one[:, lanes:], two[:, lanes:])


def pair(a, b):
    return jnp.concatenate([a, b], axis=1)


def prepare_kernel(
    w_hbm, left_hbm, right_hbm, bl_hbm, br_hbm, first_hbm, second_hbm, ema_hbm,
    moments_ref, stats_ref, bases_ref, weights_ref, turned_ref, powers_ref,
    w_ref, left_ref, right_ref, bl_ref, br_ref, first_ref, second_ref, ema_ref, sems,
):
    fetch(
        (w_hbm, left_hbm, right_hbm, bl_hbm, br_hbm, first_hbm, second_hbm, ema_hbm),
        (w_ref, left_ref, right_ref, bl_ref, br_ref, first_ref, second_ref, ema_ref),
        sems,
    )
    each = range(w_ref.shape[0])
    for b in each:
        moments_ref[b] = pair(first_ref[b], second_ref[b])
        stats_ref[b] = pair(left_ref[b], right_ref[b])
        bases_ref[b] = pair(bl_ref[b], br_ref[b])
        weights_ref[b] = pair(w_ref[b], ema_ref[b])
    half = [hdot(bl_ref[b], first_ref[b], 0, 0) for b in each]
    for b in each:
        turned_ref[b] = hdot(half[b], br_ref[b])
    lefts = [hdot(bl_ref[b], left_ref[b], 0, 0) for b in each]
    rights = [hdot(br_ref[b], right_ref[b], 0, 0) for b in each]
    for b in each:
        powers_ref[b] = pair(lefts[b], rights[b])


def turn_kernel(
    me_ref, owners_ref, g_ref, bases_ref,
    wo_hbm, mo_hbm, vo_hbm, eo_hbm, wt_hbm, mt_hbm, vt_hbm, wn_hbm, mn_hbm, vn_hbm,
    grad_ref, squares_ref, powers_ref, scale_ref,
    wide_ref, towers_ref, norms_ref, sems,
):
    local, bsize = bases_ref.shape[0], bases_ref.shape[1]
    sources = (wo_hbm, mo_hbm, vo_hbm, eo_hbm, wt_hbm, mt_hbm, vt_hbm, wn_hbm, mn_hbm, vn_hbm)
    targets = [wide_ref.at[i] for i in range(4)]
    targets += [towers_ref.at[i] for i in range(3)] + [norms_ref.at[i] for i in range(3)]
    copies = [pltpu.make_async_copy(a, b, sems.at[i]) for i, (a, b) in enumerate(zip(sources, targets))]
    for c in copies:
        c.start()
    largest = jnp.max(jnp.abs(g_ref[...]), keepdims=True)
    largest = jnp.where(largest > 0.0, largest, 1.0)
    scale_ref[...] = jnp.broadcast_to(largest, scale_ref.shape)
    half = bsize // 2
    each = range(local)
    grads = []
    for b in each:
        odd = owners_ref[me_ref[0] * local + b] % 2
        quarters = []
        for i in range(2):
            at = (i * local + b) * half // 2
            tile = g_ref[at : at + half // 2, :]
            tile = jnp.where(odd == 1, swap_halves(tile), tile)
            quarters += [tile[:, :bsize], tile[:, bsize:]]
        grads.append(jnp.concatenate(quarters, axis=0) / largest)
    bl = [bases_ref[b, :, :bsize] for b in each]
    br = [bases_ref[b, :, bsize:] for b in each]
    by_left = [hdot(bl[b], grads[b], 0, 0) for b in each]
    by_right = [hdot(grads[b], br[b]) for b in each]
    outer = [hdot(grads[b], grads[b], 1, 1) for b in each]
    inner = [hdot(grads[b], grads[b], 0, 0) for b in each]
    for b in each:
        squares_ref[b] = pair(outer[b], inner[b])
    for b in each:
        grad_ref[b] = pair(grads[b], hdot(by_left[b], br[b]))
    lefts = [hdot(by_left[b], grads[b], 1, 1) for b in each]
    rights = [hdot(by_right[b], grads[b], 0, 0) for b in each]
    for b in each:
        powers_ref[b] = pair(lefts[b], rights[b])
    for c in copies:
        c.wait()


def step_kernel(
    got_ref, d_norm_ref, d_towers_ref,
    grad_ref, squares_ref, powers_ref, scale_ref,
    old_ref, towers_ref, norms_ref,
    moments_ref, stats_ref, bases_ref, weights_ref, turned_first_ref, powers_old_ref,
    *refs, n,
):
    (
        w_out, low_out, left_out, right_out, bl_out, br_out, first_out, second_out, ema_out,
        wo_out, mo_out, vo_out, eo_out, wt_out, mt_out, vt_out, wn_out, mn_out, vn_out, gn_out,
        gram_ref, power_ref, wide_ref, dn_ref, flat_ref,
    ) = refs
    local, bsize = bases_ref.shape[0], bases_ref.shape[1]
    embed, width = old_ref.shape[1:]
    tiles = width // LANES
    held = got_ref.shape[0] // n
    if n > 1:
        chunk = held // 2
        used = functools.reduce(jnp.logical_or, [spare((chunk, LANES), i) for i in range(3)])
        squares = jnp.zeros((chunk, LANES), F32)
        for d in range(n):
            part = got_ref[d * held : (d + 1) * held, :].astype(F32)
            squares = squares + jnp.where(used, part[chunk:], 0.0)
            flat_ref[d * chunk : (d + 1) * chunk, :] = part[:chunk] + jnp.where(used, 0.0, part[chunk:])
        squares = jnp.sum(squares)
        for j in range(tiles):
            wide_ref[:, j * LANES : (j + 1) * LANES] = flat_ref[pl.ds(j, embed, stride=tiles), :]
    else:
        squares = jnp.max(got_ref[0:1, :LANES])
        wide_ref[...] = got_ref[8 : 8 + embed, :]
    squares = squares + jnp.sum(d_towers_ref[...] * d_towers_ref[...])
    squares = squares + jnp.sum(d_norm_ref[...] * d_norm_ref[...])
    norm = jnp.sqrt(jnp.full((1, LANES), squares, F32))
    gn_out[0, 0] = jnp.max(norm)
    factor = (CLIP / jnp.maximum(norm, CLIP))[:, :1]
    each = range(local)
    lead = factor * scale_ref[0:1, 0:1]
    twice = (1 - BETA_TWO) * lead * lead
    lefts, rights = [], []
    for b in each:
        powers = BETA_TWO * powers_old_ref[b] + twice * powers_ref[b]
        power_ref[b] = powers
        lefts.append(powers[:, :bsize])
        rights.append(powers[:, bsize:])
    for b in each:
        gram_ref[b] = pair(hdot(lefts[b], lefts[b], 1, 1), hdot(rights[b], rights[b], 1, 1))
    ratios = []
    for b in each:
        stats = BETA_TWO * stats_ref[b] + twice * squares_ref[b]
        left_out[b], right_out[b] = stats[:, :bsize], stats[:, bsize:]
        first_out[b] = BETA_ONE * moments_ref[b, :, :bsize] + (1 - BETA_ONE) * lead * grad_ref[b, :, :bsize]
        turned = grad_ref[b, :, bsize:]
        second = BETA_TWO * moments_ref[b, :, bsize:] + twice * turned * turned
        second_out[b] = second
        moved = BETA_ONE * turned_first_ref[b] + (1 - BETA_ONE) * lead * turned
        moved = moved / (1 - BETA_ONE**STEP)
        ratios.append(moved / (jnp.sqrt(second / (1 - BETA_TWO**STEP)) + EPSILON))
    half = [hdot(bases_ref[b, :, :bsize], ratios[b]) for b in each]
    updates = [hdot(half[b], bases_ref[b, :, bsize:], 1, 1) for b in each]
    for b in each:
        old = weights_ref[b, :, :bsize]
        new = old - RATE * (updates[b] + DECAY * old)
        w_out[b] = new
        low_out[b] = new.astype(BF)
        ema_out[b] = AVG_KEEP * weights_ref[b, :, bsize:] + AVG_TAKE * new
    new, m, v = adamw(wide_ref[...] * factor, old_ref[0], old_ref[1], old_ref[2])
    wo_out[...], mo_out[...], vo_out[...] = new, m, v
    eo_out[...] = AVG_KEEP * old_ref[3] + AVG_TAKE * new
    for t in range(2):
        wt_out[t], mt_out[t], vt_out[t] = adamw(
            d_towers_ref[t] * factor, towers_ref[0, t], towers_ref[1, t], towers_ref[2, t]
        )
        for j in range(tiles):
            dn_ref[t : t + 1, j * LANES : (j + 1) * LANES] = d_norm_ref[
                t * tiles + j : t * tiles + j + 1, :
            ]
    wn_out[...], mn_out[...], vn_out[...] = adamw(
        dn_ref[...] * factor, norms_ref[0], norms_ref[1], norms_ref[2]
    )
    eliminate(gram_ref, power_ref)
    for b in each:
        turned = power_ref[b].T
        bl_out[b], br_out[b] = turned[:bsize], turned[bsize:]


def exchange(payload):
    return lax.all_to_all(payload, AXES, 0, 0, tiled=True)


def on_device(
    plan,
    codes, field_offsets, seg_mask, neg_mask, owners,
    w_hidden, stat_left, stat_right, basis_left, basis_right, mom1_hidden, mom2_hidden, ema_hidden,
    w_out, mom1_out, mom2_out, ema_out,
    w_towers, mom1_towers, mom2_towers,
    w_norm, mom1_norm, mom2_norm,
):
    n = plan.n
    local, bsize = w_hidden.shape[0], w_hidden.shape[1]
    width, embed = w_out.shape
    slots = codes.shape[0]
    rows, total_rows = neg_mask.shape
    tiles = width // LANES
    half = bsize // 2
    bags = slots // SLOTS_BAG
    masked = total_rows <= 1024 and n <= embed
    me = lax.axis_index(AXES).astype(jnp.int32)[None]

    chunks = total_rows // LANES if masked else 0
    size = local * half + chunks * PAIR + PAIR
    (payload,) = call(
        functools.partial(pack_kernel, masked=masked),
        [((size, LANES), BF)],
        [me, in_hbm(owners), w_hidden, neg_mask, seg_mask.reshape(-1, LANES)],
        smem=2,
        hbm=3,
        scratch=[
            pltpu.VMEM(w_hidden.shape, F32),
            pltpu.VMEM(neg_mask.shape, jnp.int32),
            pltpu.VMEM((slots // LANES, LANES), jnp.int32),
            pltpu.SemaphoreType.DMA((3,)),
        ],
        name="pack",
    )
    cut = max(half, size // 2 // half * half)
    cut = min(cut, local * half)
    blocks = (local, bsize, bsize)
    twin = (local, bsize, 2 * bsize)
    state = [
        w_hidden, stat_left, stat_right, basis_left, basis_right, mom1_hidden, mom2_hidden, ema_hidden
    ]
    prepared = call(
        prepare_kernel,
        [(twin, F32)] * 4 + [(blocks, F32), (twin, F32)],
        state,
        hbm=len(state),
        scratch=[pltpu.VMEM(blocks, F32)] * len(state) + [pltpu.SemaphoreType.DMA((len(state),))],
        limit=12,
        name="prepare",
        cost=10_000_000,
    )
    turned_out, turned_mom1, turned_mom2, turned_ema = (
        a.T for a in (w_out, mom1_out, mom2_out, ema_out)
    )
    early = hash_inputs(codes, field_offsets)
    live = jnp.broadcast_to(seg_mask.astype(F32)[:, None], (slots, LANES))
    slot_bag = lax.broadcasted_iota(jnp.int32, (bags, slots), 1) // SLOTS_BAG
    in_bag = slot_bag == lax.broadcasted_iota(jnp.int32, (bags, slots), 0)
    chosen = jnp.where(in_bag, seg_mask.astype(F32)[None], 0.0).astype(BF)
    late = (*prepared, live, chosen)
    zero = (me[0] >> 16).astype(BF)

    def held_by(pieces):
        return [([m | base for m in plan.rest], row) for _, base, row in pieces]

    def place_blocks(pieces):
        (planes,) = call(
            functools.partial(assemble_kernel, holds=held_by(pieces), local=local),
            [((2, width, width), BF)],
            [me, owners] + [a for a, _, _ in pieces],
            smem=2,
            limit=8,
            name="assemble",
            cost=10_000_000,
        )
        return planes

    pieces, done, planes, (x, x_turned), (*prepared, live, chosen) = gather_pieces(
        plan, payload, cut, zero, early, late, place_blocks
    )
    mask_shape = (total_rows, total_rows) if masked else (PAIR, LANES)
    holds = held_by(pieces)
    arrays = [a for a, _, _ in pieces]
    pre, kept, sent, counts, mask, _ = call(
        functools.partial(
            pre_kernel, holds=holds, done=done, local=local, masked=masked, core=plan.core
        ),
        [
            ((slots, width), F32),
            ((tiles, LANES), F32),
            ((tiles, LANES), F32),
            ((n, LANES), F32),
            (mask_shape, BF),
            ((2, width, width), BF),
        ],
        [me, owners, planes] + arrays + [x, live],
        smem=2,
        scratch=[pltpu.VMEM((2 * tiles, LANES), F32)],
        aliases={2: 5},
        limit=16,
        name="pre",
    )
    (stats,) = call(
        functools.partial(merge_kernel, core=plan.core),
        [((n * tiles, LANES), F32)],
        [me, counts, kept, plan.swap(sent, plan.core)],
        smem=1,
        limit=4,
        name="merge",
    )
    stats = exchange(stats)
    slope, act, one, two, coef, bag_sums, pay = call(
        functools.partial(act_kernel, core=plan.core),
        [
            ((slots, width), F32),
            ((bags, width), F32),
            ((bags, width), F32),
            ((bags, width), F32),
            ((8, width), F32),
            ((bags, embed), F32),
            ((n * 8, LANES), F32),
        ],
        [stats, counts, w_norm, pre, live, chosen, turned_out],
        scratch=[
            pltpu.VMEM((slots, LANES), BF),
            pltpu.VMEM((tiles, bags * 8, LANES), F32),
            pltpu.VMEM((tiles, bags * 8, LANES), F32),
        ],
        limit=12,
        name="act",
    )
    if masked:
        chunk = embed * tiles // n
        everyone = exchange(pay)
        d_act, pay, d_towers, loss_sum, count = call(
            functools.partial(loss_kernel, n=n),
            [
                ((bags, width), F32),
                ((n * (2 * tiles + 2 * chunk), LANES), BF),
                ((2, embed, embed), F32),
                ((1, 1), F32),
                ((1, 1), F32),
            ],
            [me, everyone, mask, w_towers, turned_out, act, one, two],
            smem=1,
            smem_outs=2,
            scratch=[
                pltpu.VMEM((total_rows, total_rows), F32),
                pltpu.VMEM((total_rows, embed), F32),
                pltpu.VMEM((total_rows, embed), F32),
                pltpu.VMEM((embed * tiles, LANES), F32),
                pltpu.VMEM((2 * tiles, LANES), F32),
            ],
            name="loss",
        )
        sums, parts = exchange(pay), n
        loss_sum, count = loss_sum[0, 0], count[0, 0]
    else:
        d_act, sums, d_second, d_towers, loss_sum, count = loss_spread(
            plan, bag_sums, neg_mask, w_towers, turned_out, act, one, two
        )
        parts = 1
        chunk = 8
    groups = [m for m in (0, plan.y, plan.x, plan.x | plan.y)]
    keep_order = [g | r for g in groups for r in plan.rest]
    order = (keep_order, [m | plan.core for m in keep_order])
    packed = (n // 2 * local * half // 2, LANES)
    packed = (n // 2 * local * half // 2, LANES)
    *sent, second_chunk, d_norm, full = call(
        functools.partial(grad_kernel, parts=parts, order=order[1], local=local),
        [
            (packed, BF),
            (packed, BF),
            ((chunk, LANES), F32),
            ((2 * tiles, LANES), F32),
            ((2, width // 2, width), F32),
        ],
        [me, owners, sums, coef, w_norm, d_act, slope, pre, live, x_turned],
        smem=2,
        scratch=[pltpu.VMEM((slots, width), BF), pltpu.VMEM((8, width), F32)],
        limit=16,
        name="grad",
    )
    kept = call(
        functools.partial(keep_kernel, order=order[0], local=local),
        [(packed, F32), (packed, F32)],
        [me, owners, full],
        smem=2,
        limit=8,
        name="keep",
        cost=100_000_000,
    )
    one_sum, two_sum, others = scatter_sum(plan, kept, sent, local * half // 2)
    copies = n if masked else 1
    grad, pay = call(
        functools.partial(norm_kernel, n=copies),
        [((local * half, LANES), F32), ((copies * 2 * chunk, LANES), BF)],
        [one_sum, two_sum, second_chunk, *others],
        name="norm",
    )
    if masked:
        got = exchange(pay)
    else:
        squares = lax.psum(jnp.sum(grad * grad), AXES) + jnp.sum(d_second * d_second)
        got = jnp.concatenate([jnp.full((8, width), squares, F32), d_second], axis=0)
    moments, stats, bases, weights, turned_first, powers_old = prepared
    plain = [
        turned_out, turned_mom1, turned_mom2, turned_ema,
        w_towers, mom1_towers, mom2_towers,
        w_norm, mom1_norm, mom2_norm,
    ]
    turned = call(
        turn_kernel,
        [(twin, F32)] * 3
        + [((8, LANES), F32), ((4, embed, width), F32), ((3, 2, embed, embed), F32), ((3, 2, width), F32)],
        [me, owners, grad, bases, *plain],
        smem=2,
        hbm=len(plain),
        scratch=[pltpu.SemaphoreType.DMA((len(plain),))],
        name="turn",
        cost=10_000_000,
    )
    outs = [(blocks, F32), (blocks, BF)] + [(blocks, F32)] * 7
    outs += [((embed, width), F32)] * 4 + [((2, embed, embed), F32)] * 3 + [((2, width), F32)] * 3
    new = call(
        functools.partial(step_kernel, n=n if masked else 1),
        outs + [((1, 1), F32)],
        [
            got, d_norm, d_towers, *turned,
            moments, stats, bases, weights, turned_first, powers_old,
        ],
        smem_outs=1,
        scratch=[
            pltpu.VMEM(twin, F32),
            pltpu.VMEM(twin, F32),
            pltpu.VMEM((embed, width), F32),
            pltpu.VMEM((2, width), F32),
            pltpu.VMEM((embed * tiles, LANES), F32),
        ],
        name="step",
    )
    return (loss_sum, count, new[-1][0, 0], *new[:9], *(a.T for a in new[9:13]), *new[13:-1])


def solution(mesh):
    split = P(("gx", "gy"))
    plan = Plan(mesh.shape["gx"], mesh.shape["gy"])
    return jax.shard_map(
        functools.partial(on_device, plan),
        mesh=mesh,
        in_specs=(split, P(), split, split, P()) + (split,) * 8 + (P(),) * 10,
        out_specs=(P(),) * 3 + (split,) * 9 + (P(),) * 10,
        check_vma=False,
    )
```

```python
import functools
import math

import jax
import jax.numpy as jnp
from jax import lax
from jax.experimental import pallas as pl
from jax.experimental.pallas import tpu as pltpu
from jax.sharding import PartitionSpec as P

FIELDS = 4
BAG = 8
HASH_RANGE = 4096
STEP = 10
BETA_ONE = 0.9
BETA_TWO = 0.95
EPSILON = 1e-08
RATE = 0.03
DECAY = 0.01
CLIP = 0.01
AVG_KEEP = 0.8
AVG_TAKE = 0.2

F32 = jnp.float32
BF = jnp.bfloat16
HIGH = lax.Precision.HIGHEST
AXES = ("gx", "gy")
LANES = 128
SLOTS_BAG = FIELDS * BAG
PAIR = 16
MIB = 1 << 20


def dot(a, b, ca=1, cb=0, precision=None):
    return lax.dot_general(
        a, b, (((ca,), (cb,)), ((), ())), precision=precision, preferred_element_type=F32
    )


hdot = functools.partial(dot, precision=HIGH)


def spec(space=pltpu.VMEM):
    return pl.BlockSpec(memory_space=space)


def in_hbm(a):
    return pltpu.with_memory_space_constraint(a, pltpu.HBM)


def call(kernel, outs, args, smem=0, hbm=0, smem_outs=0, aliases=None, scratch=(), limit=16, name=None, cost=None):
    args = list(args)
    specs = [spec(pltpu.SMEM)] * smem + [spec()] * (len(args) - smem - hbm) + [spec(pltpu.HBM)] * hbm
    if hbm:
        args[-hbm:] = [in_hbm(a) for a in args[-hbm:]]
    spaces = [pltpu.VMEM] * (len(outs) - smem_outs) + [pltpu.SMEM] * smem_outs
    estimate = None
    if cost:
        estimate = pl.CostEstimate(flops=cost, bytes_accessed=cost // 100, transcendentals=0)
    return pl.pallas_call(
        kernel,
        out_shape=[jax.ShapeDtypeStruct(s, t) for s, t in outs],
        in_specs=specs,
        out_specs=[spec(space) for space in spaces],
        scratch_shapes=list(scratch),
        compiler_params=pltpu.CompilerParams(vmem_limit_bytes=limit * MIB),
        cost_estimate=estimate,
        input_output_aliases=aliases or {},
        name=name,
    )(*args)


def fetch(sources, targets, sems):
    copies = [pltpu.make_async_copy(a, b, sems.at[i]) for i, (a, b) in enumerate(zip(sources, targets))]
    for c in copies:
        c.start()
    for c in copies:
        c.wait()


def swap_halves(v):
    half = v.shape[1] // 2
    return jnp.concatenate([v[:, half:], v[:, :half]], axis=1)


def place(q, side):
    shift = side.bit_length() - 1
    return q >> shift, (q & (side - 1)) >> 1, q & 1


class Plan:
    def __init__(self, gx, gy):
        self.gx, self.gy, self.n = gx, gy, gx * gy
        self.core = gy
        self.x = 2 * gy
        self.y = 1
        bits = []
        b = 2
        while b < gy:
            bits.append(b)
            b *= 2
        b = 4
        while b < gx:
            bits.append(b * gy)
            b *= 2
        self.bits = bits
        rest = [0]
        for b in bits:
            rest = rest + [m | b for m in rest]
        self.rest = rest

    def swap(self, a, mask):
        mx, my = mask // self.gy, mask % self.gy
        if my == 0:
            return lax.ppermute(a, "gx", [(i, i ^ mx) for i in range(self.gx)])
        if mx == 0:
            return lax.ppermute(a, "gy", [(i, i ^ my) for i in range(self.gy)])
        return lax.ppermute(a, AXES, [(i, i ^ mask) for i in range(self.n)])


def pack_kernel(
    w_hbm, neg_hbm, seg_hbm, out_ref, w_ref, neg_ref, seg_ref, sems, *, masked
):
    fetch((w_hbm, neg_hbm, seg_hbm), (w_ref, neg_ref, seg_ref), sems)
    local, bsize = w_ref.shape[0], w_ref.shape[1]
    half = bsize // 2
    for b in range(local):
        both = jnp.concatenate([w_ref[b, :half, :], w_ref[b, half:, :]], axis=1)
        out_ref[b * half : (b + 1) * half, :] = both.astype(BF)
    at = local * half
    if masked:
        for c in range(neg_ref.shape[1] // LANES):
            part = neg_ref[:, c * LANES : (c + 1) * LANES].astype(F32)
            out_ref[at : at + PAIR, :] = part.astype(BF)
            at += PAIR
    used = jnp.sum(seg_ref[...].astype(F32), axis=0, keepdims=True)
    out_ref[at : at + PAIR, :] = jnp.broadcast_to(used, (PAIR, LANES)).astype(BF)


def gather_pieces(plan, payload, cut, zero, early, late, place_blocks):
    stack = payload[None]
    if len(plan.rest) <= 4:
        stack = jnp.concatenate([stack] + [plan.swap(stack, m) for m in plan.rest[1:]], axis=0)
    else:
        for b in plan.bits:
            stack = jnp.concatenate([stack, plan.swap(stack, b)], axis=0)
    stack, early = lax.optimization_barrier((stack, early))
    by_x = plan.swap(stack, plan.x)
    by_y = plan.swap(stack, plan.y)
    by_x, by_y, late = lax.optimization_barrier((by_x, by_y, late))
    first = plan.swap(by_x[:, :cut] + zero, plan.y)
    second = plan.swap(by_y[:, cut:] + zero, plan.x)
    ready = [(stack, 0, 0), (by_x, plan.x, 0), (by_y, plan.y, 0)]
    ready += swapped(plan, ready)
    planes = place_blocks(ready)
    first, second, planes = lax.optimization_barrier((first, second, planes))
    last = [(first, plan.x | plan.y, 0), (second, plan.x | plan.y, cut)]
    return ready + last + swapped(plan, last), len(ready), planes, early, late


def swapped(plan, pieces):
    return [(plan.swap(a, plan.core), m | plan.core, row) for a, m, row in pieces]


def hash_kernel(codes_hbm, offsets_hbm, x_ref, xt_ref, codes_ref, offsets_ref, sems):
    rows, width = codes_ref.shape
    groups = 2 * FIELDS
    step = 128
    head = pltpu.make_async_copy(offsets_hbm, offsets_ref, sems.at[0])
    head.start()
    parts = []
    for i in range(rows // step):
        at = pl.ds(i * step, step)
        parts.append(pltpu.make_async_copy(codes_hbm.at[at], codes_ref.at[at], sems.at[1 + i]))
        parts[i].start()
    head.wait()
    for i, part in enumerate(parts):
        part.wait()
        at = slice(i * step, (i + 1) * step)
        salted = codes_ref[at, :].reshape(-1, groups, BAG, width) + offsets_ref[...][None, :, None, :]
        salted = (salted & (HASH_RANGE - 1)).reshape(step, width)
        x = (salted.astype(F32) * (2.0 / (HASH_RANGE - 1)) - 1.0).astype(BF)
        x_ref[at, :] = x
        quarter = LANES // 4
        turned = x.T.reshape(-1, 2, quarter, step)
        for h in range(2):
            xt_ref[h * width // 2 : (h + 1) * width // 2, at] = turned[:, h].reshape(-1, step)


def hash_inputs(codes, offsets):
    rows, width = codes.shape
    return call(
        hash_kernel,
        [((rows, width), BF), ((width, rows), BF)],
        [codes, offsets],
        hbm=2,
        scratch=[
            pltpu.VMEM(codes.shape, jnp.int32),
            pltpu.VMEM(offsets.shape, jnp.int32),
            pltpu.SemaphoreType.DMA((1 + rows // 128,)),
        ],
        limit=12,
        name="hash",
        cost=20_000_000,
    )


def assemble(w_ref, me, owners_ref, piece_refs, holds, local):
    width = w_ref.shape[1]
    bsize = LANES // 2
    half = bsize // 2
    side = width // bsize
    for piece, (masks, row0) in zip(piece_refs, holds):
        for k, m in enumerate(masks):
            for b in range(local):
                at = b * half - row0
                if at < 0 or at + half > piece.shape[1]:
                    continue
                r, c, odd = place(owners_ref[(me ^ m) * local + b], side)
                tile = piece[k, at : at + half, :]
                rows = pl.multiple_of(r * bsize, bsize)
                low = pl.multiple_of(r * bsize + half, half)
                cols = pl.ds(pl.multiple_of(c * LANES, LANES), LANES)
                other = swap_halves(tile)
                w_ref[odd, pl.ds(rows, half), cols] = jnp.where(odd == 1, other, tile)
                w_ref[odd, pl.ds(low, half), cols] = jnp.where(odd == 1, tile, other)


def assemble_kernel(me_ref, owners_ref, *refs, holds, local):
    assemble(refs[-1], me_ref[0], owners_ref, refs[:-1], holds, local)


def pre_kernel(*refs, holds, done, local, masked, core):
    me_ref, owners_ref = refs[:2]
    pieces = len(holds)
    piece_refs = refs[3 : 3 + pieces]
    x_ref, live_ref = refs[3 + pieces : 5 + pieces]
    pre_ref, keep_ref, send_ref, count_ref, mask_ref, w_ref, row_ref = refs[5 + pieces :]
    width = x_ref.shape[1]
    bsize = LANES // 2
    half = bsize // 2
    tiles = width // LANES
    me = me_ref[0]
    chunks = mask_ref.shape[1] // LANES if masked else 0
    assemble(w_ref, me, owners_ref, piece_refs[done:], holds[done:], local)
    for piece, (masks, row0) in zip(piece_refs, holds):
        held = piece.shape[1]
        for k, m in enumerate(masks):
            d = me ^ m
            for c in range(chunks):
                at = local * half + c * PAIR - row0
                if at < 0 or at + PAIR > held:
                    continue
                mask_ref[pl.ds(pl.multiple_of(d * PAIR, PAIR), PAIR), c * LANES : (c + 1) * LANES] = (
                    piece[k, at : at + PAIR, :]
                )
            at = local * half + chunks * PAIR - row0
            if 0 <= at and at + PAIR <= held:
                count_ref[pl.ds(d, 1), :] = piece[k, at : at + PAIR, :].astype(F32)[:1]
    live = live_ref[...]
    used = jnp.maximum(jnp.sum(live[:, :1]), 1.0)
    step = 2 * LANES
    left = lax.broadcasted_iota(jnp.int32, (width, step), 1) % LANES < bsize
    for j in range(width // step):
        cols = slice(j * step, (j + 1) * step)
        pre_ref[:, cols] = dot(x_ref[...], jnp.where(left, w_ref[0, :, cols], w_ref[1, :, cols]))
        for i in range(2):
            t = 2 * j + i
            tile = slice(t * LANES, (t + 1) * LANES)
            total = jnp.sum(pre_ref[:, tile] * live, axis=0, keepdims=True)
            apart = pre_ref[:, tile] - total / used
            row_ref[t : t + 1, :] = total
            row_ref[tiles + t : tiles + t + 1, :] = jnp.sum(
                apart * apart * live, axis=0, keepdims=True
            )
    half = tiles // 2
    parts = [
        jnp.concatenate([row_ref[h * half : (h + 1) * half, :], row_ref[tiles + h * half : tiles + (h + 1) * half, :]])
        for h in range(2)
    ]
    odd = (me // core) % 2
    keep_ref[...] = jnp.where(odd == 1, parts[1], parts[0])
    send_ref[...] = jnp.where(odd == 1, parts[0], parts[1])


def combine(pairs):
    used = sum(c for c, _, _ in pairs)
    total = sum(t for _, t, _ in pairs)
    mean = total / jnp.maximum(used, 1.0)
    square = 0.0
    for c, t, q in pairs:
        apart = t / jnp.maximum(c, 1.0) - mean
        square = square + (q + c * apart * apart)
    return used, total, square


def merge_kernel(me_ref, count_ref, keep_ref, got_ref, out_ref, *, core):
    half = keep_ref.shape[0] // 2
    n = count_ref.shape[0]
    counts = [
        jnp.sum(count_ref[pl.ds(d, 1), :], keepdims=True) for d in (me_ref[0], me_ref[0] ^ core)
    ]
    pairs = [(c, ref[:half, :], ref[half:, :]) for c, ref in zip(counts, (keep_ref, got_ref))]
    _, total, square = combine(pairs)
    packed = jnp.concatenate([total, square])
    for d in range(n):
        out_ref[2 * half * d : 2 * half * (d + 1), :] = packed


def act_kernel(
    stats_ref, count_ref, norm_ref, pre_ref, live_ref, pick_ref, w_out_ref,
    slope_ref, act_ref, one_ref, two_ref, coef_ref, bags_ref, pay_ref,
    low_ref, ones_ref, twos_ref,
    *, core,
):
    n = count_ref.shape[0]
    rows, width = pre_ref.shape
    tiles = width // LANES
    counts = jnp.sum(count_ref[...], axis=1, keepdims=True)
    half = tiles // 2
    used, total, square = [], [], []
    for h in range(2):
        pairs = [
            (
                counts[d : d + 1, :] + counts[d ^ core : (d ^ core) + 1, :],
                stats_ref[d * tiles : d * tiles + half, :],
                stats_ref[d * tiles + half : (d + 1) * tiles, :],
            )
            for d in range(n)
            if (d // core) % 2 == h
        ]
        for held, v in zip((used, total, square), combine(pairs)):
            held.append(v)
    used = jnp.max(used[0])
    mean, square = jnp.concatenate(total) / used, jnp.concatenate(square)
    rstd = lax.rsqrt(square / used + 1e-05)
    for j in range(tiles):
        coef_ref[0:1, j * LANES : (j + 1) * LANES] = mean[j : j + 1, :]
        coef_ref[1:2, j * LANES : (j + 1) * LANES] = rstd[j : j + 1, :]
    coef_ref[2:3, :] = jnp.full((1, width), used, F32)
    coef_ref[3:4, :] = coef_ref[1:2, :] * norm_ref[0:1, :]
    bags = rows // SLOTS_BAG
    group = 8

    def fold(v):
        return (v[:group] + v[group : 2 * group]) + (v[2 * group : 3 * group] + v[3 * group :])

    def unfold(ref, j):
        total = ref[j, pl.ds(0, bags, stride=group), :]
        for i in range(1, group):
            total = total + ref[j, pl.ds(i, bags, stride=group), :]
        return total

    for j in range(tiles):
        cols = slice(j * LANES, (j + 1) * LANES)
        centre, scale, bias = coef_ref[0:1, cols], coef_ref[3:4, cols], norm_ref[1:2, cols]
        for b in range(bags):
            at = slice(b * SLOTS_BAG, (b + 1) * SLOTS_BAG)
            to = slice(b * group, (b + 1) * group)
            apart = pre_ref[at, cols] - centre
            y = scale * apart + bias
            capped = jnp.minimum(y, 20.0)
            e = jnp.exp(capped)
            top = e * (e + 2.0)
            below = top + 2.0
            inv = 1.0 / below
            gate = top * inv
            low_ref[at, :] = (y * gate).astype(BF)
            part = e * inv
            slope = gate + (4.0 * capped) * (part * (inv + part))
            slope_ref[at, cols] = slope
            slope = slope * live_ref[at, :]
            ones_ref[j, to, :] = fold(slope)
            twos_ref[j, to, :] = fold(slope * apart)
        act_ref[:, cols] = dot(pick_ref[...], low_ref[...])
        one_ref[:, cols] = unfold(ones_ref, j)
        two_ref[:, cols] = unfold(twos_ref, j) * coef_ref[1:2, cols]
    second = w_out_ref[...].astype(BF).astype(F32)
    bags = hdot(act_ref[...], second, 1, 1)
    pairs = bags.shape[0] // 2
    split = jnp.concatenate([hdot(pick(pairs, 0), bags), hdot(pick(pairs, 1), bags)], axis=0)
    bags_ref[...] = split
    eighth = pairs // 2
    packed = jnp.concatenate([split[i * eighth : (i + 1) * eighth] for i in range(4)], axis=1)
    for d in range(n):
        pay_ref[d * eighth : (d + 1) * eighth, :] = packed


def pick(pairs, which):
    r = lax.broadcasted_iota(jnp.int32, (pairs, 2 * pairs), 0)
    c = lax.broadcasted_iota(jnp.int32, (pairs, 2 * pairs), 1)
    return (c == 2 * r + which).astype(F32)


def spread(pairs, which):
    r = lax.broadcasted_iota(jnp.int32, (2 * pairs, pairs), 0)
    c = lax.broadcasted_iota(jnp.int32, (2 * pairs, pairs), 1)
    return (r == 2 * c + which).astype(F32)


def three(v):
    a = v.astype(BF)
    v = v - a.astype(F32)
    b = v.astype(BF)
    v = v - b.astype(F32)
    return a, b, v.astype(BF)


def loss_kernel(
    me_ref, all_ref, mask_ref, towers_ref, w_out_ref, act_ref, one_ref, two_ref,
    dact_ref, keep_ref, send_ref, d_towers_ref, loss_ref, total_ref,
    score_ref, user_ref, item_ref, halves_ref, *, n, core,
):
    me = me_ref[0]
    embed = towers_ref.shape[1]
    total_rows = mask_ref.shape[0]
    eighth = all_ref.shape[0] // n

    def full(i):
        a = all_ref[:, 2 * i * embed : (2 * i + 1) * embed].reshape(n, eighth, embed)
        b = all_ref[:, (2 * i + 1) * embed : (2 * i + 2) * embed].reshape(n, eighth, embed)
        return jnp.stack([a, b], axis=1).reshape(total_rows, embed)

    bags_user, bags_item = full(0), full(1)
    user = hdot(bags_user, towers_ref[0]).astype(BF)
    item = hdot(bags_item, towers_ref[1]).astype(BF)
    root = math.sqrt(embed)
    score_ref[...] = dot(user, item, 1, 1) / root
    negatives = jnp.sum(mask_ref[...].astype(F32))
    count = negatives / total_rows
    step = 32

    def rows(i, carry):
        at = slice(i * step, (i + 1) * step)
        logits = score_ref[at, :]
        r = lax.broadcasted_iota(jnp.int32, logits.shape, 0) + i * step
        own = r == lax.broadcasted_iota(jnp.int32, logits.shape, 1)
        keep = own | (mask_ref[at, :].astype(F32) == 1.0)
        top = jnp.max(jnp.where(keep, logits, -jnp.inf), axis=1, keepdims=True)
        weights = jnp.where(keep, jnp.exp(logits - top), 0.0)
        total = jnp.sum(weights, axis=1, keepdims=True)
        hit = jnp.sum(jnp.where(own, logits, 0.0), axis=1, keepdims=True)
        score_ref[at, :] = (weights / total - own.astype(F32)) / count / root
        return carry + (top + jnp.log(total) - hit)

    ce = jnp.zeros((step, 1), F32)
    for i in range(total_rows // step):
        ce = rows(i, ce)
    loss_ref[0, 0] = jnp.sum(ce)
    total_ref[0, 0] = count
    parts = three(score_ref[...])
    d_user = sum(dot(p, item) for p in parts)
    d_item = sum(dot(user, p, 0, 0) for p in parts).T
    user_ref[...] = d_user
    item_ref[...] = d_item
    d_towers_ref[0] = hdot(bags_user, d_user, 0, 0)
    d_towers_ref[1] = hdot(bags_item, d_item, 0, 0)
    mine = pl.ds(pl.multiple_of(me * PAIR, PAIR), PAIR)
    back_user = hdot(user_ref[mine, :], towers_ref[0], 1, 1).astype(BF).astype(F32)
    back_item = hdot(item_ref[mine, :], towers_ref[1], 1, 1).astype(BF).astype(F32)
    d_emb = dot(spread(PAIR, 0), back_user) + dot(spread(PAIR, 1), back_item)
    d_act = dot(d_emb.astype(BF), w_out_ref[...].astype(BF))
    dact_ref[...] = d_act
    d_bias = jnp.sum(d_act * one_ref[...], axis=0, keepdims=True)
    d_gain = jnp.sum(d_act * two_ref[...], axis=0, keepdims=True)
    d_low = d_emb.T.astype(BF)
    second = sum(dot(d_low, p) for p in three(act_ref[...]))
    width = act_ref.shape[1]
    tiles = width // LANES
    half = tiles // 2
    for j in range(tiles):
        cols = slice(j * LANES, (j + 1) * LANES)
        h, t = j // half, j % half
        halves_ref[h, t : t + 1, :] = d_bias[:, cols]
        halves_ref[h, half + t : half + t + 1, :] = d_gain[:, cols]
        halves_ref[h, pl.ds(tiles + t, embed, stride=half), :] = second[:, cols]
    odd = (me // core) % 2
    keep_ref[...] = jnp.where(odd == 1, halves_ref[1], halves_ref[0])
    send_ref[...] = jnp.where(odd == 1, halves_ref[0], halves_ref[1])


def share_kernel(keep_ref, got_ref, pay_ref, *, n, tiles):
    total = keep_ref[...] + got_ref[...]
    sums, rows = total[:tiles].astype(BF), (total.shape[0] - tiles) // n
    high = total[tiles:].astype(BF).astype(F32)
    low = total[tiles:] - high
    held = tiles + 2 * rows
    for d in range(n):
        at = slice(d * rows, (d + 1) * rows)
        part = jnp.concatenate([sums.astype(F32), high[at], low[at]], axis=0)
        pay_ref[d * held : (d + 1) * held, :] = part.astype(BF)


def loss_spread(plan, bags, neg_mask, towers, w_out, act, one, two):
    embed = towers.shape[1]
    rows = neg_mask.shape[0]
    bags_user, bags_item = bags[:rows], bags[rows:]
    user = hdot(bags_user, towers[0]).astype(BF)
    item = hdot(bags_item, towers[1]).astype(BF)
    items = lax.all_gather(item, AXES, axis=0, tiled=True)
    root = math.sqrt(embed)
    logits = dot(user, items, 1, 1) / root
    at = lax.axis_index(AXES) * rows + lax.broadcasted_iota(jnp.int32, logits.shape, 0)
    own = lax.broadcasted_iota(jnp.int32, logits.shape, 1) == at
    keep = own | (neg_mask == 1)
    top = jnp.max(jnp.where(keep, logits, -jnp.inf), axis=1, keepdims=True)
    weights = jnp.where(keep, jnp.exp(logits - top), 0.0)
    total = jnp.sum(weights, axis=1, keepdims=True)
    ce = top + jnp.log(total) - jnp.sum(jnp.where(own, logits, 0.0), axis=1, keepdims=True)
    count = lax.psum(jnp.sum(neg_mask.astype(F32)), AXES) / items.shape[0]
    scores = (weights / total - own.astype(F32)) / count / root
    d_user = hdot(scores, items.astype(F32))
    d_item = lax.psum_scatter(
        hdot(scores, user.astype(F32), 0, 0), AXES, scatter_dimension=0, tiled=True
    )
    d_towers = jnp.stack([hdot(bags_user, d_user, 0, 0), hdot(bags_item, d_item, 0, 0)])
    back = jnp.stack([hdot(d_user, towers[0], 1, 1), hdot(d_item, towers[1], 1, 1)], axis=1)
    d_emb = back.reshape(2 * rows, embed).astype(BF)
    d_act = dot(d_emb, w_out.astype(BF))
    d_second = hdot(d_emb.astype(F32), act, 0, 0)
    sums = jnp.stack([jnp.sum(d_act * one, axis=0), jnp.sum(d_act * two, axis=0)])
    sums, d_second, d_towers, loss = lax.psum((sums, d_second, d_towers, jnp.sum(ce)), AXES)
    return d_act, sums.reshape(-1, LANES), d_second, d_towers, loss, count


def block_halves(me, owners_ref, g_ref, outs, masks, local):
    width = g_ref.shape[2]
    bsize = LANES // 2
    half, quarter = bsize // 2, bsize // 4
    side = width // bsize
    lane_half = lax.broadcasted_iota(jnp.int32, (quarter, LANES), 1) // bsize
    for i, m in enumerate(masks):
        for b in range(local):
            r, c, odd = place(owners_ref[(me ^ m) * local + b], side)
            base = pl.multiple_of(r * half, half)
            cols = pl.ds(pl.multiple_of(c * LANES, LANES), LANES)
            keep = lane_half == odd
            to = (i * local + b) * quarter
            for h, out in enumerate(outs):
                tile = g_ref[h, pl.ds(base, half), cols].astype(out.dtype)
                out[to : to + quarter, :] = jnp.where(keep, tile[:quarter], swap_halves(tile[quarter:]))


def grad_kernel(
    me_ref, owners_ref, sums_ref, coef_ref, norm_ref, dact_ref, slope_ref, pre_ref, live_ref, xt_ref,
    top_ref, low_ref, chunk_ref, d_norm_ref, g_ref, d_pre_ref, row_ref,
    *, parts, order, local, core,
):
    rows, width = pre_ref.shape
    tiles = width // LANES
    held = sums_ref.shape[0] // parts
    half = tiles // 2
    if parts > 1:
        sides = []
        for h in range(2):
            side = jnp.zeros((held, LANES), F32)
            for d in range(parts):
                if (d // core) % 2 == h:
                    side = side + sums_ref[d * held : (d + 1) * held, :].astype(F32)
            sides.append(side)
        total = jnp.concatenate([s[i * half : (i + 1) * half] for i in range(2) for s in sides], axis=0)
        share = (held - tiles) // 2
        sides = [s[tiles : tiles + share] + s[tiles + share :] for s in sides]
        chunk_ref[...] = jnp.concatenate(
            [s[i * half : (i + 1) * half] for i in range(share // half) for s in sides], axis=0
        )
    else:
        total = sums_ref[...]
        chunk_ref[...] = jnp.zeros(chunk_ref.shape, F32)
    d_norm_ref[0:tiles, :] = total[tiles : 2 * tiles]
    d_norm_ref[tiles : 2 * tiles, :] = total[:tiles]
    for j in range(tiles):
        cols = slice(j * LANES, (j + 1) * LANES)
        row_ref[0:1, cols] = total[j : j + 1]
        row_ref[1:2, cols] = total[tiles + j : tiles + j + 1]
    scale = norm_ref[0:1, :] * coef_ref[1:2, :]
    flat = scale * row_ref[0:1, :] / coef_ref[2:3, :]
    tilt = scale * row_ref[1:2, :] / coef_ref[2:3, :] * coef_ref[1:2, :]
    row_ref[2:3, :] = scale
    row_ref[3:4, :] = flat
    row_ref[4:5, :] = tilt
    block = 2 * LANES
    for j in range(width // block):
        for i in range(2):
            cols = slice(j * block + i * LANES, j * block + (i + 1) * LANES)
            for b in range(rows // SLOTS_BAG):
                at = slice(b * SLOTS_BAG, (b + 1) * SLOTS_BAG)
                lead = dact_ref[b : b + 1, cols] * row_ref[2:3, cols]
                apart = (pre_ref[at, cols] - coef_ref[0:1, cols]) * row_ref[4:5, cols]
                d_pre = slope_ref[at, cols] * lead - row_ref[3:4, cols] - apart
                d_pre_ref[at, cols] = (live_ref[at, :] * d_pre).astype(BF)
        cols = slice(j * block, (j + 1) * block)
        g_ref[:, :, cols] = dot(xt_ref[...], d_pre_ref[:, cols]).reshape(2, width // 2, block)
    block_halves(me_ref[0], owners_ref, g_ref, (top_ref, low_ref), order, local)


def keep_kernel(me_ref, owners_ref, g_ref, top_ref, low_ref, *, order, local):
    block_halves(me_ref[0], owners_ref, g_ref, (top_ref, low_ref), order, local)


def scatter_sum(plan, kept, sent, rows):
    rest = len(plan.rest)
    shape = (2, 2, rest, rows, LANES)
    one, two = (
        (k + plan.swap(s, plan.core).astype(F32)).reshape(shape) for k, s in zip(kept, sent)
    )
    got_one = plan.swap(one[1].astype(BF), plan.x)
    got_two = plan.swap(two[:, 1].astype(BF), plan.y)
    one = one[0] + got_one.astype(F32)
    two = two[:, 0] + got_two.astype(F32)
    got_one = plan.swap(one[1].astype(BF), plan.y)
    got_two = plan.swap(two[1].astype(BF), plan.x)
    one = one[0] + got_one.astype(F32)
    two = two[0] + got_two.astype(F32)
    if rest <= 4:
        both = jnp.concatenate([one[1:], two[1:]], axis=1).astype(BF)
        return one, two, [plan.swap(both[k], m) for k, m in enumerate(plan.rest[1:])]
    both = jnp.concatenate([one, two], axis=1)
    for b in reversed(plan.bits):
        both = both.reshape(2, -1, 2 * rows, LANES)
        both = both[0] + plan.swap(both[1].astype(BF), b).astype(F32)
    return both[:, :rows], both[:, rows:], []


def norm_kernel(*refs, n):
    one_ref, two_ref, chunk_ref = refs[:3]
    got = refs[3:-2]
    g_ref, pay_ref = refs[-2:]
    total = jnp.concatenate([one_ref[0], two_ref[0]], axis=0)
    for g in got:
        total = total + g[...].astype(F32)
    g_ref[...] = total
    chunk = chunk_ref[...]
    squares = jnp.sum(total * total, keepdims=True) + jnp.sum(chunk * chunk, keepdims=True)
    high = chunk.astype(BF)
    low = chunk - high.astype(F32)
    for i, v in enumerate(three(squares)):
        low = jnp.where(spare(chunk.shape, i), v.astype(F32), low)
    packed = jnp.concatenate([high, low.astype(BF)], axis=0)
    rows = packed.shape[0]
    for d in range(n):
        pay_ref[d * rows : (d + 1) * rows, :] = packed


def spare(shape, i):
    row = lax.broadcasted_iota(jnp.int32, shape, 0)
    lane = lax.broadcasted_iota(jnp.int32, shape, 1)
    return (row == shape[0] - 1) & (lane == LANES - 3 + i)


def adamw(grad, weight, first, second):
    first = BETA_ONE * first + (1 - BETA_ONE) * grad
    second = BETA_TWO * second + (1 - BETA_TWO) * grad * grad
    step = (
        first / (1 - BETA_ONE**STEP) / (jnp.sqrt(second / (1 - BETA_TWO**STEP)) + EPSILON)
    )
    return weight - RATE * (step + DECAY * weight), first, second


def eliminate(gram_ref, power_ref):
    count, size, lanes = gram_ref.shape
    group = 8
    lane = lax.broadcasted_iota(jnp.int32, (count * group, lanes), 1)
    left = lax.broadcasted_iota(jnp.int32, (1, lanes), 1) < size
    for at in range(0, size, group):
        rest = at + group
        gram, power = gram_ref[:, at:rest, :], power_ref[:, at:rest, :]
        flat = gram.reshape(count * group, lanes)
        cols = [
            jnp.take_along_axis(flat, (lane // size) * size + at + i, axis=1).reshape(gram.shape)
            for i in range(group)
        ]
        for i in range(group):
            inv = lax.rsqrt(cols[i][:, i : i + 1, :])
            row, power_row = gram[:, i : i + 1, :] * inv, power[:, i : i + 1, :] * inv
            gram_ref[:, at + i : at + i + 1, :] = row
            power_ref[:, at + i : at + i + 1, :] = power_row
            f = cols[i] * inv
            gram, power = gram - f * row, power - f * power_row
            for j in range(i + 1, group):
                cols[j] = cols[j] - f * f[:, j : j + 1, :]
        if rest == size:
            return
        a, b, c = (v.astype(F32) for v in three(gram_ref[:, at:rest, :]))
        d, e, f = (v.astype(F32) for v in three(power_ref[:, at:rest, :]))
        lhs = jnp.concatenate([a, a, b, b, a, c], axis=1).astype(BF)
        rhs = jnp.concatenate([a, b, a, b, c, a], axis=1)
        rhs = jnp.concatenate([rhs, jnp.concatenate([d, e, d, e, f, d], axis=1)], axis=2).astype(BF)
        turned = [lhs[m].T for m in range(count)]
        for m in range(count):
            one = dot(turned[m][rest:size], rhs[m])
            two = dot(turned[m][size + rest :], rhs[m])
            gram_ref[m, rest:, :] = gram_ref[m, rest:, :] - jnp.where(left, one[:, :lanes], two[:, :lanes])
            power_ref[m, rest:, :] = power_ref[m, rest:, :] - jnp.where(left, one[:, lanes:], two[:, lanes:])


def pair(a, b):
    return jnp.concatenate([a, b], axis=1)


def prepare_kernel(
    w_hbm, left_hbm, right_hbm, bl_hbm, br_hbm, first_hbm, second_hbm, ema_hbm,
    moments_ref, stats_ref, bases_ref, weights_ref, turned_ref, powers_ref,
    w_ref, left_ref, right_ref, bl_ref, br_ref, first_ref, second_ref, ema_ref, sems,
):
    fetch(
        (w_hbm, left_hbm, right_hbm, bl_hbm, br_hbm, first_hbm, second_hbm, ema_hbm),
        (w_ref, left_ref, right_ref, bl_ref, br_ref, first_ref, second_ref, ema_ref),
        sems,
    )
    each = range(w_ref.shape[0])
    for b in each:
        moments_ref[b] = pair(first_ref[b], second_ref[b])
        stats_ref[b] = pair(left_ref[b], right_ref[b])
        bases_ref[b] = pair(bl_ref[b], br_ref[b])
        weights_ref[b] = pair(w_ref[b], ema_ref[b])
    half = [hdot(bl_ref[b], first_ref[b], 0, 0) for b in each]
    for b in each:
        turned_ref[b] = hdot(half[b], br_ref[b])
    lefts = [hdot(bl_ref[b], left_ref[b], 0, 0) for b in each]
    rights = [hdot(br_ref[b], right_ref[b], 0, 0) for b in each]
    for b in each:
        powers_ref[b] = pair(lefts[b], rights[b])


def turn_kernel(
    me_ref, owners_ref, g_ref, bases_ref,
    wo_hbm, mo_hbm, vo_hbm, eo_hbm, wt_hbm, mt_hbm, vt_hbm, wn_hbm, mn_hbm, vn_hbm,
    grad_ref, squares_ref, powers_ref, scale_ref,
    wide_ref, towers_ref, norms_ref, sems,
):
    local, bsize = bases_ref.shape[0], bases_ref.shape[1]
    sources = (wo_hbm, mo_hbm, vo_hbm, eo_hbm, wt_hbm, mt_hbm, vt_hbm, wn_hbm, mn_hbm, vn_hbm)
    targets = [wide_ref.at[i] for i in range(4)]
    targets += [towers_ref.at[i] for i in range(3)] + [norms_ref.at[i] for i in range(3)]
    copies = [pltpu.make_async_copy(a, b, sems.at[i]) for i, (a, b) in enumerate(zip(sources, targets))]
    for c in copies:
        c.start()
    largest = jnp.max(jnp.abs(g_ref[...]), keepdims=True)
    largest = jnp.where(largest > 0.0, largest, 1.0)
    scale_ref[...] = jnp.broadcast_to(largest, scale_ref.shape)
    half = bsize // 2
    each = range(local)
    grads = []
    for b in each:
        odd = owners_ref[me_ref[0] * local + b] % 2
        quarters = []
        for i in range(2):
            at = (i * local + b) * half // 2
            tile = g_ref[at : at + half // 2, :]
            tile = jnp.where(odd == 1, swap_halves(tile), tile)
            quarters += [tile[:, :bsize], tile[:, bsize:]]
        grads.append(jnp.concatenate(quarters, axis=0) / largest)
    bl = [bases_ref[b, :, :bsize] for b in each]
    br = [bases_ref[b, :, bsize:] for b in each]
    by_left = [hdot(bl[b], grads[b], 0, 0) for b in each]
    by_right = [hdot(grads[b], br[b]) for b in each]
    outer = [hdot(grads[b], grads[b], 1, 1) for b in each]
    inner = [hdot(grads[b], grads[b], 0, 0) for b in each]
    for b in each:
        squares_ref[b] = pair(outer[b], inner[b])
    for b in each:
        grad_ref[b] = pair(grads[b], hdot(by_left[b], br[b]))
    lefts = [hdot(by_left[b], grads[b], 1, 1) for b in each]
    rights = [hdot(by_right[b], grads[b], 0, 0) for b in each]
    for b in each:
        powers_ref[b] = pair(lefts[b], rights[b])
    for c in copies:
        c.wait()


def step_kernel(
    got_ref, d_norm_ref, d_towers_ref,
    grad_ref, squares_ref, powers_ref, scale_ref,
    old_ref, towers_ref, norms_ref,
    moments_ref, stats_ref, bases_ref, weights_ref, turned_first_ref, powers_old_ref,
    *refs, n,
):
    (
        w_out, low_out, left_out, right_out, bl_out, br_out, first_out, second_out, ema_out,
        wo_out, mo_out, vo_out, eo_out, wt_out, mt_out, vt_out, wn_out, mn_out, vn_out, gn_out,
        gram_ref, power_ref, wide_ref, dn_ref, flat_ref,
    ) = refs
    local, bsize = bases_ref.shape[0], bases_ref.shape[1]
    embed, width = old_ref.shape[1:]
    tiles = width // LANES
    held = got_ref.shape[0] // n
    if n > 1:
        chunk = held // 2
        used = functools.reduce(jnp.logical_or, [spare((chunk, LANES), i) for i in range(3)])
        squares = jnp.zeros((chunk, LANES), F32)
        for d in range(n):
            part = got_ref[d * held : (d + 1) * held, :].astype(F32)
            squares = squares + jnp.where(used, part[chunk:], 0.0)
            flat_ref[d * chunk : (d + 1) * chunk, :] = part[:chunk] + jnp.where(used, 0.0, part[chunk:])
        squares = jnp.sum(squares)
        for j in range(tiles):
            wide_ref[:, j * LANES : (j + 1) * LANES] = flat_ref[pl.ds(j, embed, stride=tiles), :]
    else:
        squares = jnp.max(got_ref[0:1, :LANES])
        wide_ref[...] = got_ref[8 : 8 + embed, :]
    squares = squares + jnp.sum(d_towers_ref[...] * d_towers_ref[...])
    squares = squares + jnp.sum(d_norm_ref[...] * d_norm_ref[...])
    norm = jnp.sqrt(jnp.full((1, LANES), squares, F32))
    gn_out[0, 0] = jnp.max(norm)
    factor = (CLIP / jnp.maximum(norm, CLIP))[:, :1]
    each = range(local)
    lead = factor * scale_ref[0:1, 0:1]
    twice = (1 - BETA_TWO) * lead * lead
    lefts, rights = [], []
    for b in each:
        powers = BETA_TWO * powers_old_ref[b] + twice * powers_ref[b]
        power_ref[b] = powers
        lefts.append(powers[:, :bsize])
        rights.append(powers[:, bsize:])
    for b in each:
        gram_ref[b] = pair(hdot(lefts[b], lefts[b], 1, 1), hdot(rights[b], rights[b], 1, 1))
    ratios = []
    for b in each:
        stats = BETA_TWO * stats_ref[b] + twice * squares_ref[b]
        left_out[b], right_out[b] = stats[:, :bsize], stats[:, bsize:]
        first_out[b] = BETA_ONE * moments_ref[b, :, :bsize] + (1 - BETA_ONE) * lead * grad_ref[b, :, :bsize]
        turned = grad_ref[b, :, bsize:]
        second = BETA_TWO * moments_ref[b, :, bsize:] + twice * turned * turned
        second_out[b] = second
        moved = BETA_ONE * turned_first_ref[b] + (1 - BETA_ONE) * lead * turned
        moved = moved / (1 - BETA_ONE**STEP)
        ratios.append(moved / (jnp.sqrt(second / (1 - BETA_TWO**STEP)) + EPSILON))
    half = [hdot(bases_ref[b, :, :bsize], ratios[b]) for b in each]
    updates = [hdot(half[b], bases_ref[b, :, bsize:], 1, 1) for b in each]
    for b in each:
        old = weights_ref[b, :, :bsize]
        new = old - RATE * (updates[b] + DECAY * old)
        w_out[b] = new
        low_out[b] = new.astype(BF)
        ema_out[b] = AVG_KEEP * weights_ref[b, :, bsize:] + AVG_TAKE * new
    new, m, v = adamw(wide_ref[...] * factor, old_ref[0], old_ref[1], old_ref[2])
    wo_out[...], mo_out[...], vo_out[...] = new, m, v
    eo_out[...] = AVG_KEEP * old_ref[3] + AVG_TAKE * new
    for t in range(2):
        wt_out[t], mt_out[t], vt_out[t] = adamw(
            d_towers_ref[t] * factor, towers_ref[0, t], towers_ref[1, t], towers_ref[2, t]
        )
        for j in range(tiles):
            dn_ref[t : t + 1, j * LANES : (j + 1) * LANES] = d_norm_ref[
                t * tiles + j : t * tiles + j + 1, :
            ]
    wn_out[...], mn_out[...], vn_out[...] = adamw(
        dn_ref[...] * factor, norms_ref[0], norms_ref[1], norms_ref[2]
    )
    eliminate(gram_ref, power_ref)
    for b in each:
        turned = power_ref[b].T
        bl_out[b], br_out[b] = turned[:bsize], turned[bsize:]


def exchange(payload):
    return lax.all_to_all(payload, AXES, 0, 0, tiled=True)


def on_device(
    plan,
    codes, field_offsets, seg_mask, neg_mask, owners,
    w_hidden, stat_left, stat_right, basis_left, basis_right, mom1_hidden, mom2_hidden, ema_hidden,
    w_out, mom1_out, mom2_out, ema_out,
    w_towers, mom1_towers, mom2_towers,
    w_norm, mom1_norm, mom2_norm,
):
    n = plan.n
    local, bsize = w_hidden.shape[0], w_hidden.shape[1]
    width, embed = w_out.shape
    slots = codes.shape[0]
    rows, total_rows = neg_mask.shape
    tiles = width // LANES
    half = bsize // 2
    bags = slots // SLOTS_BAG
    masked = total_rows <= 1024 and n <= embed
    me = lax.axis_index(AXES).astype(jnp.int32)[None]

    chunks = total_rows // LANES if masked else 0
    size = local * half + chunks * PAIR + PAIR
    (payload,) = call(
        functools.partial(pack_kernel, masked=masked),
        [((size, LANES), BF)],
        [w_hidden, neg_mask, seg_mask.reshape(-1, LANES)],
        hbm=3,
        scratch=[
            pltpu.VMEM(w_hidden.shape, F32),
            pltpu.VMEM(neg_mask.shape, jnp.int32),
            pltpu.VMEM((slots // LANES, LANES), jnp.int32),
            pltpu.SemaphoreType.DMA((3,)),
        ],
        name="pack",
    )
    cut = max(half, size // 2 // half * half)
    cut = min(cut, local * half)
    blocks = (local, bsize, bsize)
    twin = (local, bsize, 2 * bsize)
    state = [
        w_hidden, stat_left, stat_right, basis_left, basis_right, mom1_hidden, mom2_hidden, ema_hidden
    ]
    prepared = call(
        prepare_kernel,
        [(twin, F32)] * 4 + [(blocks, F32), (twin, F32)],
        state,
        hbm=len(state),
        scratch=[pltpu.VMEM(blocks, F32)] * len(state) + [pltpu.SemaphoreType.DMA((len(state),))],
        limit=12,
        name="prepare",
        cost=10_000_000,
    )
    turned_out, turned_mom1, turned_mom2, turned_ema = (
        a.T for a in (w_out, mom1_out, mom2_out, ema_out)
    )
    early = hash_inputs(codes, field_offsets)
    live = jnp.broadcast_to(seg_mask.astype(F32)[:, None], (slots, LANES))
    slot_bag = lax.broadcasted_iota(jnp.int32, (bags, slots), 1) // SLOTS_BAG
    in_bag = slot_bag == lax.broadcasted_iota(jnp.int32, (bags, slots), 0)
    chosen = jnp.where(in_bag, seg_mask.astype(F32)[None], 0.0).astype(BF)
    late = (*prepared, live, chosen)
    zero = (me[0] >> 16).astype(BF)

    def held_by(pieces):
        return [([m | base for m in plan.rest], row) for _, base, row in pieces]

    def place_blocks(pieces):
        (planes,) = call(
            functools.partial(assemble_kernel, holds=held_by(pieces), local=local),
            [((2, width, width), BF)],
            [me, owners] + [a for a, _, _ in pieces],
            smem=2,
            limit=8,
            name="assemble",
            cost=10_000_000,
        )
        return planes

    pieces, done, planes, (x, x_turned), (*prepared, live, chosen) = gather_pieces(
        plan, payload, cut, zero, early, late, place_blocks
    )
    mask_shape = (total_rows, total_rows) if masked else (PAIR, LANES)
    holds = held_by(pieces)
    arrays = [a for a, _, _ in pieces]
    pre, kept, sent, counts, mask, _ = call(
        functools.partial(
            pre_kernel, holds=holds, done=done, local=local, masked=masked, core=plan.core
        ),
        [
            ((slots, width), F32),
            ((tiles, LANES), F32),
            ((tiles, LANES), F32),
            ((n, LANES), F32),
            (mask_shape, BF),
            ((2, width, width), BF),
        ],
        [me, owners, planes] + arrays + [x, live],
        smem=2,
        scratch=[pltpu.VMEM((2 * tiles, LANES), F32)],
        aliases={2: 5},
        limit=16,
        name="pre",
    )
    (stats,) = call(
        functools.partial(merge_kernel, core=plan.core),
        [((n * tiles, LANES), F32)],
        [me, counts, kept, plan.swap(sent, plan.core)],
        smem=1,
        limit=4,
        name="merge",
    )
    stats = exchange(stats)
    slope, act, one, two, coef, bag_sums, pay = call(
        functools.partial(act_kernel, core=plan.core),
        [
            ((slots, width), F32),
            ((bags, width), F32),
            ((bags, width), F32),
            ((bags, width), F32),
            ((8, width), F32),
            ((bags, embed), F32),
            ((n * 8, LANES), F32),
        ],
        [stats, counts, w_norm, pre, live, chosen, turned_out],
        scratch=[
            pltpu.VMEM((slots, LANES), BF),
            pltpu.VMEM((tiles, bags * 8, LANES), F32),
            pltpu.VMEM((tiles, bags * 8, LANES), F32),
        ],
        limit=12,
        name="act",
    )
    if masked:
        chunk = embed * tiles // n
        everyone = exchange(pay)
        shared = (tiles + embed * tiles // 2, LANES)
        d_act, kept, sent, d_towers, loss_sum, count = call(
            functools.partial(loss_kernel, n=n, core=plan.core),
            [
                ((bags, width), F32),
                (shared, F32),
                (shared, F32),
                ((2, embed, embed), F32),
                ((1, 1), F32),
                ((1, 1), F32),
            ],
            [me, everyone, mask, w_towers, turned_out, act, one, two],
            smem=1,
            smem_outs=2,
            scratch=[
                pltpu.VMEM((total_rows, total_rows), F32),
                pltpu.VMEM((total_rows, embed), F32),
                pltpu.VMEM((total_rows, embed), F32),
                pltpu.VMEM((2, *shared), F32),
            ],
            name="loss",
        )
        (pay,) = call(
            functools.partial(share_kernel, n=n, tiles=tiles),
            [((n * (tiles + chunk), LANES), BF)],
            [kept, plan.swap(sent, plan.core)],
            limit=4,
            name="share",
        )
        sums, parts = exchange(pay), n
        loss_sum, count = loss_sum[0, 0], count[0, 0]
    else:
        d_act, sums, d_second, d_towers, loss_sum, count = loss_spread(
            plan, bag_sums, neg_mask, w_towers, turned_out, act, one, two
        )
        parts = 1
        chunk = 8
    groups = [m for m in (0, plan.y, plan.x, plan.x | plan.y)]
    keep_order = [g | r for g in groups for r in plan.rest]
    order = (keep_order, [m | plan.core for m in keep_order])
    packed = (n // 2 * local * half // 2, LANES)
    packed = (n // 2 * local * half // 2, LANES)
    *sent, second_chunk, d_norm, full = call(
        functools.partial(grad_kernel, parts=parts, order=order[1], local=local, core=plan.core),
        [
            (packed, BF),
            (packed, BF),
            ((chunk, LANES), F32),
            ((2 * tiles, LANES), F32),
            ((2, width // 2, width), F32),
        ],
        [me, owners, sums, coef, w_norm, d_act, slope, pre, live, x_turned],
        smem=2,
        scratch=[pltpu.VMEM((slots, width), BF), pltpu.VMEM((8, width), F32)],
        limit=16,
        name="grad",
    )
    kept = call(
        functools.partial(keep_kernel, order=order[0], local=local),
        [(packed, F32), (packed, F32)],
        [me, owners, full],
        smem=2,
        limit=8,
        name="keep",
        cost=100_000_000,
    )
    one_sum, two_sum, others = scatter_sum(plan, kept, sent, local * half // 2)
    copies = n if masked else 1
    grad, pay = call(
        functools.partial(norm_kernel, n=copies),
        [((local * half, LANES), F32), ((copies * 2 * chunk, LANES), BF)],
        [one_sum, two_sum, second_chunk, *others],
        name="norm",
    )
    if masked:
        got = exchange(pay)
    else:
        squares = lax.psum(jnp.sum(grad * grad), AXES) + jnp.sum(d_second * d_second)
        got = jnp.concatenate([jnp.full((8, width), squares, F32), d_second], axis=0)
    moments, stats, bases, weights, turned_first, powers_old = prepared
    plain = [
        turned_out, turned_mom1, turned_mom2, turned_ema,
        w_towers, mom1_towers, mom2_towers,
        w_norm, mom1_norm, mom2_norm,
    ]
    turned = call(
        turn_kernel,
        [(twin, F32)] * 3
        + [((8, LANES), F32), ((4, embed, width), F32), ((3, 2, embed, embed), F32), ((3, 2, width), F32)],
        [me, owners, grad, bases, *plain],
        smem=2,
        hbm=len(plain),
        scratch=[pltpu.SemaphoreType.DMA((len(plain),))],
        name="turn",
        cost=10_000_000,
    )
    outs = [(blocks, F32), (blocks, BF)] + [(blocks, F32)] * 7
    outs += [((embed, width), F32)] * 4 + [((2, embed, embed), F32)] * 3 + [((2, width), F32)] * 3
    new = call(
        functools.partial(step_kernel, n=n if masked else 1),
        outs + [((1, 1), F32)],
        [
            got, d_norm, d_towers, *turned,
            moments, stats, bases, weights, turned_first, powers_old,
        ],
        smem_outs=1,
        scratch=[
            pltpu.VMEM(twin, F32),
            pltpu.VMEM(twin, F32),
            pltpu.VMEM((embed, width), F32),
            pltpu.VMEM((2, width), F32),
            pltpu.VMEM((embed * tiles, LANES), F32),
        ],
        name="step",
    )
    return (loss_sum, count, new[-1][0, 0], *new[:9], *(a.T for a in new[9:13]), *new[13:-1])


def solution(mesh):
    split = P(("gx", "gy"))
    plan = Plan(mesh.shape["gx"], mesh.shape["gy"])
    return jax.shard_map(
        functools.partial(on_device, plan),
        mesh=mesh,
        in_specs=(split, P(), split, split, P()) + (split,) * 8 + (P(),) * 10,
        out_specs=(P(),) * 3 + (split,) * 9 + (P(),) * 10,
        check_vma=False,
    )
```

```python
import functools
import math

import jax
import jax.numpy as jnp
from jax import lax
from jax.experimental import pallas as pl
from jax.experimental.pallas import tpu as pltpu
from jax.sharding import PartitionSpec as P

FIELDS = 4
BAG = 8
HASH_RANGE = 4096
STEP = 10
BETA_ONE = 0.9
BETA_TWO = 0.95
EPSILON = 1e-08
RATE = 0.03
DECAY = 0.01
CLIP = 0.01
AVG_KEEP = 0.8
AVG_TAKE = 0.2

F32 = jnp.float32
BF = jnp.bfloat16
HIGH = lax.Precision.HIGHEST
AXES = ("gx", "gy")
LANES = 128
SLOTS_BAG = FIELDS * BAG
PAIR = 16
MIB = 1 << 20


def dot(a, b, ca=1, cb=0, precision=None):
    return lax.dot_general(
        a, b, (((ca,), (cb,)), ((), ())), precision=precision, preferred_element_type=F32
    )


hdot = functools.partial(dot, precision=HIGH)


def spec(space=pltpu.VMEM):
    return pl.BlockSpec(memory_space=space)


def in_hbm(a):
    return pltpu.with_memory_space_constraint(a, pltpu.HBM)


def call(kernel, outs, args, smem=0, hbm=0, smem_outs=0, aliases=None, scratch=(), limit=16, name=None, cost=None):
    args = list(args)
    specs = [spec(pltpu.SMEM)] * smem + [spec()] * (len(args) - smem - hbm) + [spec(pltpu.HBM)] * hbm
    if hbm:
        args[-hbm:] = [in_hbm(a) for a in args[-hbm:]]
    spaces = [pltpu.VMEM] * (len(outs) - smem_outs) + [pltpu.SMEM] * smem_outs
    estimate = None
    if cost:
        estimate = pl.CostEstimate(flops=cost, bytes_accessed=cost // 100, transcendentals=0)
    return pl.pallas_call(
        kernel,
        out_shape=[jax.ShapeDtypeStruct(s, t) for s, t in outs],
        in_specs=specs,
        out_specs=[spec(space) for space in spaces],
        scratch_shapes=list(scratch),
        compiler_params=pltpu.CompilerParams(vmem_limit_bytes=limit * MIB),
        cost_estimate=estimate,
        input_output_aliases=aliases or {},
        name=name,
    )(*args)


def fetch(sources, targets, sems):
    copies = [pltpu.make_async_copy(a, b, sems.at[i]) for i, (a, b) in enumerate(zip(sources, targets))]
    for c in copies:
        c.start()
    for c in copies:
        c.wait()


def swap_halves(v):
    half = v.shape[1] // 2
    return jnp.concatenate([v[:, half:], v[:, :half]], axis=1)


def place(q, side):
    shift = side.bit_length() - 1
    return q >> shift, (q & (side - 1)) >> 1, q & 1


class Plan:
    def __init__(self, gx, gy):
        self.gx, self.gy, self.n = gx, gy, gx * gy
        self.core = gy
        self.x = 2 * gy
        self.y = 1
        bits = []
        b = 2
        while b < gy:
            bits.append(b)
            b *= 2
        b = 4
        while b < gx:
            bits.append(b * gy)
            b *= 2
        self.bits = bits
        rest = [0]
        for b in bits:
            rest = rest + [m | b for m in rest]
        self.rest = rest

    def swap(self, a, mask):
        mx, my = mask // self.gy, mask % self.gy
        if my == 0:
            return lax.ppermute(a, "gx", [(i, i ^ mx) for i in range(self.gx)])
        if mx == 0:
            return lax.ppermute(a, "gy", [(i, i ^ my) for i in range(self.gy)])
        return lax.ppermute(a, AXES, [(i, i ^ mask) for i in range(self.n)])


def pack_kernel(
    w_hbm, neg_hbm, seg_hbm, out_ref, w_ref, neg_ref, seg_ref, sems, *, masked
):
    fetch((w_hbm, neg_hbm, seg_hbm), (w_ref, neg_ref, seg_ref), sems)
    local, bsize = w_ref.shape[0], w_ref.shape[1]
    half = bsize // 2
    for b in range(local):
        both = jnp.concatenate([w_ref[b, :half, :], w_ref[b, half:, :]], axis=1)
        out_ref[b * half : (b + 1) * half, :] = both.astype(BF)
    at = local * half
    if masked:
        for c in range(neg_ref.shape[1] // LANES):
            part = neg_ref[:, c * LANES : (c + 1) * LANES].astype(F32)
            out_ref[at : at + PAIR, :] = part.astype(BF)
            at += PAIR
    used = jnp.sum(seg_ref[...].astype(F32), axis=0, keepdims=True)
    out_ref[at : at + PAIR, :] = jnp.broadcast_to(used, (PAIR, LANES)).astype(BF)


def gather_pieces(plan, payload, cut, zero, early, late, place_blocks):
    stack = payload[None]
    if len(plan.rest) <= 4:
        stack = jnp.concatenate([stack] + [plan.swap(stack, m) for m in plan.rest[1:]], axis=0)
    else:
        for b in plan.bits:
            stack = jnp.concatenate([stack, plan.swap(stack, b)], axis=0)
    stack, early = lax.optimization_barrier((stack, early))
    by_x = plan.swap(stack, plan.x)
    by_y = plan.swap(stack, plan.y)
    by_x, by_y, late = lax.optimization_barrier((by_x, by_y, late))
    first = plan.swap(by_x[:, :cut] + zero, plan.y)
    second = plan.swap(by_y[:, cut:] + zero, plan.x)
    ready = [(stack, 0, 0), (by_x, plan.x, 0), (by_y, plan.y, 0)]
    ready += swapped(plan, ready)
    planes = place_blocks(ready)
    first, second, planes = lax.optimization_barrier((first, second, planes))
    last = [(first, plan.x | plan.y, 0), (second, plan.x | plan.y, cut)]
    return ready + last + swapped(plan, last), len(ready), planes, early, late


def swapped(plan, pieces):
    return [(plan.swap(a, plan.core), m | plan.core, row) for a, m, row in pieces]


def hash_kernel(codes_hbm, offsets_hbm, x_ref, xt_ref, codes_ref, offsets_ref, sems):
    rows, width = codes_ref.shape
    groups = 2 * FIELDS
    step = 128
    head = pltpu.make_async_copy(offsets_hbm, offsets_ref, sems.at[0])
    head.start()
    parts = []
    for i in range(rows // step):
        at = pl.ds(i * step, step)
        parts.append(pltpu.make_async_copy(codes_hbm.at[at], codes_ref.at[at], sems.at[1 + i]))
        parts[i].start()
    head.wait()
    for i, part in enumerate(parts):
        part.wait()
        at = slice(i * step, (i + 1) * step)
        salted = codes_ref[at, :].reshape(-1, groups, BAG, width) + offsets_ref[...][None, :, None, :]
        salted = (salted & (HASH_RANGE - 1)).reshape(step, width)
        x = (salted.astype(F32) * (2.0 / (HASH_RANGE - 1)) - 1.0).astype(BF)
        x_ref[at, :] = x
        quarter = LANES // 4
        turned = x.T.reshape(-1, 2, quarter, step)
        for h in range(2):
            xt_ref[h * width // 2 : (h + 1) * width // 2, at] = turned[:, h].reshape(-1, step)


def hash_inputs(codes, offsets):
    rows, width = codes.shape
    return call(
        hash_kernel,
        [((rows, width), BF), ((width, rows), BF)],
        [codes, offsets],
        hbm=2,
        scratch=[
            pltpu.VMEM(codes.shape, jnp.int32),
            pltpu.VMEM(offsets.shape, jnp.int32),
            pltpu.SemaphoreType.DMA((1 + rows // 128,)),
        ],
        limit=12,
        name="hash",
        cost=20_000_000,
    )


def assemble(w_ref, me, owners_ref, piece_refs, holds, local):
    width = w_ref.shape[1]
    bsize = LANES // 2
    half = bsize // 2
    side = width // bsize
    for piece, (masks, row0) in zip(piece_refs, holds):
        for k, m in enumerate(masks):
            for b in range(local):
                at = b * half - row0
                if at < 0 or at + half > piece.shape[1]:
                    continue
                r, c, odd = place(owners_ref[(me ^ m) * local + b], side)
                tile = piece[k, at : at + half, :]
                rows = pl.multiple_of(r * bsize, bsize)
                low = pl.multiple_of(r * bsize + half, half)
                cols = pl.ds(pl.multiple_of(c * LANES, LANES), LANES)
                other = swap_halves(tile)
                w_ref[odd, pl.ds(rows, half), cols] = jnp.where(odd == 1, other, tile)
                w_ref[odd, pl.ds(low, half), cols] = jnp.where(odd == 1, tile, other)


def assemble_kernel(me_ref, owners_ref, *refs, holds, local):
    assemble(refs[-1], me_ref[0], owners_ref, refs[:-1], holds, local)


def pre_kernel(*refs, holds, done, local, masked, core):
    me_ref, owners_ref = refs[:2]
    pieces = len(holds)
    piece_refs = refs[3 : 3 + pieces]
    x_ref, live_ref = refs[3 + pieces : 5 + pieces]
    pre_ref, keep_ref, send_ref, count_ref, mask_ref, w_ref, row_ref = refs[5 + pieces :]
    width = x_ref.shape[1]
    bsize = LANES // 2
    half = bsize // 2
    tiles = width // LANES
    me = me_ref[0]
    chunks = mask_ref.shape[1] // LANES if masked else 0
    assemble(w_ref, me, owners_ref, piece_refs[done:], holds[done:], local)
    for piece, (masks, row0) in zip(piece_refs, holds):
        held = piece.shape[1]
        for k, m in enumerate(masks):
            d = me ^ m
            for c in range(chunks):
                at = local * half + c * PAIR - row0
                if at < 0 or at + PAIR > held:
                    continue
                mask_ref[pl.ds(pl.multiple_of(d * PAIR, PAIR), PAIR), c * LANES : (c + 1) * LANES] = (
                    piece[k, at : at + PAIR, :]
                )
            at = local * half + chunks * PAIR - row0
            if 0 <= at and at + PAIR <= held:
                count_ref[pl.ds(d, 1), :] = piece[k, at : at + PAIR, :].astype(F32)[:1]
    live = live_ref[...]
    used = jnp.maximum(jnp.sum(live[:, :1]), 1.0)
    step = 2 * LANES
    left = lax.broadcasted_iota(jnp.int32, (width, step), 1) % LANES < bsize
    for j in range(width // step):
        cols = slice(j * step, (j + 1) * step)
        pre_ref[:, cols] = dot(x_ref[...], jnp.where(left, w_ref[0, :, cols], w_ref[1, :, cols]))
        for i in range(2):
            t = 2 * j + i
            tile = slice(t * LANES, (t + 1) * LANES)
            total = jnp.sum(pre_ref[:, tile] * live, axis=0, keepdims=True)
            apart = pre_ref[:, tile] - total / used
            row_ref[t : t + 1, :] = total
            row_ref[tiles + t : tiles + t + 1, :] = jnp.sum(
                apart * apart * live, axis=0, keepdims=True
            )
    half = tiles // 2
    parts = [
        jnp.concatenate([row_ref[h * half : (h + 1) * half, :], row_ref[tiles + h * half : tiles + (h + 1) * half, :]])
        for h in range(2)
    ]
    odd = (me // core) % 2
    keep_ref[...] = jnp.where(odd == 1, parts[1], parts[0])
    send_ref[...] = jnp.where(odd == 1, parts[0], parts[1])


def combine(pairs):
    used = sum(c for c, _, _ in pairs)
    total = sum(t for _, t, _ in pairs)
    mean = total / jnp.maximum(used, 1.0)
    square = 0.0
    for c, t, q in pairs:
        apart = t / jnp.maximum(c, 1.0) - mean
        square = square + (q + c * apart * apart)
    return used, total, square


def merge_kernel(me_ref, count_ref, keep_ref, got_ref, out_ref, *, core):
    half = keep_ref.shape[0] // 2
    n = count_ref.shape[0]
    counts = [
        jnp.sum(count_ref[pl.ds(d, 1), :], keepdims=True) for d in (me_ref[0], me_ref[0] ^ core)
    ]
    pairs = [(c, ref[:half, :], ref[half:, :]) for c, ref in zip(counts, (keep_ref, got_ref))]
    _, total, square = combine(pairs)
    packed = jnp.concatenate([total, square])
    for d in range(n):
        out_ref[2 * half * d : 2 * half * (d + 1), :] = packed


def act_kernel(
    stats_ref, count_ref, norm_ref, pre_ref, live_ref, pick_ref, w_out_ref,
    slope_ref, act_ref, one_ref, two_ref, coef_ref, bags_ref, pay_ref,
    low_ref, ones_ref, twos_ref,
    *, core,
):
    n = count_ref.shape[0]
    rows, width = pre_ref.shape
    tiles = width // LANES
    counts = jnp.sum(count_ref[...], axis=1, keepdims=True)
    half = tiles // 2
    used, total, square = [], [], []
    for h in range(2):
        pairs = [
            (
                counts[d : d + 1, :] + counts[d ^ core : (d ^ core) + 1, :],
                stats_ref[d * tiles : d * tiles + half, :],
                stats_ref[d * tiles + half : (d + 1) * tiles, :],
            )
            for d in range(n)
            if (d // core) % 2 == h
        ]
        for held, v in zip((used, total, square), combine(pairs)):
            held.append(v)
    used = jnp.max(used[0])
    mean, square = jnp.concatenate(total) / used, jnp.concatenate(square)
    rstd = lax.rsqrt(square / used + 1e-05)
    for j in range(tiles):
        coef_ref[0:1, j * LANES : (j + 1) * LANES] = mean[j : j + 1, :]
        coef_ref[1:2, j * LANES : (j + 1) * LANES] = rstd[j : j + 1, :]
    coef_ref[2:3, :] = jnp.full((1, width), used, F32)
    coef_ref[3:4, :] = coef_ref[1:2, :] * norm_ref[0:1, :]
    bags = rows // SLOTS_BAG
    group = 8

    def fold(v):
        return (v[:group] + v[group : 2 * group]) + (v[2 * group : 3 * group] + v[3 * group :])

    def unfold(ref, j):
        total = ref[j, pl.ds(0, bags, stride=group), :]
        for i in range(1, group):
            total = total + ref[j, pl.ds(i, bags, stride=group), :]
        return total

    for j in range(tiles):
        cols = slice(j * LANES, (j + 1) * LANES)
        centre, scale, bias = coef_ref[0:1, cols], coef_ref[3:4, cols], norm_ref[1:2, cols]
        for b in range(bags):
            at = slice(b * SLOTS_BAG, (b + 1) * SLOTS_BAG)
            to = slice(b * group, (b + 1) * group)
            apart = pre_ref[at, cols] - centre
            y = scale * apart + bias
            capped = jnp.minimum(y, 20.0)
            e = jnp.exp(capped)
            top = e * (e + 2.0)
            below = top + 2.0
            inv = 1.0 / below
            gate = top * inv
            low_ref[at, :] = (y * gate).astype(BF)
            part = e * inv
            slope = gate + (4.0 * capped) * (part * (inv + part))
            slope_ref[at, cols] = slope
            slope = slope * live_ref[at, :]
            ones_ref[j, to, :] = fold(slope)
            twos_ref[j, to, :] = fold(slope * apart)
        act_ref[:, cols] = dot(pick_ref[...], low_ref[...])
        one_ref[:, cols] = unfold(ones_ref, j)
        two_ref[:, cols] = unfold(twos_ref, j) * coef_ref[1:2, cols]
    second = w_out_ref[...].astype(BF).astype(F32)
    bags = hdot(act_ref[...], second, 1, 1)
    pairs = bags.shape[0] // 2
    split = jnp.concatenate([hdot(pick(pairs, 0), bags), hdot(pick(pairs, 1), bags)], axis=0)
    bags_ref[...] = split
    eighth = pairs // 2
    packed = jnp.concatenate([split[i * eighth : (i + 1) * eighth] for i in range(4)], axis=1)
    for d in range(n):
        pay_ref[d * eighth : (d + 1) * eighth, :] = packed


def pick(pairs, which):
    r = lax.broadcasted_iota(jnp.int32, (pairs, 2 * pairs), 0)
    c = lax.broadcasted_iota(jnp.int32, (pairs, 2 * pairs), 1)
    return (c == 2 * r + which).astype(F32)


def spread(pairs, which):
    r = lax.broadcasted_iota(jnp.int32, (2 * pairs, pairs), 0)
    c = lax.broadcasted_iota(jnp.int32, (2 * pairs, pairs), 1)
    return (r == 2 * c + which).astype(F32)


def three(v):
    a = v.astype(BF)
    v = v - a.astype(F32)
    b = v.astype(BF)
    v = v - b.astype(F32)
    return a, b, v.astype(BF)


def loss_kernel(
    me_ref, all_ref, mask_ref, towers_ref, w_out_ref, act_ref, one_ref, two_ref,
    dact_ref, keep_ref, send_ref, d_towers_ref, loss_ref, total_ref,
    score_ref, user_ref, item_ref, halves_ref, *, n, core,
):
    me = me_ref[0]
    embed = towers_ref.shape[1]
    total_rows = mask_ref.shape[0]
    eighth = all_ref.shape[0] // n

    def full(i):
        a = all_ref[:, 2 * i * embed : (2 * i + 1) * embed].reshape(n, eighth, embed)
        b = all_ref[:, (2 * i + 1) * embed : (2 * i + 2) * embed].reshape(n, eighth, embed)
        return jnp.stack([a, b], axis=1).reshape(total_rows, embed)

    bags_user, bags_item = full(0), full(1)
    user = hdot(bags_user, towers_ref[0]).astype(BF)
    item = hdot(bags_item, towers_ref[1]).astype(BF)
    root = math.sqrt(embed)
    score_ref[...] = dot(user, item, 1, 1) / root
    negatives = jnp.sum(mask_ref[...].astype(F32))
    count = negatives / total_rows
    step = 32

    def rows(i, carry):
        at = slice(i * step, (i + 1) * step)
        logits = score_ref[at, :]
        r = lax.broadcasted_iota(jnp.int32, logits.shape, 0) + i * step
        own = r == lax.broadcasted_iota(jnp.int32, logits.shape, 1)
        keep = own | (mask_ref[at, :].astype(F32) == 1.0)
        top = jnp.max(jnp.where(keep, logits, -jnp.inf), axis=1, keepdims=True)
        weights = jnp.where(keep, jnp.exp(logits - top), 0.0)
        total = jnp.sum(weights, axis=1, keepdims=True)
        hit = jnp.sum(jnp.where(own, logits, 0.0), axis=1, keepdims=True)
        score_ref[at, :] = (weights / total - own.astype(F32)) / count / root
        return carry + (top + jnp.log(total) - hit)

    ce = jnp.zeros((step, 1), F32)
    for i in range(total_rows // step):
        ce = rows(i, ce)
    loss_ref[0, 0] = jnp.sum(ce)
    total_ref[0, 0] = count
    parts = three(score_ref[...])
    d_user = sum(dot(p, item) for p in parts)
    d_item = sum(dot(user, p, 0, 0) for p in parts).T
    user_ref[...] = d_user
    item_ref[...] = d_item
    d_towers_ref[0] = hdot(bags_user, d_user, 0, 0)
    d_towers_ref[1] = hdot(bags_item, d_item, 0, 0)
    mine = pl.ds(pl.multiple_of(me * PAIR, PAIR), PAIR)
    back_user = hdot(user_ref[mine, :], towers_ref[0], 1, 1).astype(BF).astype(F32)
    back_item = hdot(item_ref[mine, :], towers_ref[1], 1, 1).astype(BF).astype(F32)
    d_emb = dot(spread(PAIR, 0), back_user) + dot(spread(PAIR, 1), back_item)
    d_act = dot(d_emb.astype(BF), w_out_ref[...].astype(BF))
    dact_ref[...] = d_act
    d_bias = jnp.sum(d_act * one_ref[...], axis=0, keepdims=True)
    d_gain = jnp.sum(d_act * two_ref[...], axis=0, keepdims=True)
    d_low = d_emb.T.astype(BF)
    second = sum(dot(d_low, p) for p in three(act_ref[...]))
    width = act_ref.shape[1]
    tiles = width // LANES
    half = tiles // 2
    for j in range(tiles):
        cols = slice(j * LANES, (j + 1) * LANES)
        h, t = j // half, j % half
        halves_ref[h, t : t + 1, :] = d_bias[:, cols]
        halves_ref[h, half + t : half + t + 1, :] = d_gain[:, cols]
        halves_ref[h, pl.ds(tiles + t, embed, stride=half), :] = second[:, cols]
    odd = (me // core) % 2
    one, two = (halves_ref[h, : keep_ref.shape[0], :] for h in range(2))
    keep_ref[...] = jnp.where(odd == 1, two, one)
    send_ref[...] = jnp.where(odd == 1, one, two)


def share_kernel(keep_ref, got_ref, pay_ref, *, n, tiles):
    total = keep_ref[...] + got_ref[...]
    sums, rows = total[:tiles].astype(BF), (total.shape[0] - tiles) // n
    high = total[tiles:].astype(BF).astype(F32)
    low = total[tiles:] - high
    held = tiles + 2 * rows
    for d in range(n):
        at = slice(d * rows, (d + 1) * rows)
        part = jnp.concatenate([sums.astype(F32), high[at], low[at]], axis=0)
        pay_ref[d * held : (d + 1) * held, :] = part.astype(BF)


def loss_spread(plan, bags, neg_mask, towers, w_out, act, one, two):
    embed = towers.shape[1]
    rows = neg_mask.shape[0]
    bags_user, bags_item = bags[:rows], bags[rows:]
    user = hdot(bags_user, towers[0]).astype(BF)
    item = hdot(bags_item, towers[1]).astype(BF)
    items = lax.all_gather(item, AXES, axis=0, tiled=True)
    root = math.sqrt(embed)
    logits = dot(user, items, 1, 1) / root
    at = lax.axis_index(AXES) * rows + lax.broadcasted_iota(jnp.int32, logits.shape, 0)
    own = lax.broadcasted_iota(jnp.int32, logits.shape, 1) == at
    keep = own | (neg_mask == 1)
    top = jnp.max(jnp.where(keep, logits, -jnp.inf), axis=1, keepdims=True)
    weights = jnp.where(keep, jnp.exp(logits - top), 0.0)
    total = jnp.sum(weights, axis=1, keepdims=True)
    ce = top + jnp.log(total) - jnp.sum(jnp.where(own, logits, 0.0), axis=1, keepdims=True)
    count = lax.psum(jnp.sum(neg_mask.astype(F32)), AXES) / items.shape[0]
    scores = (weights / total - own.astype(F32)) / count / root
    d_user = hdot(scores, items.astype(F32))
    d_item = lax.psum_scatter(
        hdot(scores, user.astype(F32), 0, 0), AXES, scatter_dimension=0, tiled=True
    )
    d_towers = jnp.stack([hdot(bags_user, d_user, 0, 0), hdot(bags_item, d_item, 0, 0)])
    back = jnp.stack([hdot(d_user, towers[0], 1, 1), hdot(d_item, towers[1], 1, 1)], axis=1)
    d_emb = back.reshape(2 * rows, embed).astype(BF)
    d_act = dot(d_emb, w_out.astype(BF))
    d_second = hdot(d_emb.astype(F32), act, 0, 0)
    sums = jnp.stack([jnp.sum(d_act * one, axis=0), jnp.sum(d_act * two, axis=0)])
    sums, d_second, d_towers, loss = lax.psum((sums, d_second, d_towers, jnp.sum(ce)), AXES)
    return d_act, sums.reshape(-1, LANES), d_second, d_towers, loss, count


def block_halves(me, owners_ref, g_ref, outs, masks, local):
    width = g_ref.shape[2]
    bsize = LANES // 2
    half, quarter = bsize // 2, bsize // 4
    side = width // bsize
    lane_half = lax.broadcasted_iota(jnp.int32, (quarter, LANES), 1) // bsize
    for i, m in enumerate(masks):
        for b in range(local):
            r, c, odd = place(owners_ref[(me ^ m) * local + b], side)
            base = pl.multiple_of(r * half, half)
            cols = pl.ds(pl.multiple_of(c * LANES, LANES), LANES)
            keep = lane_half == odd
            to = (i * local + b) * quarter
            for h, out in enumerate(outs):
                tile = g_ref[h, pl.ds(base, half), cols].astype(out.dtype)
                out[to : to + quarter, :] = jnp.where(keep, tile[:quarter], swap_halves(tile[quarter:]))


def grad_kernel(
    me_ref, owners_ref, sums_ref, coef_ref, norm_ref, dact_ref, slope_ref, pre_ref, live_ref, xt_ref,
    top_ref, low_ref, chunk_ref, d_norm_ref, g_ref, d_pre_ref, row_ref,
    *, parts, order, local, core,
):
    rows, width = pre_ref.shape
    tiles = width // LANES
    held = sums_ref.shape[0] // parts
    half = tiles // 2
    if parts > 1:
        sides = []
        for h in range(2):
            side = jnp.zeros((held, LANES), F32)
            for d in range(parts):
                if (d // core) % 2 == h:
                    side = side + sums_ref[d * held : (d + 1) * held, :].astype(F32)
            sides.append(side)
        total = jnp.concatenate([s[i * half : (i + 1) * half] for i in range(2) for s in sides], axis=0)
        share = (held - tiles) // 2
        sides = [s[tiles : tiles + share] + s[tiles + share :] for s in sides]
        chunk_ref[...] = jnp.concatenate(
            [s[i * half : (i + 1) * half] for i in range(share // half) for s in sides], axis=0
        )
    else:
        total = sums_ref[...]
        chunk_ref[...] = jnp.zeros(chunk_ref.shape, F32)
    d_norm_ref[0:tiles, :] = total[tiles : 2 * tiles]
    d_norm_ref[tiles : 2 * tiles, :] = total[:tiles]
    for j in range(tiles):
        cols = slice(j * LANES, (j + 1) * LANES)
        row_ref[0:1, cols] = total[j : j + 1]
        row_ref[1:2, cols] = total[tiles + j : tiles + j + 1]
    scale = norm_ref[0:1, :] * coef_ref[1:2, :]
    flat = scale * row_ref[0:1, :] / coef_ref[2:3, :]
    tilt = scale * row_ref[1:2, :] / coef_ref[2:3, :] * coef_ref[1:2, :]
    row_ref[2:3, :] = scale
    row_ref[3:4, :] = flat
    row_ref[4:5, :] = tilt
    block = 2 * LANES
    for j in range(width // block):
        for i in range(2):
            cols = slice(j * block + i * LANES, j * block + (i + 1) * LANES)
            for b in range(rows // SLOTS_BAG):
                at = slice(b * SLOTS_BAG, (b + 1) * SLOTS_BAG)
                lead = dact_ref[b : b + 1, cols] * row_ref[2:3, cols]
                apart = (pre_ref[at, cols] - coef_ref[0:1, cols]) * row_ref[4:5, cols]
                d_pre = slope_ref[at, cols] * lead - row_ref[3:4, cols] - apart
                d_pre_ref[at, cols] = (live_ref[at, :] * d_pre).astype(BF)
        cols = slice(j * block, (j + 1) * block)
        g_ref[:, :, cols] = dot(xt_ref[...], d_pre_ref[:, cols]).reshape(2, width // 2, block)
    block_halves(me_ref[0], owners_ref, g_ref, (top_ref, low_ref), order, local)


def keep_kernel(me_ref, owners_ref, g_ref, top_ref, low_ref, *, order, local):
    block_halves(me_ref[0], owners_ref, g_ref, (top_ref, low_ref), order, local)


def scatter_sum(plan, kept, sent, rows):
    rest = len(plan.rest)
    shape = (2, 2, rest, rows, LANES)
    one, two = (
        (k + plan.swap(s, plan.core).astype(F32)).reshape(shape) for k, s in zip(kept, sent)
    )
    got_one = plan.swap(one[1].astype(BF), plan.x)
    got_two = plan.swap(two[:, 1].astype(BF), plan.y)
    one = one[0] + got_one.astype(F32)
    two = two[:, 0] + got_two.astype(F32)
    got_one = plan.swap(one[1].astype(BF), plan.y)
    got_two = plan.swap(two[1].astype(BF), plan.x)
    one = one[0] + got_one.astype(F32)
    two = two[0] + got_two.astype(F32)
    if rest <= 4:
        both = jnp.concatenate([one[1:], two[1:]], axis=1).astype(BF)
        return one, two, [plan.swap(both[k], m) for k, m in enumerate(plan.rest[1:])]
    both = jnp.concatenate([one, two], axis=1)
    for b in reversed(plan.bits):
        both = both.reshape(2, -1, 2 * rows, LANES)
        both = both[0] + plan.swap(both[1].astype(BF), b).astype(F32)
    return both[:, :rows], both[:, rows:], []


def norm_kernel(*refs, n):
    one_ref, two_ref, chunk_ref = refs[:3]
    got = refs[3:-2]
    g_ref, pay_ref = refs[-2:]
    total = jnp.concatenate([one_ref[0], two_ref[0]], axis=0)
    for g in got:
        total = total + g[...].astype(F32)
    g_ref[...] = total
    chunk = chunk_ref[...]
    squares = jnp.sum(total * total, keepdims=True) + jnp.sum(chunk * chunk, keepdims=True)
    high = chunk.astype(BF)
    low = chunk - high.astype(F32)
    for i, v in enumerate(three(squares)):
        low = jnp.where(spare(chunk.shape, i), v.astype(F32), low)
    packed = jnp.concatenate([high, low.astype(BF)], axis=0)
    rows = packed.shape[0]
    for d in range(n):
        pay_ref[d * rows : (d + 1) * rows, :] = packed


def spare(shape, i):
    row = lax.broadcasted_iota(jnp.int32, shape, 0)
    lane = lax.broadcasted_iota(jnp.int32, shape, 1)
    return (row == shape[0] - 1) & (lane == LANES - 3 + i)


def adamw(grad, weight, first, second):
    first = BETA_ONE * first + (1 - BETA_ONE) * grad
    second = BETA_TWO * second + (1 - BETA_TWO) * grad * grad
    step = (
        first / (1 - BETA_ONE**STEP) / (jnp.sqrt(second / (1 - BETA_TWO**STEP)) + EPSILON)
    )
    return weight - RATE * (step + DECAY * weight), first, second


def eliminate(gram_ref, power_ref):
    count, size, lanes = gram_ref.shape
    group = 8
    lane = lax.broadcasted_iota(jnp.int32, (count * group, lanes), 1)
    left = lax.broadcasted_iota(jnp.int32, (1, lanes), 1) < size
    for at in range(0, size, group):
        rest = at + group
        gram, power = gram_ref[:, at:rest, :], power_ref[:, at:rest, :]
        flat = gram.reshape(count * group, lanes)
        cols = [
            jnp.take_along_axis(flat, (lane // size) * size + at + i, axis=1).reshape(gram.shape)
            for i in range(group)
        ]
        for i in range(group):
            inv = lax.rsqrt(cols[i][:, i : i + 1, :])
            row, power_row = gram[:, i : i + 1, :] * inv, power[:, i : i + 1, :] * inv
            gram_ref[:, at + i : at + i + 1, :] = row
            power_ref[:, at + i : at + i + 1, :] = power_row
            f = cols[i] * inv
            gram, power = gram - f * row, power - f * power_row
            for j in range(i + 1, group):
                cols[j] = cols[j] - f * f[:, j : j + 1, :]
        if rest == size:
            return
        a, b, c = (v.astype(F32) for v in three(gram_ref[:, at:rest, :]))
        d, e, f = (v.astype(F32) for v in three(power_ref[:, at:rest, :]))
        lhs = jnp.concatenate([a, a, b, b, a, c], axis=1).astype(BF)
        rhs = jnp.concatenate([a, b, a, b, c, a], axis=1)
        rhs = jnp.concatenate([rhs, jnp.concatenate([d, e, d, e, f, d], axis=1)], axis=2).astype(BF)
        turned = [lhs[m].T for m in range(count)]
        for m in range(count):
            one = dot(turned[m][rest:size], rhs[m])
            two = dot(turned[m][size + rest :], rhs[m])
            gram_ref[m, rest:, :] = gram_ref[m, rest:, :] - jnp.where(left, one[:, :lanes], two[:, :lanes])
            power_ref[m, rest:, :] = power_ref[m, rest:, :] - jnp.where(left, one[:, lanes:], two[:, lanes:])


def pair(a, b):
    return jnp.concatenate([a, b], axis=1)


def prepare_kernel(
    w_hbm, left_hbm, right_hbm, bl_hbm, br_hbm, first_hbm, second_hbm, ema_hbm,
    moments_ref, stats_ref, bases_ref, weights_ref, turned_ref, powers_ref,
    w_ref, left_ref, right_ref, bl_ref, br_ref, first_ref, second_ref, ema_ref, sems,
):
    fetch(
        (w_hbm, left_hbm, right_hbm, bl_hbm, br_hbm, first_hbm, second_hbm, ema_hbm),
        (w_ref, left_ref, right_ref, bl_ref, br_ref, first_ref, second_ref, ema_ref),
        sems,
    )
    each = range(w_ref.shape[0])
    for b in each:
        moments_ref[b] = pair(first_ref[b], second_ref[b])
        stats_ref[b] = pair(left_ref[b], right_ref[b])
        bases_ref[b] = pair(bl_ref[b], br_ref[b])
        weights_ref[b] = pair(w_ref[b], ema_ref[b])
    half = [hdot(bl_ref[b], first_ref[b], 0, 0) for b in each]
    for b in each:
        turned_ref[b] = hdot(half[b], br_ref[b])
    lefts = [hdot(bl_ref[b], left_ref[b], 0, 0) for b in each]
    rights = [hdot(br_ref[b], right_ref[b], 0, 0) for b in each]
    for b in each:
        powers_ref[b] = pair(lefts[b], rights[b])


def turn_kernel(
    me_ref, owners_ref, g_ref, bases_ref,
    wo_hbm, mo_hbm, vo_hbm, eo_hbm, wt_hbm, mt_hbm, vt_hbm, wn_hbm, mn_hbm, vn_hbm,
    grad_ref, squares_ref, powers_ref, scale_ref,
    wide_ref, towers_ref, norms_ref, sems,
):
    local, bsize = bases_ref.shape[0], bases_ref.shape[1]
    sources = (wo_hbm, mo_hbm, vo_hbm, eo_hbm, wt_hbm, mt_hbm, vt_hbm, wn_hbm, mn_hbm, vn_hbm)
    targets = [wide_ref.at[i] for i in range(4)]
    targets += [towers_ref.at[i] for i in range(3)] + [norms_ref.at[i] for i in range(3)]
    copies = [pltpu.make_async_copy(a, b, sems.at[i]) for i, (a, b) in enumerate(zip(sources, targets))]
    for c in copies:
        c.start()
    largest = jnp.max(jnp.abs(g_ref[...]), keepdims=True)
    largest = jnp.where(largest > 0.0, largest, 1.0)
    scale_ref[...] = jnp.broadcast_to(largest, scale_ref.shape)
    half = bsize // 2
    each = range(local)
    grads = []
    for b in each:
        odd = owners_ref[me_ref[0] * local + b] % 2
        quarters = []
        for i in range(2):
            at = (i * local + b) * half // 2
            tile = g_ref[at : at + half // 2, :]
            tile = jnp.where(odd == 1, swap_halves(tile), tile)
            quarters += [tile[:, :bsize], tile[:, bsize:]]
        grads.append(jnp.concatenate(quarters, axis=0) / largest)
    bl = [bases_ref[b, :, :bsize] for b in each]
    br = [bases_ref[b, :, bsize:] for b in each]
    by_left = [hdot(bl[b], grads[b], 0, 0) for b in each]
    by_right = [hdot(grads[b], br[b]) for b in each]
    outer = [hdot(grads[b], grads[b], 1, 1) for b in each]
    inner = [hdot(grads[b], grads[b], 0, 0) for b in each]
    for b in each:
        squares_ref[b] = pair(outer[b], inner[b])
    for b in each:
        grad_ref[b] = pair(grads[b], hdot(by_left[b], br[b]))
    lefts = [hdot(by_left[b], grads[b], 1, 1) for b in each]
    rights = [hdot(by_right[b], grads[b], 0, 0) for b in each]
    for b in each:
        powers_ref[b] = pair(lefts[b], rights[b])
    for c in copies:
        c.wait()


def step_kernel(
    got_ref, d_norm_ref, d_towers_ref,
    grad_ref, squares_ref, powers_ref, scale_ref,
    old_ref, towers_ref, norms_ref,
    moments_ref, stats_ref, bases_ref, weights_ref, turned_first_ref, powers_old_ref,
    *refs, n,
):
    (
        w_out, low_out, left_out, right_out, bl_out, br_out, first_out, second_out, ema_out,
        wo_out, mo_out, vo_out, eo_out, wt_out, mt_out, vt_out, wn_out, mn_out, vn_out, gn_out,
        gram_ref, power_ref, wide_ref, dn_ref, flat_ref,
    ) = refs
    local, bsize = bases_ref.shape[0], bases_ref.shape[1]
    embed, width = old_ref.shape[1:]
    tiles = width // LANES
    held = got_ref.shape[0] // n
    if n > 1:
        chunk = held // 2
        used = functools.reduce(jnp.logical_or, [spare((chunk, LANES), i) for i in range(3)])
        squares = jnp.zeros((chunk, LANES), F32)
        for d in range(n):
            part = got_ref[d * held : (d + 1) * held, :].astype(F32)
            squares = squares + jnp.where(used, part[chunk:], 0.0)
            flat_ref[d * chunk : (d + 1) * chunk, :] = part[:chunk] + jnp.where(used, 0.0, part[chunk:])
        squares = jnp.sum(squares)
        for j in range(tiles):
            wide_ref[:, j * LANES : (j + 1) * LANES] = flat_ref[pl.ds(j, embed, stride=tiles), :]
    else:
        squares = jnp.max(got_ref[0:1, :LANES])
        wide_ref[...] = got_ref[8 : 8 + embed, :]
    squares = squares + jnp.sum(d_towers_ref[...] * d_towers_ref[...])
    squares = squares + jnp.sum(d_norm_ref[...] * d_norm_ref[...])
    norm = jnp.sqrt(jnp.full((1, LANES), squares, F32))
    gn_out[0, 0] = jnp.max(norm)
    factor = (CLIP / jnp.maximum(norm, CLIP))[:, :1]
    each = range(local)
    lead = factor * scale_ref[0:1, 0:1]
    twice = (1 - BETA_TWO) * lead * lead
    lefts, rights = [], []
    for b in each:
        powers = BETA_TWO * powers_old_ref[b] + twice * powers_ref[b]
        power_ref[b] = powers
        lefts.append(powers[:, :bsize])
        rights.append(powers[:, bsize:])
    for b in each:
        gram_ref[b] = pair(hdot(lefts[b], lefts[b], 1, 1), hdot(rights[b], rights[b], 1, 1))
    ratios = []
    for b in each:
        stats = BETA_TWO * stats_ref[b] + twice * squares_ref[b]
        left_out[b], right_out[b] = stats[:, :bsize], stats[:, bsize:]
        first_out[b] = BETA_ONE * moments_ref[b, :, :bsize] + (1 - BETA_ONE) * lead * grad_ref[b, :, :bsize]
        turned = grad_ref[b, :, bsize:]
        second = BETA_TWO * moments_ref[b, :, bsize:] + twice * turned * turned
        second_out[b] = second
        moved = BETA_ONE * turned_first_ref[b] + (1 - BETA_ONE) * lead * turned
        moved = moved / (1 - BETA_ONE**STEP)
        ratios.append(moved / (jnp.sqrt(second / (1 - BETA_TWO**STEP)) + EPSILON))
    half = [hdot(bases_ref[b, :, :bsize], ratios[b]) for b in each]
    updates = [hdot(half[b], bases_ref[b, :, bsize:], 1, 1) for b in each]
    for b in each:
        old = weights_ref[b, :, :bsize]
        new = old - RATE * (updates[b] + DECAY * old)
        w_out[b] = new
        low_out[b] = new.astype(BF)
        ema_out[b] = AVG_KEEP * weights_ref[b, :, bsize:] + AVG_TAKE * new
    new, m, v = adamw(wide_ref[...] * factor, old_ref[0], old_ref[1], old_ref[2])
    wo_out[...], mo_out[...], vo_out[...] = new, m, v
    eo_out[...] = AVG_KEEP * old_ref[3] + AVG_TAKE * new
    for t in range(2):
        wt_out[t], mt_out[t], vt_out[t] = adamw(
            d_towers_ref[t] * factor, towers_ref[0, t], towers_ref[1, t], towers_ref[2, t]
        )
        for j in range(tiles):
            dn_ref[t : t + 1, j * LANES : (j + 1) * LANES] = d_norm_ref[
                t * tiles + j : t * tiles + j + 1, :
            ]
    wn_out[...], mn_out[...], vn_out[...] = adamw(
        dn_ref[...] * factor, norms_ref[0], norms_ref[1], norms_ref[2]
    )
    eliminate(gram_ref, power_ref)
    for b in each:
        turned = power_ref[b].T
        bl_out[b], br_out[b] = turned[:bsize], turned[bsize:]


def exchange(payload):
    return lax.all_to_all(payload, AXES, 0, 0, tiled=True)


def on_device(
    plan,
    codes, field_offsets, seg_mask, neg_mask, owners,
    w_hidden, stat_left, stat_right, basis_left, basis_right, mom1_hidden, mom2_hidden, ema_hidden,
    w_out, mom1_out, mom2_out, ema_out,
    w_towers, mom1_towers, mom2_towers,
    w_norm, mom1_norm, mom2_norm,
):
    n = plan.n
    local, bsize = w_hidden.shape[0], w_hidden.shape[1]
    width, embed = w_out.shape
    slots = codes.shape[0]
    rows, total_rows = neg_mask.shape
    tiles = width // LANES
    half = bsize // 2
    bags = slots // SLOTS_BAG
    masked = total_rows <= 1024 and n <= embed
    me = lax.axis_index(AXES).astype(jnp.int32)[None]

    chunks = total_rows // LANES if masked else 0
    size = local * half + chunks * PAIR + PAIR
    (payload,) = call(
        functools.partial(pack_kernel, masked=masked),
        [((size, LANES), BF)],
        [w_hidden, neg_mask, seg_mask.reshape(-1, LANES)],
        hbm=3,
        scratch=[
            pltpu.VMEM(w_hidden.shape, F32),
            pltpu.VMEM(neg_mask.shape, jnp.int32),
            pltpu.VMEM((slots // LANES, LANES), jnp.int32),
            pltpu.SemaphoreType.DMA((3,)),
        ],
        name="pack",
    )
    cut = max(half, size // 2 // half * half)
    cut = min(cut, local * half)
    blocks = (local, bsize, bsize)
    twin = (local, bsize, 2 * bsize)
    state = [
        w_hidden, stat_left, stat_right, basis_left, basis_right, mom1_hidden, mom2_hidden, ema_hidden
    ]
    prepared = call(
        prepare_kernel,
        [(twin, F32)] * 4 + [(blocks, F32), (twin, F32)],
        state,
        hbm=len(state),
        scratch=[pltpu.VMEM(blocks, F32)] * len(state) + [pltpu.SemaphoreType.DMA((len(state),))],
        limit=12,
        name="prepare",
        cost=10_000_000,
    )
    turned_out, turned_mom1, turned_mom2, turned_ema = (
        a.T for a in (w_out, mom1_out, mom2_out, ema_out)
    )
    early = hash_inputs(codes, field_offsets)
    live = jnp.broadcast_to(seg_mask.astype(F32)[:, None], (slots, LANES))
    slot_bag = lax.broadcasted_iota(jnp.int32, (bags, slots), 1) // SLOTS_BAG
    in_bag = slot_bag == lax.broadcasted_iota(jnp.int32, (bags, slots), 0)
    chosen = jnp.where(in_bag, seg_mask.astype(F32)[None], 0.0).astype(BF)
    late = (*prepared, live, chosen)
    zero = (me[0] >> 16).astype(BF)

    def held_by(pieces):
        return [([m | base for m in plan.rest], row) for _, base, row in pieces]

    def place_blocks(pieces):
        (planes,) = call(
            functools.partial(assemble_kernel, holds=held_by(pieces), local=local),
            [((2, width, width), BF)],
            [me, owners] + [a for a, _, _ in pieces],
            smem=2,
            limit=8,
            name="assemble",
            cost=10_000_000,
        )
        return planes

    pieces, done, planes, (x, x_turned), (*prepared, live, chosen) = gather_pieces(
        plan, payload, cut, zero, early, late, place_blocks
    )
    mask_shape = (total_rows, total_rows) if masked else (PAIR, LANES)
    holds = held_by(pieces)
    arrays = [a for a, _, _ in pieces]
    pre, kept, sent, counts, mask, _ = call(
        functools.partial(
            pre_kernel, holds=holds, done=done, local=local, masked=masked, core=plan.core
        ),
        [
            ((slots, width), F32),
            ((tiles, LANES), F32),
            ((tiles, LANES), F32),
            ((n, LANES), F32),
            (mask_shape, BF),
            ((2, width, width), BF),
        ],
        [me, owners, planes] + arrays + [x, live],
        smem=2,
        scratch=[pltpu.VMEM((2 * tiles, LANES), F32)],
        aliases={2: 5},
        limit=16,
        name="pre",
    )
    (stats,) = call(
        functools.partial(merge_kernel, core=plan.core),
        [((n * tiles, LANES), F32)],
        [me, counts, kept, plan.swap(sent, plan.core)],
        smem=1,
        limit=4,
        name="merge",
    )
    stats = exchange(stats)
    slope, act, one, two, coef, bag_sums, pay = call(
        functools.partial(act_kernel, core=plan.core),
        [
            ((slots, width), F32),
            ((bags, width), F32),
            ((bags, width), F32),
            ((bags, width), F32),
            ((8, width), F32),
            ((bags, embed), F32),
            ((n * 8, LANES), F32),
        ],
        [stats, counts, w_norm, pre, live, chosen, turned_out],
        scratch=[
            pltpu.VMEM((slots, LANES), BF),
            pltpu.VMEM((tiles, bags * 8 + 8, LANES), F32),
            pltpu.VMEM((tiles, bags * 8 + 8, LANES), F32),
        ],
        limit=12,
        name="act",
    )
    if masked:
        chunk = embed * tiles // n
        everyone = exchange(pay)
        shared = (tiles + embed * tiles // 2, LANES)
        d_act, kept, sent, d_towers, loss_sum, count = call(
            functools.partial(loss_kernel, n=n, core=plan.core),
            [
                ((bags, width), F32),
                (shared, F32),
                (shared, F32),
                ((2, embed, embed), F32),
                ((1, 1), F32),
                ((1, 1), F32),
            ],
            [me, everyone, mask, w_towers, turned_out, act, one, two],
            smem=1,
            smem_outs=2,
            scratch=[
                pltpu.VMEM((total_rows, total_rows), F32),
                pltpu.VMEM((total_rows, embed), F32),
                pltpu.VMEM((total_rows, embed), F32),
                pltpu.VMEM((2, shared[0] + 8, LANES), F32),
            ],
            name="loss",
        )
        (pay,) = call(
            functools.partial(share_kernel, n=n, tiles=tiles),
            [((n * (tiles + chunk), LANES), BF)],
            [kept, plan.swap(sent, plan.core)],
            limit=4,
            name="share",
        )
        sums, parts = exchange(pay), n
        loss_sum, count = loss_sum[0, 0], count[0, 0]
    else:
        d_act, sums, d_second, d_towers, loss_sum, count = loss_spread(
            plan, bag_sums, neg_mask, w_towers, turned_out, act, one, two
        )
        parts = 1
        chunk = 8
    groups = [m for m in (0, plan.y, plan.x, plan.x | plan.y)]
    keep_order = [g | r for g in groups for r in plan.rest]
    order = (keep_order, [m | plan.core for m in keep_order])
    packed = (n // 2 * local * half // 2, LANES)
    packed = (n // 2 * local * half // 2, LANES)
    *sent, second_chunk, d_norm, full = call(
        functools.partial(grad_kernel, parts=parts, order=order[1], local=local, core=plan.core),
        [
            (packed, BF),
            (packed, BF),
            ((chunk, LANES), F32),
            ((2 * tiles, LANES), F32),
            ((2, width // 2, width), F32),
        ],
        [me, owners, sums, coef, w_norm, d_act, slope, pre, live, x_turned],
        smem=2,
        scratch=[pltpu.VMEM((slots, width), BF), pltpu.VMEM((8, width), F32)],
        limit=16,
        name="grad",
    )
    kept = call(
        functools.partial(keep_kernel, order=order[0], local=local),
        [(packed, F32), (packed, F32)],
        [me, owners, full],
        smem=2,
        limit=8,
        name="keep",
        cost=100_000_000,
    )
    one_sum, two_sum, others = scatter_sum(plan, kept, sent, local * half // 2)
    copies = n if masked else 1
    grad, pay = call(
        functools.partial(norm_kernel, n=copies),
        [((local * half, LANES), F32), ((copies * 2 * chunk, LANES), BF)],
        [one_sum, two_sum, second_chunk, *others],
        name="norm",
    )
    if masked:
        got = exchange(pay)
    else:
        squares = lax.psum(jnp.sum(grad * grad), AXES) + jnp.sum(d_second * d_second)
        got = jnp.concatenate([jnp.full((8, width), squares, F32), d_second], axis=0)
    moments, stats, bases, weights, turned_first, powers_old = prepared
    plain = [
        turned_out, turned_mom1, turned_mom2, turned_ema,
        w_towers, mom1_towers, mom2_towers,
        w_norm, mom1_norm, mom2_norm,
    ]
    turned = call(
        turn_kernel,
        [(twin, F32)] * 3
        + [((8, LANES), F32), ((4, embed, width), F32), ((3, 2, embed, embed), F32), ((3, 2, width), F32)],
        [me, owners, grad, bases, *plain],
        smem=2,
        hbm=len(plain),
        scratch=[pltpu.SemaphoreType.DMA((len(plain),))],
        name="turn",
        cost=10_000_000,
    )
    outs = [(blocks, F32), (blocks, BF)] + [(blocks, F32)] * 7
    outs += [((embed, width), F32)] * 4 + [((2, embed, embed), F32)] * 3 + [((2, width), F32)] * 3
    new = call(
        functools.partial(step_kernel, n=n if masked else 1),
        outs + [((1, 1), F32)],
        [
            got, d_norm, d_towers, *turned,
            moments, stats, bases, weights, turned_first, powers_old,
        ],
        smem_outs=1,
        scratch=[
            pltpu.VMEM(twin, F32),
            pltpu.VMEM(twin, F32),
            pltpu.VMEM((embed, width), F32),
            pltpu.VMEM((2, width), F32),
            pltpu.VMEM((embed * tiles + tiles, LANES), F32),
        ],
        name="step",
    )
    return (loss_sum, count, new[-1][0, 0], *new[:9], *(a.T for a in new[9:13]), *new[13:-1])


def solution(mesh):
    split = P(("gx", "gy"))
    plan = Plan(mesh.shape["gx"], mesh.shape["gy"])
    return jax.shard_map(
        functools.partial(on_device, plan),
        mesh=mesh,
        in_specs=(split, P(), split, split, P()) + (split,) * 8 + (P(),) * 10,
        out_specs=(P(),) * 3 + (split,) * 9 + (P(),) * 10,
        check_vma=False,
    )
```

```python
import functools
import math

import jax
import jax.numpy as jnp
from jax import lax
from jax.experimental import pallas as pl
from jax.experimental.pallas import tpu as pltpu
from jax.sharding import PartitionSpec as P

FIELDS = 4
BAG = 8
HASH_RANGE = 4096
STEP = 10
BETA_ONE = 0.9
BETA_TWO = 0.95
EPSILON = 1e-08
RATE = 0.03
DECAY = 0.01
CLIP = 0.01
AVG_KEEP = 0.8
AVG_TAKE = 0.2

F32 = jnp.float32
BF = jnp.bfloat16
HIGH = lax.Precision.HIGHEST
AXES = ("gx", "gy")
LANES = 128
SLOTS_BAG = FIELDS * BAG
PAIR = 16
MIB = 1 << 20


def dot(a, b, ca=1, cb=0, precision=None):
    return lax.dot_general(
        a, b, (((ca,), (cb,)), ((), ())), precision=precision, preferred_element_type=F32
    )


hdot = functools.partial(dot, precision=HIGH)


def spec(space=pltpu.VMEM):
    return pl.BlockSpec(memory_space=space)


def in_hbm(a):
    return pltpu.with_memory_space_constraint(a, pltpu.HBM)


def call(kernel, outs, args, smem=0, hbm=0, smem_outs=0, aliases=None, scratch=(), limit=16, name=None, cost=None):
    args = list(args)
    specs = [spec(pltpu.SMEM)] * smem + [spec()] * (len(args) - smem - hbm) + [spec(pltpu.HBM)] * hbm
    if hbm:
        args[-hbm:] = [in_hbm(a) for a in args[-hbm:]]
    spaces = [pltpu.VMEM] * (len(outs) - smem_outs) + [pltpu.SMEM] * smem_outs
    estimate = None
    if cost:
        estimate = pl.CostEstimate(flops=cost, bytes_accessed=cost // 100, transcendentals=0)
    return pl.pallas_call(
        kernel,
        out_shape=[jax.ShapeDtypeStruct(s, t) for s, t in outs],
        in_specs=specs,
        out_specs=[spec(space) for space in spaces],
        scratch_shapes=list(scratch),
        compiler_params=pltpu.CompilerParams(vmem_limit_bytes=limit * MIB),
        cost_estimate=estimate,
        input_output_aliases=aliases or {},
        name=name,
    )(*args)


def fetch(sources, targets, sems):
    copies = [pltpu.make_async_copy(a, b, sems.at[i]) for i, (a, b) in enumerate(zip(sources, targets))]
    for c in copies:
        c.start()
    for c in copies:
        c.wait()


def swap_halves(v):
    half = v.shape[1] // 2
    return jnp.concatenate([v[:, half:], v[:, :half]], axis=1)


def place(q, side):
    shift = side.bit_length() - 1
    return q >> shift, (q & (side - 1)) >> 1, q & 1


class Plan:
    def __init__(self, gx, gy):
        self.gx, self.gy, self.n = gx, gy, gx * gy
        self.core = gy
        self.x = 2 * gy
        self.y = 1
        bits = []
        b = 2
        while b < gy:
            bits.append(b)
            b *= 2
        b = 4
        while b < gx:
            bits.append(b * gy)
            b *= 2
        self.bits = bits
        rest = [0]
        for b in bits:
            rest = rest + [m | b for m in rest]
        self.rest = rest

    def swap(self, a, mask):
        mx, my = mask // self.gy, mask % self.gy
        if my == 0:
            return lax.ppermute(a, "gx", [(i, i ^ mx) for i in range(self.gx)])
        if mx == 0:
            return lax.ppermute(a, "gy", [(i, i ^ my) for i in range(self.gy)])
        return lax.ppermute(a, AXES, [(i, i ^ mask) for i in range(self.n)])


def pack_kernel(
    w_hbm, neg_hbm, seg_hbm, out_ref, w_ref, neg_ref, seg_ref, sems, *, masked
):
    fetch((w_hbm, neg_hbm, seg_hbm), (w_ref, neg_ref, seg_ref), sems)
    local, bsize = w_ref.shape[0], w_ref.shape[1]
    half = bsize // 2
    for b in range(local):
        both = jnp.concatenate([w_ref[b, :half, :], w_ref[b, half:, :]], axis=1)
        out_ref[b * half : (b + 1) * half, :] = both.astype(BF)
    at = local * half
    if masked:
        for c in range(neg_ref.shape[1] // LANES):
            part = neg_ref[:, c * LANES : (c + 1) * LANES].astype(F32)
            out_ref[at : at + PAIR, :] = part.astype(BF)
            at += PAIR
    used = jnp.sum(seg_ref[...].astype(F32), axis=0, keepdims=True)
    out_ref[at : at + PAIR, :] = jnp.broadcast_to(used, (PAIR, LANES)).astype(BF)


def gather_pieces(plan, payload, cut, zero, early, late, place_blocks):
    stack = payload[None]
    if len(plan.rest) <= 4:
        stack = jnp.concatenate([stack] + [plan.swap(stack, m) for m in plan.rest[1:]], axis=0)
    else:
        for b in plan.bits:
            stack = jnp.concatenate([stack, plan.swap(stack, b)], axis=0)
    stack, early = lax.optimization_barrier((stack, early))
    by_x = plan.swap(stack, plan.x)
    by_y = plan.swap(stack, plan.y)
    by_x, by_y, late = lax.optimization_barrier((by_x, by_y, late))
    first = plan.swap(by_x[:, :cut] + zero, plan.y)
    second = plan.swap(by_y[:, cut:] + zero, plan.x)
    ready = [(stack, 0, 0), (by_x, plan.x, 0), (by_y, plan.y, 0)]
    ready += swapped(plan, ready)
    planes = place_blocks(ready)
    first, second, planes = lax.optimization_barrier((first, second, planes))
    last = [(first, plan.x | plan.y, 0), (second, plan.x | plan.y, cut)]
    return ready + last + swapped(plan, last), len(ready), planes, early, late


def swapped(plan, pieces):
    return [(plan.swap(a, plan.core), m | plan.core, row) for a, m, row in pieces]


def hash_kernel(codes_hbm, offsets_hbm, x_ref, xt_ref, codes_ref, offsets_ref, sems):
    rows, width = codes_ref.shape
    groups = 2 * FIELDS
    step = 128
    head = pltpu.make_async_copy(offsets_hbm, offsets_ref, sems.at[0])
    head.start()
    parts = []
    for i in range(rows // step):
        at = pl.ds(i * step, step)
        parts.append(pltpu.make_async_copy(codes_hbm.at[at], codes_ref.at[at], sems.at[1 + i]))
        parts[i].start()
    head.wait()
    for i, part in enumerate(parts):
        part.wait()
        at = slice(i * step, (i + 1) * step)
        salted = codes_ref[at, :].reshape(-1, groups, BAG, width) + offsets_ref[...][None, :, None, :]
        salted = (salted & (HASH_RANGE - 1)).reshape(step, width)
        x = (salted.astype(F32) * (2.0 / (HASH_RANGE - 1)) - 1.0).astype(BF)
        x_ref[at, :] = x
        quarter = LANES // 4
        turned = x.T.reshape(-1, 2, quarter, step)
        for h in range(2):
            xt_ref[h * width // 2 : (h + 1) * width // 2, at] = turned[:, h].reshape(-1, step)


def hash_inputs(codes, offsets):
    rows, width = codes.shape
    return call(
        hash_kernel,
        [((rows, width), BF), ((width, rows), BF)],
        [codes, offsets],
        hbm=2,
        scratch=[
            pltpu.VMEM(codes.shape, jnp.int32),
            pltpu.VMEM(offsets.shape, jnp.int32),
            pltpu.SemaphoreType.DMA((1 + rows // 128,)),
        ],
        limit=12,
        name="hash",
        cost=20_000_000,
    )


def assemble(w_ref, me, owners_ref, piece_refs, holds, local):
    width = w_ref.shape[1]
    bsize = LANES // 2
    half = bsize // 2
    side = width // bsize
    for piece, (masks, row0) in zip(piece_refs, holds):
        for k, m in enumerate(masks):
            for b in range(local):
                at = b * half - row0
                if at < 0 or at + half > piece.shape[1]:
                    continue
                r, c, odd = place(owners_ref[(me ^ m) * local + b], side)
                tile = piece[k, at : at + half, :]
                rows = pl.multiple_of(r * bsize, bsize)
                low = pl.multiple_of(r * bsize + half, half)
                cols = pl.ds(pl.multiple_of(c * LANES, LANES), LANES)
                other = swap_halves(tile)
                w_ref[odd, pl.ds(rows, half), cols] = jnp.where(odd == 1, other, tile)
                w_ref[odd, pl.ds(low, half), cols] = jnp.where(odd == 1, tile, other)


def assemble_kernel(me_ref, owners_ref, *refs, holds, local):
    assemble(refs[-1], me_ref[0], owners_ref, refs[:-1], holds, local)


def pre_kernel(*refs, holds, done, local, masked, core):
    me_ref, owners_ref = refs[:2]
    pieces = len(holds)
    piece_refs = refs[3 : 3 + pieces]
    x_ref, live_ref = refs[3 + pieces : 5 + pieces]
    pre_ref, keep_ref, send_ref, count_ref, mask_ref, w_ref, row_ref = refs[5 + pieces :]
    width = x_ref.shape[1]
    bsize = LANES // 2
    half = bsize // 2
    tiles = width // LANES
    me = me_ref[0]
    chunks = mask_ref.shape[1] // LANES if masked else 0
    assemble(w_ref, me, owners_ref, piece_refs[done:], holds[done:], local)
    for piece, (masks, row0) in zip(piece_refs, holds):
        held = piece.shape[1]
        for k, m in enumerate(masks):
            d = me ^ m
            for c in range(chunks):
                at = local * half + c * PAIR - row0
                if at < 0 or at + PAIR > held:
                    continue
                mask_ref[pl.ds(pl.multiple_of(d * PAIR, PAIR), PAIR), c * LANES : (c + 1) * LANES] = (
                    piece[k, at : at + PAIR, :]
                )
            at = local * half + chunks * PAIR - row0
            if 0 <= at and at + PAIR <= held:
                count_ref[pl.ds(d, 1), :] = piece[k, at : at + PAIR, :].astype(F32)[:1]
    live = live_ref[...]
    used = jnp.maximum(jnp.sum(live[:, :1]), 1.0)
    step = 2 * LANES
    left = lax.broadcasted_iota(jnp.int32, (width, step), 1) % LANES < bsize
    for j in range(width // step):
        cols = slice(j * step, (j + 1) * step)
        pre_ref[:, cols] = dot(x_ref[...], jnp.where(left, w_ref[0, :, cols], w_ref[1, :, cols]))
        for i in range(2):
            t = 2 * j + i
            tile = slice(t * LANES, (t + 1) * LANES)
            total = jnp.sum(pre_ref[:, tile] * live, axis=0, keepdims=True)
            apart = pre_ref[:, tile] - total / used
            row_ref[t : t + 1, :] = total
            row_ref[tiles + t : tiles + t + 1, :] = jnp.sum(
                apart * apart * live, axis=0, keepdims=True
            )
    half = tiles // 2
    parts = [
        jnp.concatenate([row_ref[h * half : (h + 1) * half, :], row_ref[tiles + h * half : tiles + (h + 1) * half, :]])
        for h in range(2)
    ]
    odd = (me // core) % 2
    keep_ref[...] = jnp.where(odd == 1, parts[1], parts[0])
    send_ref[...] = jnp.where(odd == 1, parts[0], parts[1])


def combine(pairs):
    used = sum(c for c, _, _ in pairs)
    total = sum(t for _, t, _ in pairs)
    mean = total / jnp.maximum(used, 1.0)
    square = 0.0
    for c, t, q in pairs:
        apart = t / jnp.maximum(c, 1.0) - mean
        square = square + (q + c * apart * apart)
    return used, total, square


def merge_kernel(me_ref, count_ref, keep_ref, got_ref, out_ref, *, core):
    half = keep_ref.shape[0] // 2
    n = count_ref.shape[0]
    counts = [
        jnp.sum(count_ref[pl.ds(d, 1), :], keepdims=True) for d in (me_ref[0], me_ref[0] ^ core)
    ]
    pairs = [(c, ref[:half, :], ref[half:, :]) for c, ref in zip(counts, (keep_ref, got_ref))]
    _, total, square = combine(pairs)
    packed = jnp.concatenate([total, square])
    for d in range(n):
        out_ref[2 * half * d : 2 * half * (d + 1), :] = packed


def act_kernel(
    stats_ref, count_ref, norm_ref, pre_ref, live_ref, pick_ref, w_out_ref,
    slope_ref, act_ref, one_ref, two_ref, coef_ref, bags_ref, pay_ref,
    low_ref, ones_ref, twos_ref,
    *, core,
):
    n = count_ref.shape[0]
    rows, width = pre_ref.shape
    tiles = width // LANES
    counts = jnp.sum(count_ref[...], axis=1, keepdims=True)
    half = tiles // 2
    used, total, square = [], [], []
    for h in range(2):
        pairs = [
            (
                counts[d : d + 1, :] + counts[d ^ core : (d ^ core) + 1, :],
                stats_ref[d * tiles : d * tiles + half, :],
                stats_ref[d * tiles + half : (d + 1) * tiles, :],
            )
            for d in range(n)
            if (d // core) % 2 == h
        ]
        for held, v in zip((used, total, square), combine(pairs)):
            held.append(v)
    used = jnp.max(used[0])
    mean, square = jnp.concatenate(total) / used, jnp.concatenate(square)
    rstd = lax.rsqrt(square / used + 1e-05)
    for j in range(tiles):
        coef_ref[0:1, j * LANES : (j + 1) * LANES] = mean[j : j + 1, :]
        coef_ref[1:2, j * LANES : (j + 1) * LANES] = rstd[j : j + 1, :]
    coef_ref[2:3, :] = jnp.full((1, width), used, F32)
    coef_ref[3:4, :] = coef_ref[1:2, :] * norm_ref[0:1, :]
    bags = rows // SLOTS_BAG
    group = 8

    def fold(v):
        return (v[:group] + v[group : 2 * group]) + (v[2 * group : 3 * group] + v[3 * group :])

    def unfold(ref, j):
        total = ref[j, pl.ds(0, bags, stride=group), :]
        for i in range(1, group):
            total = total + ref[j, pl.ds(i, bags, stride=group), :]
        return total

    for j in range(tiles):
        cols = slice(j * LANES, (j + 1) * LANES)
        centre, scale, bias = coef_ref[0:1, cols], coef_ref[3:4, cols], norm_ref[1:2, cols]
        for b in range(bags):
            at = slice(b * SLOTS_BAG, (b + 1) * SLOTS_BAG)
            to = slice(b * group, (b + 1) * group)
            apart = pre_ref[at, cols] - centre
            y = scale * apart + bias
            capped = jnp.minimum(y, 20.0)
            e = jnp.exp(capped)
            top = e * (e + 2.0)
            below = top + 2.0
            inv = 1.0 / below
            gate = top * inv
            low_ref[at, :] = (y * gate).astype(BF)
            part = e * inv
            slope = gate + (4.0 * capped) * (part * (inv + part))
            slope_ref[at, cols] = slope
            slope = slope * live_ref[at, :]
            ones_ref[j, to, :] = fold(slope)
            twos_ref[j, to, :] = fold(slope * apart)
        act_ref[:, cols] = dot(pick_ref[...], low_ref[...])
        one_ref[:, cols] = unfold(ones_ref, j)
        two_ref[:, cols] = unfold(twos_ref, j) * coef_ref[1:2, cols]
    second = w_out_ref[...].astype(BF).astype(F32)
    bags = hdot(act_ref[...], second, 1, 1)
    pairs = bags.shape[0] // 2
    split = jnp.concatenate([hdot(pick(pairs, 0), bags), hdot(pick(pairs, 1), bags)], axis=0)
    bags_ref[...] = split
    eighth = pairs // 2
    packed = jnp.concatenate([split[i * eighth : (i + 1) * eighth] for i in range(4)], axis=1)
    for d in range(n):
        pay_ref[d * eighth : (d + 1) * eighth, :] = packed


def pick(pairs, which):
    r = lax.broadcasted_iota(jnp.int32, (pairs, 2 * pairs), 0)
    c = lax.broadcasted_iota(jnp.int32, (pairs, 2 * pairs), 1)
    return (c == 2 * r + which).astype(F32)


def spread(pairs, which):
    r = lax.broadcasted_iota(jnp.int32, (2 * pairs, pairs), 0)
    c = lax.broadcasted_iota(jnp.int32, (2 * pairs, pairs), 1)
    return (r == 2 * c + which).astype(F32)


def three(v):
    a = v.astype(BF)
    v = v - a.astype(F32)
    b = v.astype(BF)
    v = v - b.astype(F32)
    return a, b, v.astype(BF)


def loss_kernel(
    me_ref, all_ref, mask_ref, towers_ref, w_out_ref, act_ref, one_ref, two_ref,
    dact_ref, keep_ref, send_ref, d_towers_ref, loss_ref, total_ref,
    score_ref, user_ref, item_ref, halves_ref, *, n, core,
):
    me = me_ref[0]
    embed = towers_ref.shape[1]
    total_rows = mask_ref.shape[0]
    eighth = all_ref.shape[0] // n

    def full(i):
        a = all_ref[:, 2 * i * embed : (2 * i + 1) * embed].reshape(n, eighth, embed)
        b = all_ref[:, (2 * i + 1) * embed : (2 * i + 2) * embed].reshape(n, eighth, embed)
        return jnp.stack([a, b], axis=1).reshape(total_rows, embed)

    bags_user, bags_item = full(0), full(1)
    user = hdot(bags_user, towers_ref[0]).astype(BF)
    item = hdot(bags_item, towers_ref[1]).astype(BF)
    root = math.sqrt(embed)
    score_ref[...] = dot(user, item, 1, 1) / root
    negatives = jnp.sum(mask_ref[...].astype(F32))
    count = negatives / total_rows
    step = 32

    def rows(i, carry):
        at = slice(i * step, (i + 1) * step)
        logits = score_ref[at, :]
        r = lax.broadcasted_iota(jnp.int32, logits.shape, 0) + i * step
        own = r == lax.broadcasted_iota(jnp.int32, logits.shape, 1)
        keep = own | (mask_ref[at, :].astype(F32) == 1.0)
        top = jnp.max(jnp.where(keep, logits, -jnp.inf), axis=1, keepdims=True)
        weights = jnp.where(keep, jnp.exp(logits - top), 0.0)
        total = jnp.sum(weights, axis=1, keepdims=True)
        hit = jnp.sum(jnp.where(own, logits, 0.0), axis=1, keepdims=True)
        score_ref[at, :] = (weights / total - own.astype(F32)) / count / root
        return carry + (top + jnp.log(total) - hit)

    ce = jnp.zeros((step, 1), F32)
    for i in range(total_rows // step):
        ce = rows(i, ce)
    loss_ref[0, 0] = jnp.sum(ce)
    total_ref[0, 0] = count
    parts = three(score_ref[...])
    d_user = sum(dot(p, item) for p in parts)
    d_item = sum(dot(user, p, 0, 0) for p in parts).T
    user_ref[...] = d_user
    item_ref[...] = d_item
    d_towers_ref[0] = hdot(bags_user, d_user, 0, 0)
    d_towers_ref[1] = hdot(bags_item, d_item, 0, 0)
    mine = pl.ds(pl.multiple_of(me * PAIR, PAIR), PAIR)
    back_user = hdot(user_ref[mine, :], towers_ref[0], 1, 1).astype(BF).astype(F32)
    back_item = hdot(item_ref[mine, :], towers_ref[1], 1, 1).astype(BF).astype(F32)
    d_emb = dot(spread(PAIR, 0), back_user) + dot(spread(PAIR, 1), back_item)
    d_act = dot(d_emb.astype(BF), w_out_ref[...].astype(BF))
    dact_ref[...] = d_act
    d_bias = jnp.sum(d_act * one_ref[...], axis=0, keepdims=True)
    d_gain = jnp.sum(d_act * two_ref[...], axis=0, keepdims=True)
    d_low = d_emb.T.astype(BF)
    second = sum(dot(d_low, p) for p in three(act_ref[...]))
    width = act_ref.shape[1]
    tiles = width // LANES
    half = tiles // 2
    for j in range(tiles):
        cols = slice(j * LANES, (j + 1) * LANES)
        h, t = j // half, j % half
        halves_ref[h, t : t + 1, :] = d_bias[:, cols]
        halves_ref[h, half + t : half + t + 1, :] = d_gain[:, cols]
        halves_ref[h, pl.ds(tiles + t, embed, stride=half), :] = second[:, cols]
    odd = (me // core) % 2
    one, two = (halves_ref[h, : keep_ref.shape[0], :] for h in range(2))
    keep_ref[...] = jnp.where(odd == 1, two, one)
    send_ref[...] = jnp.where(odd == 1, one, two)


def share_kernel(keep_ref, got_ref, pay_ref, *, n, tiles):
    total = keep_ref[...] + got_ref[...]
    sums, rows = total[:tiles].astype(BF), (total.shape[0] - tiles) // n
    high = total[tiles:].astype(BF).astype(F32)
    low = total[tiles:] - high
    held = tiles + 2 * rows
    for d in range(n):
        at = slice(d * rows, (d + 1) * rows)
        part = jnp.concatenate([sums.astype(F32), high[at], low[at]], axis=0)
        pay_ref[d * held : (d + 1) * held, :] = part.astype(BF)


def loss_spread(plan, bags, neg_mask, towers, w_out, act, one, two):
    embed = towers.shape[1]
    rows = neg_mask.shape[0]
    bags_user, bags_item = bags[:rows], bags[rows:]
    user = hdot(bags_user, towers[0]).astype(BF)
    item = hdot(bags_item, towers[1]).astype(BF)
    items = lax.all_gather(item, AXES, axis=0, tiled=True)
    root = math.sqrt(embed)
    logits = dot(user, items, 1, 1) / root
    at = lax.axis_index(AXES) * rows + lax.broadcasted_iota(jnp.int32, logits.shape, 0)
    own = lax.broadcasted_iota(jnp.int32, logits.shape, 1) == at
    keep = own | (neg_mask == 1)
    top = jnp.max(jnp.where(keep, logits, -jnp.inf), axis=1, keepdims=True)
    weights = jnp.where(keep, jnp.exp(logits - top), 0.0)
    total = jnp.sum(weights, axis=1, keepdims=True)
    ce = top + jnp.log(total) - jnp.sum(jnp.where(own, logits, 0.0), axis=1, keepdims=True)
    count = lax.psum(jnp.sum(neg_mask.astype(F32)), AXES) / items.shape[0]
    scores = (weights / total - own.astype(F32)) / count / root
    d_user = hdot(scores, items.astype(F32))
    d_item = lax.psum_scatter(
        hdot(scores, user.astype(F32), 0, 0), AXES, scatter_dimension=0, tiled=True
    )
    d_towers = jnp.stack([hdot(bags_user, d_user, 0, 0), hdot(bags_item, d_item, 0, 0)])
    back = jnp.stack([hdot(d_user, towers[0], 1, 1), hdot(d_item, towers[1], 1, 1)], axis=1)
    d_emb = back.reshape(2 * rows, embed).astype(BF)
    d_act = dot(d_emb, w_out.astype(BF))
    d_second = hdot(d_emb.astype(F32), act, 0, 0)
    sums = jnp.stack([jnp.sum(d_act * one, axis=0), jnp.sum(d_act * two, axis=0)])
    sums, d_second, d_towers, loss = lax.psum((sums, d_second, d_towers, jnp.sum(ce)), AXES)
    return d_act, sums.reshape(-1, LANES), d_second, d_towers, loss, count


def block_halves(me, owners_ref, g_ref, outs, masks, local):
    width = g_ref.shape[2]
    bsize = LANES // 2
    half, quarter = bsize // 2, bsize // 4
    side = width // bsize
    lane_half = lax.broadcasted_iota(jnp.int32, (quarter, LANES), 1) // bsize
    for i, m in enumerate(masks):
        for b in range(local):
            r, c, odd = place(owners_ref[(me ^ m) * local + b], side)
            base = pl.multiple_of(r * half, half)
            cols = pl.ds(pl.multiple_of(c * LANES, LANES), LANES)
            keep = lane_half == odd
            to = (i * local + b) * quarter
            for h, out in enumerate(outs):
                tile = g_ref[h, pl.ds(base, half), cols].astype(out.dtype)
                out[to : to + quarter, :] = jnp.where(keep, tile[:quarter], swap_halves(tile[quarter:]))


def grad_kernel(
    me_ref, owners_ref, sums_ref, coef_ref, norm_ref, dact_ref, slope_ref, pre_ref, live_ref, xt_ref,
    top_ref, low_ref, chunk_ref, d_norm_ref, g_ref, d_pre_ref, row_ref,
    *, parts, order, local, core,
):
    rows, width = pre_ref.shape
    tiles = width // LANES
    held = sums_ref.shape[0] // parts
    half = tiles // 2
    if parts > 1:
        sides = []
        for h in range(2):
            side = jnp.zeros((held, LANES), F32)
            for d in range(parts):
                if (d // core) % 2 == h:
                    side = side + sums_ref[d * held : (d + 1) * held, :].astype(F32)
            sides.append(side)
        total = jnp.concatenate([s[i * half : (i + 1) * half] for i in range(2) for s in sides], axis=0)
        share = (held - tiles) // 2
        sides = [s[tiles : tiles + share] + s[tiles + share :] for s in sides]
        chunk_ref[...] = jnp.concatenate(
            [s[i * half : (i + 1) * half] for i in range(share // half) for s in sides], axis=0
        )
    else:
        total = sums_ref[...]
        chunk_ref[...] = jnp.zeros(chunk_ref.shape, F32)
    d_norm_ref[0:tiles, :] = total[tiles : 2 * tiles]
    d_norm_ref[tiles : 2 * tiles, :] = total[:tiles]
    for j in range(tiles):
        cols = slice(j * LANES, (j + 1) * LANES)
        row_ref[0:1, cols] = total[j : j + 1]
        row_ref[1:2, cols] = total[tiles + j : tiles + j + 1]
    scale = norm_ref[0:1, :] * coef_ref[1:2, :]
    flat = scale * row_ref[0:1, :] / coef_ref[2:3, :]
    tilt = scale * row_ref[1:2, :] / coef_ref[2:3, :] * coef_ref[1:2, :]
    row_ref[2:3, :] = scale
    row_ref[3:4, :] = flat
    row_ref[4:5, :] = tilt
    block = 2 * LANES
    for j in range(width // block):
        for i in range(2):
            cols = slice(j * block + i * LANES, j * block + (i + 1) * LANES)
            for b in range(rows // SLOTS_BAG):
                at = slice(b * SLOTS_BAG, (b + 1) * SLOTS_BAG)
                lead = dact_ref[b : b + 1, cols] * row_ref[2:3, cols]
                apart = (pre_ref[at, cols] - coef_ref[0:1, cols]) * row_ref[4:5, cols]
                d_pre = slope_ref[at, cols] * lead - row_ref[3:4, cols] - apart
                d_pre_ref[at, cols] = (live_ref[at, :] * d_pre).astype(BF)
        cols = slice(j * block, (j + 1) * block)
        g_ref[:, :, cols] = dot(xt_ref[...], d_pre_ref[:, cols]).reshape(2, width // 2, block)
    block_halves(me_ref[0], owners_ref, g_ref, (top_ref, low_ref), order, local)


def keep_kernel(me_ref, owners_ref, g_ref, top_ref, low_ref, *, order, local):
    block_halves(me_ref[0], owners_ref, g_ref, (top_ref, low_ref), order, local)


def scatter_sum(plan, kept, sent, rows):
    rest = len(plan.rest)
    shape = (2, 2, rest, rows, LANES)
    one, two = (
        (k + plan.swap(s, plan.core).astype(F32)).reshape(shape) for k, s in zip(kept, sent)
    )
    got_one = plan.swap(one[1], plan.x)
    got_two = plan.swap(two[:, 1], plan.y)
    one = one[0] + got_one.astype(F32)
    two = two[:, 0] + got_two.astype(F32)
    got_one = plan.swap(one[1], plan.y)
    got_two = plan.swap(two[1], plan.x)
    one = one[0] + got_one.astype(F32)
    two = two[0] + got_two.astype(F32)
    if rest <= 4:
        both = jnp.concatenate([one[1:], two[1:]], axis=1)
        return one, two, [plan.swap(both[k], m) for k, m in enumerate(plan.rest[1:])]
    both = jnp.concatenate([one, two], axis=1)
    for b in reversed(plan.bits):
        both = both.reshape(2, -1, 2 * rows, LANES)
        both = both[0] + plan.swap(both[1], b).astype(F32)
    return both[:, :rows], both[:, rows:], []


def norm_kernel(*refs, n):
    one_ref, two_ref, chunk_ref = refs[:3]
    got = refs[3:-2]
    g_ref, pay_ref = refs[-2:]
    total = jnp.concatenate([one_ref[0], two_ref[0]], axis=0)
    for g in got:
        total = total + g[...].astype(F32)
    g_ref[...] = total
    chunk = chunk_ref[...]
    squares = jnp.sum(total * total, keepdims=True) + jnp.sum(chunk * chunk, keepdims=True)
    high = chunk.astype(BF)
    low = chunk - high.astype(F32)
    for i, v in enumerate(three(squares)):
        low = jnp.where(spare(chunk.shape, i), v.astype(F32), low)
    packed = jnp.concatenate([high, low.astype(BF)], axis=0)
    rows = packed.shape[0]
    for d in range(n):
        pay_ref[d * rows : (d + 1) * rows, :] = packed


def spare(shape, i):
    row = lax.broadcasted_iota(jnp.int32, shape, 0)
    lane = lax.broadcasted_iota(jnp.int32, shape, 1)
    return (row == shape[0] - 1) & (lane == LANES - 3 + i)


def adamw(grad, weight, first, second):
    first = BETA_ONE * first + (1 - BETA_ONE) * grad
    second = BETA_TWO * second + (1 - BETA_TWO) * grad * grad
    step = (
        first / (1 - BETA_ONE**STEP) / (jnp.sqrt(second / (1 - BETA_TWO**STEP)) + EPSILON)
    )
    return weight - RATE * (step + DECAY * weight), first, second


def eliminate(gram_ref, power_ref):
    count, size, lanes = gram_ref.shape
    group = 8
    lane = lax.broadcasted_iota(jnp.int32, (count * group, lanes), 1)
    left = lax.broadcasted_iota(jnp.int32, (1, lanes), 1) < size
    for at in range(0, size, group):
        rest = at + group
        gram, power = gram_ref[:, at:rest, :], power_ref[:, at:rest, :]
        flat = gram.reshape(count * group, lanes)
        cols = [
            jnp.take_along_axis(flat, (lane // size) * size + at + i, axis=1).reshape(gram.shape)
            for i in range(group)
        ]
        for i in range(group):
            inv = lax.rsqrt(cols[i][:, i : i + 1, :])
            row, power_row = gram[:, i : i + 1, :] * inv, power[:, i : i + 1, :] * inv
            gram_ref[:, at + i : at + i + 1, :] = row
            power_ref[:, at + i : at + i + 1, :] = power_row
            f = cols[i] * inv
            gram, power = gram - f * row, power - f * power_row
            for j in range(i + 1, group):
                cols[j] = cols[j] - f * f[:, j : j + 1, :]
        if rest == size:
            return
        a, b, c = (v.astype(F32) for v in three(gram_ref[:, at:rest, :]))
        d, e, f = (v.astype(F32) for v in three(power_ref[:, at:rest, :]))
        lhs = jnp.concatenate([a, a, b, b, a, c], axis=1).astype(BF)
        rhs = jnp.concatenate([a, b, a, b, c, a], axis=1)
        rhs = jnp.concatenate([rhs, jnp.concatenate([d, e, d, e, f, d], axis=1)], axis=2).astype(BF)
        turned = [lhs[m].T for m in range(count)]
        for m in range(count):
            one = dot(turned[m][rest:size], rhs[m])
            two = dot(turned[m][size + rest :], rhs[m])
            gram_ref[m, rest:, :] = gram_ref[m, rest:, :] - jnp.where(left, one[:, :lanes], two[:, :lanes])
            power_ref[m, rest:, :] = power_ref[m, rest:, :] - jnp.where(left, one[:, lanes:], two[:, lanes:])


def pair(a, b):
    return jnp.concatenate([a, b], axis=1)


def prepare_kernel(
    w_hbm, left_hbm, right_hbm, bl_hbm, br_hbm, first_hbm, second_hbm, ema_hbm,
    moments_ref, stats_ref, bases_ref, weights_ref, turned_ref, powers_ref,
    w_ref, left_ref, right_ref, bl_ref, br_ref, first_ref, second_ref, ema_ref, sems,
):
    fetch(
        (w_hbm, left_hbm, right_hbm, bl_hbm, br_hbm, first_hbm, second_hbm, ema_hbm),
        (w_ref, left_ref, right_ref, bl_ref, br_ref, first_ref, second_ref, ema_ref),
        sems,
    )
    each = range(w_ref.shape[0])
    for b in each:
        moments_ref[b] = pair(first_ref[b], second_ref[b])
        stats_ref[b] = pair(left_ref[b], right_ref[b])
        bases_ref[b] = pair(bl_ref[b], br_ref[b])
        weights_ref[b] = pair(w_ref[b], ema_ref[b])
    half = [hdot(bl_ref[b], first_ref[b], 0, 0) for b in each]
    for b in each:
        turned_ref[b] = hdot(half[b], br_ref[b])
    lefts = [hdot(bl_ref[b], left_ref[b], 0, 0) for b in each]
    rights = [hdot(br_ref[b], right_ref[b], 0, 0) for b in each]
    for b in each:
        powers_ref[b] = pair(lefts[b], rights[b])


def turn_kernel(
    me_ref, owners_ref, g_ref, bases_ref,
    wo_hbm, mo_hbm, vo_hbm, eo_hbm, wt_hbm, mt_hbm, vt_hbm, wn_hbm, mn_hbm, vn_hbm,
    grad_ref, squares_ref, powers_ref, scale_ref,
    wide_ref, towers_ref, norms_ref, sems,
):
    local, bsize = bases_ref.shape[0], bases_ref.shape[1]
    sources = (wo_hbm, mo_hbm, vo_hbm, eo_hbm, wt_hbm, mt_hbm, vt_hbm, wn_hbm, mn_hbm, vn_hbm)
    targets = [wide_ref.at[i] for i in range(4)]
    targets += [towers_ref.at[i] for i in range(3)] + [norms_ref.at[i] for i in range(3)]
    copies = [pltpu.make_async_copy(a, b, sems.at[i]) for i, (a, b) in enumerate(zip(sources, targets))]
    for c in copies:
        c.start()
    largest = jnp.max(jnp.abs(g_ref[...]), keepdims=True)
    largest = jnp.where(largest > 0.0, largest, 1.0)
    scale_ref[...] = jnp.broadcast_to(largest, scale_ref.shape)
    half = bsize // 2
    each = range(local)
    grads = []
    for b in each:
        odd = owners_ref[me_ref[0] * local + b] % 2
        quarters = []
        for i in range(2):
            at = (i * local + b) * half // 2
            tile = g_ref[at : at + half // 2, :]
            tile = jnp.where(odd == 1, swap_halves(tile), tile)
            quarters += [tile[:, :bsize], tile[:, bsize:]]
        grads.append(jnp.concatenate(quarters, axis=0) / largest)
    bl = [bases_ref[b, :, :bsize] for b in each]
    br = [bases_ref[b, :, bsize:] for b in each]
    by_left = [hdot(bl[b], grads[b], 0, 0) for b in each]
    by_right = [hdot(grads[b], br[b]) for b in each]
    outer = [hdot(grads[b], grads[b], 1, 1) for b in each]
    inner = [hdot(grads[b], grads[b], 0, 0) for b in each]
    for b in each:
        squares_ref[b] = pair(outer[b], inner[b])
    for b in each:
        grad_ref[b] = pair(grads[b], hdot(by_left[b], br[b]))
    lefts = [hdot(by_left[b], grads[b], 1, 1) for b in each]
    rights = [hdot(by_right[b], grads[b], 0, 0) for b in each]
    for b in each:
        powers_ref[b] = pair(lefts[b], rights[b])
    for c in copies:
        c.wait()


def step_kernel(
    got_ref, d_norm_ref, d_towers_ref,
    grad_ref, squares_ref, powers_ref, scale_ref,
    old_ref, towers_ref, norms_ref,
    moments_ref, stats_ref, bases_ref, weights_ref, turned_first_ref, powers_old_ref,
    *refs, n,
):
    (
        w_out, low_out, left_out, right_out, bl_out, br_out, first_out, second_out, ema_out,
        wo_out, mo_out, vo_out, eo_out, wt_out, mt_out, vt_out, wn_out, mn_out, vn_out, gn_out,
        gram_ref, power_ref, wide_ref, dn_ref, flat_ref,
    ) = refs
    local, bsize = bases_ref.shape[0], bases_ref.shape[1]
    embed, width = old_ref.shape[1:]
    tiles = width // LANES
    held = got_ref.shape[0] // n
    if n > 1:
        chunk = held // 2
        used = functools.reduce(jnp.logical_or, [spare((chunk, LANES), i) for i in range(3)])
        squares = jnp.zeros((chunk, LANES), F32)
        for d in range(n):
            part = got_ref[d * held : (d + 1) * held, :].astype(F32)
            squares = squares + jnp.where(used, part[chunk:], 0.0)
            flat_ref[d * chunk : (d + 1) * chunk, :] = part[:chunk] + jnp.where(used, 0.0, part[chunk:])
        squares = jnp.sum(squares)
        for j in range(tiles):
            wide_ref[:, j * LANES : (j + 1) * LANES] = flat_ref[pl.ds(j, embed, stride=tiles), :]
    else:
        squares = jnp.max(got_ref[0:1, :LANES])
        wide_ref[...] = got_ref[8 : 8 + embed, :]
    squares = squares + jnp.sum(d_towers_ref[...] * d_towers_ref[...])
    squares = squares + jnp.sum(d_norm_ref[...] * d_norm_ref[...])
    norm = jnp.sqrt(jnp.full((1, LANES), squares, F32))
    gn_out[0, 0] = jnp.max(norm)
    factor = (CLIP / jnp.maximum(norm, CLIP))[:, :1]
    each = range(local)
    lead = factor * scale_ref[0:1, 0:1]
    twice = (1 - BETA_TWO) * lead * lead
    lefts, rights = [], []
    for b in each:
        powers = BETA_TWO * powers_old_ref[b] + twice * powers_ref[b]
        power_ref[b] = powers
        lefts.append(powers[:, :bsize])
        rights.append(powers[:, bsize:])
    for b in each:
        gram_ref[b] = pair(hdot(lefts[b], lefts[b], 1, 1), hdot(rights[b], rights[b], 1, 1))
    ratios = []
    for b in each:
        stats = BETA_TWO * stats_ref[b] + twice * squares_ref[b]
        left_out[b], right_out[b] = stats[:, :bsize], stats[:, bsize:]
        first_out[b] = BETA_ONE * moments_ref[b, :, :bsize] + (1 - BETA_ONE) * lead * grad_ref[b, :, :bsize]
        turned = grad_ref[b, :, bsize:]
        second = BETA_TWO * moments_ref[b, :, bsize:] + twice * turned * turned
        second_out[b] = second
        moved = BETA_ONE * turned_first_ref[b] + (1 - BETA_ONE) * lead * turned
        moved = moved / (1 - BETA_ONE**STEP)
        ratios.append(moved / (jnp.sqrt(second / (1 - BETA_TWO**STEP)) + EPSILON))
    half = [hdot(bases_ref[b, :, :bsize], ratios[b]) for b in each]
    updates = [hdot(half[b], bases_ref[b, :, bsize:], 1, 1) for b in each]
    for b in each:
        old = weights_ref[b, :, :bsize]
        new = old - RATE * (updates[b] + DECAY * old)
        w_out[b] = new
        low_out[b] = new.astype(BF)
        ema_out[b] = AVG_KEEP * weights_ref[b, :, bsize:] + AVG_TAKE * new
    new, m, v = adamw(wide_ref[...] * factor, old_ref[0], old_ref[1], old_ref[2])
    wo_out[...], mo_out[...], vo_out[...] = new, m, v
    eo_out[...] = AVG_KEEP * old_ref[3] + AVG_TAKE * new
    for t in range(2):
        wt_out[t], mt_out[t], vt_out[t] = adamw(
            d_towers_ref[t] * factor, towers_ref[0, t], towers_ref[1, t], towers_ref[2, t]
        )
        for j in range(tiles):
            dn_ref[t : t + 1, j * LANES : (j + 1) * LANES] = d_norm_ref[
                t * tiles + j : t * tiles + j + 1, :
            ]
    wn_out[...], mn_out[...], vn_out[...] = adamw(
        dn_ref[...] * factor, norms_ref[0], norms_ref[1], norms_ref[2]
    )
    eliminate(gram_ref, power_ref)
    for b in each:
        turned = power_ref[b].T
        bl_out[b], br_out[b] = turned[:bsize], turned[bsize:]


def exchange(payload):
    return lax.all_to_all(payload, AXES, 0, 0, tiled=True)


def on_device(
    plan,
    codes, field_offsets, seg_mask, neg_mask, owners,
    w_hidden, stat_left, stat_right, basis_left, basis_right, mom1_hidden, mom2_hidden, ema_hidden,
    w_out, mom1_out, mom2_out, ema_out,
    w_towers, mom1_towers, mom2_towers,
    w_norm, mom1_norm, mom2_norm,
):
    n = plan.n
    local, bsize = w_hidden.shape[0], w_hidden.shape[1]
    width, embed = w_out.shape
    slots = codes.shape[0]
    rows, total_rows = neg_mask.shape
    tiles = width // LANES
    half = bsize // 2
    bags = slots // SLOTS_BAG
    masked = total_rows <= 1024 and n <= embed
    me = lax.axis_index(AXES).astype(jnp.int32)[None]

    chunks = total_rows // LANES if masked else 0
    size = local * half + chunks * PAIR + PAIR
    (payload,) = call(
        functools.partial(pack_kernel, masked=masked),
        [((size, LANES), BF)],
        [w_hidden, neg_mask, seg_mask.reshape(-1, LANES)],
        hbm=3,
        scratch=[
            pltpu.VMEM(w_hidden.shape, F32),
            pltpu.VMEM(neg_mask.shape, jnp.int32),
            pltpu.VMEM((slots // LANES, LANES), jnp.int32),
            pltpu.SemaphoreType.DMA((3,)),
        ],
        name="pack",
    )
    cut = max(half, size // 2 // half * half)
    cut = min(cut, local * half)
    blocks = (local, bsize, bsize)
    twin = (local, bsize, 2 * bsize)
    state = [
        w_hidden, stat_left, stat_right, basis_left, basis_right, mom1_hidden, mom2_hidden, ema_hidden
    ]
    prepared = call(
        prepare_kernel,
        [(twin, F32)] * 4 + [(blocks, F32), (twin, F32)],
        state,
        hbm=len(state),
        scratch=[pltpu.VMEM(blocks, F32)] * len(state) + [pltpu.SemaphoreType.DMA((len(state),))],
        limit=12,
        name="prepare",
        cost=10_000_000,
    )
    turned_out, turned_mom1, turned_mom2, turned_ema = (
        a.T for a in (w_out, mom1_out, mom2_out, ema_out)
    )
    early = hash_inputs(codes, field_offsets)
    live = jnp.broadcast_to(seg_mask.astype(F32)[:, None], (slots, LANES))
    slot_bag = lax.broadcasted_iota(jnp.int32, (bags, slots), 1) // SLOTS_BAG
    in_bag = slot_bag == lax.broadcasted_iota(jnp.int32, (bags, slots), 0)
    chosen = jnp.where(in_bag, seg_mask.astype(F32)[None], 0.0).astype(BF)
    late = (*prepared, live, chosen)
    zero = (me[0] >> 16).astype(BF)

    def held_by(pieces):
        return [([m | base for m in plan.rest], row) for _, base, row in pieces]

    def place_blocks(pieces):
        (planes,) = call(
            functools.partial(assemble_kernel, holds=held_by(pieces), local=local),
            [((2, width, width), BF)],
            [me, owners] + [a for a, _, _ in pieces],
            smem=2,
            limit=8,
            name="assemble",
            cost=10_000_000,
        )
        return planes

    pieces, done, planes, (x, x_turned), (*prepared, live, chosen) = gather_pieces(
        plan, payload, cut, zero, early, late, place_blocks
    )
    mask_shape = (total_rows, total_rows) if masked else (PAIR, LANES)
    holds = held_by(pieces)
    arrays = [a for a, _, _ in pieces]
    pre, kept, sent, counts, mask, _ = call(
        functools.partial(
            pre_kernel, holds=holds, done=done, local=local, masked=masked, core=plan.core
        ),
        [
            ((slots, width), F32),
            ((tiles, LANES), F32),
            ((tiles, LANES), F32),
            ((n, LANES), F32),
            (mask_shape, BF),
            ((2, width, width), BF),
        ],
        [me, owners, planes] + arrays + [x, live],
        smem=2,
        scratch=[pltpu.VMEM((2 * tiles, LANES), F32)],
        aliases={2: 5},
        limit=16,
        name="pre",
    )
    (stats,) = call(
        functools.partial(merge_kernel, core=plan.core),
        [((n * tiles, LANES), F32)],
        [me, counts, kept, plan.swap(sent, plan.core)],
        smem=1,
        limit=4,
        name="merge",
    )
    stats = exchange(stats)
    slope, act, one, two, coef, bag_sums, pay = call(
        functools.partial(act_kernel, core=plan.core),
        [
            ((slots, width), F32),
            ((bags, width), F32),
            ((bags, width), F32),
            ((bags, width), F32),
            ((8, width), F32),
            ((bags, embed), F32),
            ((n * 8, LANES), F32),
        ],
        [stats, counts, w_norm, pre, live, chosen, turned_out],
        scratch=[
            pltpu.VMEM((slots, LANES), BF),
            pltpu.VMEM((tiles, bags * 8 + 8, LANES), F32),
            pltpu.VMEM((tiles, bags * 8 + 8, LANES), F32),
        ],
        limit=12,
        name="act",
    )
    if masked:
        chunk = embed * tiles // n
        everyone = exchange(pay)
        shared = (tiles + embed * tiles // 2, LANES)
        d_act, kept, sent, d_towers, loss_sum, count = call(
            functools.partial(loss_kernel, n=n, core=plan.core),
            [
                ((bags, width), F32),
                (shared, F32),
                (shared, F32),
                ((2, embed, embed), F32),
                ((1, 1), F32),
                ((1, 1), F32),
            ],
            [me, everyone, mask, w_towers, turned_out, act, one, two],
            smem=1,
            smem_outs=2,
            scratch=[
                pltpu.VMEM((total_rows, total_rows), F32),
                pltpu.VMEM((total_rows, embed), F32),
                pltpu.VMEM((total_rows, embed), F32),
                pltpu.VMEM((2, shared[0] + 8, LANES), F32),
            ],
            name="loss",
        )
        (pay,) = call(
            functools.partial(share_kernel, n=n, tiles=tiles),
            [((n * (tiles + chunk), LANES), BF)],
            [kept, plan.swap(sent, plan.core)],
            limit=4,
            name="share",
        )
        sums, parts = exchange(pay), n
        loss_sum, count = loss_sum[0, 0], count[0, 0]
    else:
        d_act, sums, d_second, d_towers, loss_sum, count = loss_spread(
            plan, bag_sums, neg_mask, w_towers, turned_out, act, one, two
        )
        parts = 1
        chunk = 8
    groups = [m for m in (0, plan.y, plan.x, plan.x | plan.y)]
    keep_order = [g | r for g in groups for r in plan.rest]
    order = (keep_order, [m | plan.core for m in keep_order])
    packed = (n // 2 * local * half // 2, LANES)
    packed = (n // 2 * local * half // 2, LANES)
    *sent, second_chunk, d_norm, full = call(
        functools.partial(grad_kernel, parts=parts, order=order[1], local=local, core=plan.core),
        [
            (packed, F32),
            (packed, F32),
            ((chunk, LANES), F32),
            ((2 * tiles, LANES), F32),
            ((2, width // 2, width), F32),
        ],
        [me, owners, sums, coef, w_norm, d_act, slope, pre, live, x_turned],
        smem=2,
        scratch=[pltpu.VMEM((slots, width), BF), pltpu.VMEM((8, width), F32)],
        limit=16,
        name="grad",
    )
    kept = call(
        functools.partial(keep_kernel, order=order[0], local=local),
        [(packed, F32), (packed, F32)],
        [me, owners, full],
        smem=2,
        limit=8,
        name="keep",
        cost=100_000_000,
    )
    one_sum, two_sum, others = scatter_sum(plan, kept, sent, local * half // 2)
    copies = n if masked else 1
    grad, pay = call(
        functools.partial(norm_kernel, n=copies),
        [((local * half, LANES), F32), ((copies * 2 * chunk, LANES), BF)],
        [one_sum, two_sum, second_chunk, *others],
        name="norm",
    )
    if masked:
        got = exchange(pay)
    else:
        squares = lax.psum(jnp.sum(grad * grad), AXES) + jnp.sum(d_second * d_second)
        got = jnp.concatenate([jnp.full((8, width), squares, F32), d_second], axis=0)
    moments, stats, bases, weights, turned_first, powers_old = prepared
    plain = [
        turned_out, turned_mom1, turned_mom2, turned_ema,
        w_towers, mom1_towers, mom2_towers,
        w_norm, mom1_norm, mom2_norm,
    ]
    turned = call(
        turn_kernel,
        [(twin, F32)] * 3
        + [((8, LANES), F32), ((4, embed, width), F32), ((3, 2, embed, embed), F32), ((3, 2, width), F32)],
        [me, owners, grad, bases, *plain],
        smem=2,
        hbm=len(plain),
        scratch=[pltpu.SemaphoreType.DMA((len(plain),))],
        name="turn",
        cost=10_000_000,
    )
    outs = [(blocks, F32), (blocks, BF)] + [(blocks, F32)] * 7
    outs += [((embed, width), F32)] * 4 + [((2, embed, embed), F32)] * 3 + [((2, width), F32)] * 3
    new = call(
        functools.partial(step_kernel, n=n if masked else 1),
        outs + [((1, 1), F32)],
        [
            got, d_norm, d_towers, *turned,
            moments, stats, bases, weights, turned_first, powers_old,
        ],
        smem_outs=1,
        scratch=[
            pltpu.VMEM(twin, F32),
            pltpu.VMEM(twin, F32),
            pltpu.VMEM((embed, width), F32),
            pltpu.VMEM((2, width), F32),
            pltpu.VMEM((embed * tiles + tiles, LANES), F32),
        ],
        name="step",
    )
    return (loss_sum, count, new[-1][0, 0], *new[:9], *(a.T for a in new[9:13]), *new[13:-1])


def solution(mesh):
    split = P(("gx", "gy"))
    plan = Plan(mesh.shape["gx"], mesh.shape["gy"])
    return jax.shard_map(
        functools.partial(on_device, plan),
        mesh=mesh,
        in_specs=(split, P(), split, split, P()) + (split,) * 8 + (P(),) * 10,
        out_specs=(P(),) * 3 + (split,) * 9 + (P(),) * 10,
        check_vma=False,
    )
```
